32 devices in a mesh: batch: 8 (over z, core), rows: 4 (over y, x).
Axes of the slice: x: 2, y: 2, z: 4, core: 2. Of those that a mesh axis runs over, the one named last changes fastest.
Arguments:
- velocity: float32 [16, 2, 128, 128], P('batch', None, 'rows'), may hold values from -4 to 4
- targets: float32 [16, 2, 2, 128, 128], P('batch', None, None, 'rows'), may hold values from -4 to 4
- keyframes: int32 [16, 2], P('batch'), may hold values from 0 to 4, as said below
- boxes: int32 [16, 2, 4], P('batch'), may hold values from 0 to 128, as said below
- w_in: float32 [64, 3, 3, 3], replicated, may hold values from -1.25 to 1.25
- w_mid: float32 [5, 9, 4096], replicated, may hold values from -0.25 to 0.25
- norm_params: float32 [2, 5, 64], replicated, may hold values from 0.5 to 1.5
- head_params: float32 [2, 65], replicated, may hold values from -0.75 to 0.75
- m_in: float32 [64, 3, 3, 3], replicated, may hold values from -3.8146973e-06 to 3.8146973e-06
- m_mid: float32 [5, 9, 4096], replicated, may hold values from -3.8146973e-06 to 3.8146973e-06
- m_norm: float32 [2, 5, 64], replicated, may hold values from -3.8146973e-06 to 3.8146973e-06
- m_head: float32 [2, 65], replicated, may hold values from -3.8146973e-06 to 3.8146973e-06
- v_in: float32 [64, 3, 3, 3], replicated, may hold values from 2.8155747e-13 to 1.1240887e-12
- v_mid: float32 [5, 9, 4096], replicated, may hold values from 2.8155747e-13 to 1.1240887e-12
- v_norm: float32 [2, 5, 64], replicated, may hold values from 2.8155747e-13 to 1.1240887e-12
- v_head: float32 [2, 65], replicated, may hold values from 2.8155747e-13 to 1.1240887e-12
Outputs:
- new_w_in: float32 [64, 3, 3, 3], replicated
- new_w_mid: float32 [5, 9, 4096], replicated
- new_norm: float32 [2, 5, 64], replicated
- new_head: float32 [2, 65], replicated
- new_m_in: float32 [64, 3, 3, 3], replicated
- new_m_mid: float32 [5, 9, 4096], replicated
- new_m_norm: float32 [2, 5, 64], replicated
- new_m_head: float32 [2, 65], replicated
- new_v_in: float32 [64, 3, 3, 3], replicated
- new_v_mid: float32 [5, 9, 4096], replicated
- new_v_norm: float32 [2, 5, 64], replicated
- new_v_head: float32 [2, 65], replicated
- low_w_in: bfloat16 [64, 3, 3, 3], replicated
- low_w_mid: bfloat16 [5, 9, 4096], replicated
- low_head: bfloat16 [2, 65], replicated
- loss_sum: float32 [], replicated
- frame_cells: float32 [], replicated
- grad_norm: float32 [], replicated
The draws below stay inside these ranges and needn't reach their ends.
Inputs may be any that keep to these rules, and one draw needn't show every extreme that they name: `keyframes`: 0 marks an unused slot; slot 0 of every sample is used. `boxes`: each box has a first index below its end index, spans 8 to 32 lines along each side.
All inputs are finite; a program needn't handle non-finite values.
Results may differ from the reference program's by a relative error of at most 0.0089.
The reference program's roundings to bfloat16 on the way count: a program that leaves them out, or rounds other values in their place, can miss the bound.
Values may be sent and summed in bfloat16 or wider, within the bound.
A program may use at most 576 MiB of HBM per device.

```python
import math
import jax
import jax.numpy as jnp
from jax import lax

GRID = 128
CH = 64
GROUPS = 8
LAYERS = 4
STEPS = 4
JACOBI = 4
KEYS = 2
BOXES = 2
STEP_NUM = 10
SAMPLES = 16
TILE = 32


def band_values(key, lead, lo, hi):
    bands = GRID // TILE
    band = (jnp.arange(GRID) // TILE).astype(jnp.int32)
    values = jax.random.uniform(key, lead + (bands,), jnp.float32, lo, hi)
    return jnp.take(values, band, axis=len(lead))[..., None]


def rough_part(key, shape):
    values = jax.random.normal(key, shape, jnp.float32)
    return values


def draw_velocity(key, part):
    key = jax.random.fold_in(key, 31)
    keys = jax.random.split(key, 4)
    lead = (SAMPLES, 2)
    level = jnp.exp(band_values(keys[0], lead, -1.2, 0.3))
    offset = band_values(keys[1], lead, -1.0, 1.0)
    rough = rough_part(keys[2], (SAMPLES, 2, GRID, GRID))
    amplitude = jax.random.uniform(keys[3], (SAMPLES, 1, 1, 1), jnp.float32, 1.0, 2.0)
    phase = ((jnp.arange(GRID) % TILE).astype(jnp.float32) + 0.5) / TILE
    profile = -jnp.cos(math.pi * phase)
    along_rows = jnp.broadcast_to(profile[None, None, :, None], (SAMPLES, 1, GRID, GRID))
    along_cols = jnp.broadcast_to(profile[None, None, None, :], (SAMPLES, 1, GRID, GRID))
    smooth = amplitude * jnp.concatenate([along_rows, along_cols], axis=1)
    return jnp.clip(smooth + offset + level * rough, -4.0, 4.0).astype(jnp.float32)


def draw_targets(key, part):
    key = jax.random.fold_in(key, 37)
    keys = jax.random.split(key, 3)
    lead = (SAMPLES, KEYS, 2)
    level = jnp.exp(band_values(keys[0], lead, -1.2, 0.3))
    offset = band_values(keys[1], lead, -2.0, 2.0)
    rough = rough_part(keys[2], (SAMPLES, KEYS, 2, GRID, GRID))
    return jnp.clip(offset + level * rough, -4.0, 4.0).astype(jnp.float32)


def draw_keyframes(key, part):
    key = jax.random.fold_in(key, 11)
    first_key, second_key, live_key = jax.random.split(key, 3)
    first = jax.random.randint(first_key, (SAMPLES, 1), 1, STEPS + 1)
    first = first.at[0, 0].set(STEPS)
    second = jax.random.randint(second_key, (SAMPLES, KEYS - 1), 1, STEPS + 1)
    chance = jax.random.randint(live_key, (SAMPLES, KEYS - 1), 0, 3 * SAMPLES)
    order = jnp.arange(SAMPLES)[:, None]
    second = jnp.where(chance < SAMPLES + 2 * order, second, 0)
    second = second.at[0].set(0)
    return jnp.concatenate([first, second], axis=1).astype(jnp.int32)


def draw_boxes(key, part):
    key = jax.random.fold_in(key, 23)
    keys = jax.random.split(key, 4)
    extent_rows = jax.random.randint(keys[0], (SAMPLES, BOXES), GRID // 16, GRID // 4 + 1)
    extent_cols = jax.random.randint(keys[1], (SAMPLES, BOXES), GRID // 16, GRID // 4 + 1)
    start_rows = jax.random.randint(keys[2], (SAMPLES, BOXES), 0, GRID - GRID // 4 + 1)
    start_cols = jax.random.randint(keys[3], (SAMPLES, BOXES), 0, GRID - GRID // 4 + 1)
    boxes = jnp.stack([start_rows, start_rows + extent_rows, start_cols, start_cols + extent_cols], axis=2)
    corner = jnp.array([0, GRID // 4, GRID - GRID // 4, GRID], jnp.int32)
    boxes = boxes.at[0, 0].set(corner)
    return boxes.astype(jnp.int32)


def normal_values(rng, dims, spread, most, kind=jnp.bfloat16):
    values = spread * jax.random.normal(rng, dims, jnp.float32)
    return jnp.clip(values, min=-most, max=most).astype(kind)


def setup_inputs(seed: int = 0) -> dict:
    key_list = jax.random.split(jax.random.key(seed), 17)
    velocity = draw_velocity(jax.random.fold_in(key_list[16], 71), 0)
    targets = draw_targets(jax.random.fold_in(key_list[16], 71), 0)
    keyframes = draw_keyframes(jax.random.fold_in(key_list[16], 71), 0)
    boxes = draw_boxes(jax.random.fold_in(key_list[16], 71), 0)
    w_in = normal_values(key_list[4], (CH, 3, 3, 3), 27 ** -0.5, 1.25, jnp.float32)
    w_mid = normal_values(key_list[5], (LAYERS + 1, 9, CH * CH), (9 * CH) ** -0.5, 0.25, jnp.float32)
    norm_params = jnp.clip(1.0 + 0.1 * jax.random.normal(key_list[6], (2, LAYERS + 1, CH), jnp.float32), 0.5, 1.5)
    head_params = normal_values(key_list[7], (2, CH + 1), CH ** -0.5, 0.75, jnp.float32)
    m_in = normal_values(key_list[8], (CH, 3, 3, 3), (0.000111 / (27 * CH + 9 * (LAYERS + 1) * CH * CH + 2 * (LAYERS + 1) * CH + 2 * CH + 2) ** 0.5), 3.814697265625e-06, jnp.float32)
    m_mid = normal_values(key_list[9], (LAYERS + 1, 9, CH * CH), (0.000111 / (27 * CH + 9 * (LAYERS + 1) * CH * CH + 2 * (LAYERS + 1) * CH + 2 * CH + 2) ** 0.5), 3.814697265625e-06, jnp.float32)
    m_norm = normal_values(key_list[10], (2, LAYERS + 1, CH), (0.000111 / (27 * CH + 9 * (LAYERS + 1) * CH * CH + 2 * (LAYERS + 1) * CH + 2 * CH + 2) ** 0.5), 3.814697265625e-06, jnp.float32)
    m_head = normal_values(key_list[11], (2, CH + 1), (0.000111 / (27 * CH + 9 * (LAYERS + 1) * CH * CH + 2 * (LAYERS + 1) * CH + 2 * CH + 2) ** 0.5), 3.814697265625e-06, jnp.float32)
    v_in = jnp.clip(jnp.exp(jax.random.uniform(key_list[12], (CH, 3, 3, 3), jnp.float32, math.log(2.815574650597702e-13), math.log(1.1240886693686392e-12))), 2.815574650597702e-13, 1.1240886693686392e-12)
    v_mid = jnp.clip(jnp.exp(jax.random.uniform(key_list[13], (LAYERS + 1, 9, CH * CH), jnp.float32, math.log(2.815574650597702e-13), math.log(1.1240886693686392e-12))), 2.815574650597702e-13, 1.1240886693686392e-12)
    v_norm = jnp.clip(jnp.exp(jax.random.uniform(key_list[14], (2, LAYERS + 1, CH), jnp.float32, math.log(2.815574650597702e-13), math.log(1.1240886693686392e-12))), 2.815574650597702e-13, 1.1240886693686392e-12)
    v_head = jnp.clip(jnp.exp(jax.random.uniform(key_list[15], (2, CH + 1), jnp.float32, math.log(2.815574650597702e-13), math.log(1.1240886693686392e-12))), 2.815574650597702e-13, 1.1240886693686392e-12)
    return dict(velocity=velocity, targets=targets, keyframes=keyframes, boxes=boxes, w_in=w_in, w_mid=w_mid, norm_params=norm_params, head_params=head_params, m_in=m_in, m_mid=m_mid, m_norm=m_norm, m_head=m_head, v_in=v_in, v_mid=v_mid, v_norm=v_norm, v_head=v_head)


@jax.custom_vjp
def low(v):
    return lax.optimization_barrier(v.astype(jnp.bfloat16)).astype(jnp.float32)

@jax.custom_vjp
def low_back(v):
    return v

def low_keep(v):
    return (low(v), None)

def low_pass(kept, grad):
    return (grad,)

def back_keep(v):
    return (v, None)

def back_low(kept, grad):
    return (low(grad),)
low.defvjp(low_keep, low_pass)
low_back.defvjp(back_keep, back_low)
EPS_NORM = 1e-05
DT_FORCE = 0.5
DT_ADV = 0.2
CLIP_NORM = 0.001
BETA_ONE = 0.9
BETA_TWO = 0.95
ADAM_EPS = 1e-08
DECAY = 0.01
RATES = (0.2, 0.05, 1.0, 0.15)
HIGH = lax.Precision.HIGHEST

def open_mask(boxes, rows_at, cols_at):
    r = rows_at[None, None, :, None]
    c = cols_at[None, None, None, :]
    b = boxes[:, :, :, None, None]
    inside = (r >= b[:, :, 0]) & (r < b[:, :, 1]) & (c >= b[:, :, 2]) & (c < b[:, :, 3])
    return 1.0 - lax.optimization_barrier(jnp.max(inside.astype(jnp.float32), axis=1))

def framed(x):
    return jnp.pad(x, ((0, 0), (0, 0), (1, 1), (1, 1)))

def drows(q):
    return 0.5 * (q[:, :, 2:, 1:-1] - q[:, :, :-2, 1:-1])

def dcols(q):
    return 0.5 * (q[:, :, 1:-1, 2:] - q[:, :, 1:-1, :-2])

def nsum(q):
    return q[:, :, 2:, 1:-1] + q[:, :, :-2, 1:-1] + q[:, :, 1:-1, 2:] + q[:, :, 1:-1, :-2]

def advect_local(q):
    inner = q[:, :, 1:-1, 1:-1]
    return inner - DT_ADV * (inner[:, 0:1] * drows(q) + inner[:, 1:2] * dcols(q))

def project_core(v):
    q = framed(v)
    div = drows(q[:, 0:1]) + dcols(q[:, 1:2])
    press = -0.25 * div
    for sweep in range(JACOBI - 1):
        press = 0.25 * (nsum(framed(press)) - div)
    r = framed(press)
    return v - jnp.concatenate([drows(r), dcols(r)], axis=1)

def kernel_of(flat):
    return jnp.transpose(flat.reshape(3, 3, CH, CH), (2, 3, 0, 1))

def conv(h, weight):
    return lax.conv_general_dilated(h, weight, (1, 1), ((1, 1), (1, 1)), dimension_numbers=('NCHW', 'OIHW', 'NCHW'), precision=HIGH)

def group_norm(z, gain, shift):
    s, c, hh, ww = z.shape
    grouped = z.reshape(s, GROUPS, c // GROUPS, hh, ww)
    mean = lax.optimization_barrier(jnp.mean(grouped, axis=(2, 3, 4), keepdims=True))
    square = lax.optimization_barrier(jnp.mean(grouped * grouped, axis=(2, 3, 4), keepdims=True))
    scaled = (grouped - mean) * lax.rsqrt(square - mean * mean + EPS_NORM)
    return scaled.reshape(z.shape) * gain[None, :, None, None] + shift[None, :, None, None]

def finish(z, norms, layer):
    return low(jax.nn.silu(group_norm(low_back(z), norms[0, layer], norms[1, layer])))

def pooling(h):
    s, c, hh, ww = h.shape
    return lax.optimization_barrier(jnp.mean(h.reshape(s, c, hh // 2, 2, ww // 2, 2), axis=(3, 5)))

def upsample(h):
    return jnp.repeat(jnp.repeat(h, 2, axis=2), 2, axis=3)

def one_step(params, u, opened):
    w_in, w_mid, norms, head = params
    h0 = low(jnp.concatenate([u, opened], axis=1))
    h1 = finish(conv(h0, low(w_in)), norms, 0)
    skip = finish(conv(h1, low(kernel_of(w_mid[0]))), norms, 1)
    pooled = low(pooling(skip))
    h3 = finish(conv(pooled, low(kernel_of(w_mid[1]))), norms, 2)
    h4 = finish(conv(h3, low(kernel_of(w_mid[2]))), norms, 3)
    z5 = conv(upsample(h4), low(kernel_of(w_mid[3]))) + conv(skip, low(kernel_of(w_mid[4])))
    h = finish(z5, norms, 4)
    force = low_back(jnp.einsum('oc,schw->sohw', low(head[:, :CH]), h, precision=HIGH)) + head[:, CH][None, :, None, None]
    pushed = (u + DT_FORCE * force) * opened
    return opened * project_core(advect_local(framed(pushed)))

def forward(params, velocity, targets, keyframes, opened):
    stepper = jax.checkpoint(one_step)
    u = velocity
    total = jnp.zeros((), jnp.float32)
    for step in range(STEPS):
        u = stepper(params, u, opened)
        live = (keyframes == step + 1).astype(jnp.float32)
        miss = u[:, None] - targets
        err = lax.optimization_barrier(jnp.sum(opened[:, None] * miss * miss, axis=(2, 3, 4)))
        total = total + jnp.sum(live * err)
    return total

def reference(velocity, targets, keyframes, boxes, w_in, w_mid, norm_params, head_params, m_in, m_mid, m_norm, m_head, v_in, v_mid, v_norm, v_head):
    index = jnp.arange(GRID).astype(jnp.int32)
    opened = open_mask(boxes, index, index)[:, None]
    count = jnp.sum((keyframes > 0).astype(jnp.float32) * lax.optimization_barrier(jnp.sum(opened, axis=(1, 2, 3)))[:, None])
    params = (w_in, w_mid, norm_params, head_params)
    total, pull = jax.vjp(lambda p: forward(p, velocity, targets, keyframes, opened), params)
    grads, = pull(1.0 / count)
    norm = jnp.sqrt(sum((jnp.sum(g * g) for g in grads)))
    scale = jnp.minimum(1.0, CLIP_NORM / norm)
    new_w, new_m, new_v = ([], [], [])
    for weight, m, v, g, rate in zip(params, (m_in, m_mid, m_norm, m_head), (v_in, v_mid, v_norm, v_head), grads, RATES):
        g = g * scale
        m2 = BETA_ONE * m + (1 - BETA_ONE) * g
        v2 = BETA_TWO * v + (1 - BETA_TWO) * g * g
        mhat = m2 / (1 - BETA_ONE ** STEP_NUM)
        vhat = v2 / (1 - BETA_TWO ** STEP_NUM)
        new_w.append(weight - rate * (mhat / (jnp.sqrt(vhat) + ADAM_EPS) + DECAY * weight))
        new_m.append(m2)
        new_v.append(v2)
    return (new_w[0], new_w[1], new_w[2], new_w[3], new_m[0], new_m[1], new_m[2], new_m[3], new_v[0], new_v[1], new_v[2], new_v[3], new_w[0].astype(jnp.bfloat16), new_w[1].astype(jnp.bfloat16), new_w[3].astype(jnp.bfloat16), total, count, norm)
```

```python
import functools

import jax
import jax.numpy as jnp
from jax import lax
from jax.experimental import pallas as pl
from jax.experimental.pallas import tpu as pltpu
from jax.sharding import PartitionSpec as P

CH = 64
GROUPS = 8
LAYERS = 4
STEPS = 4
JACOBI = 4
STEP_NUM = 10
LANES = 128
EDGE = 8

EPS_NORM = 1e-05
DT_FORCE = 0.5
DT_ADV = 0.2
CLIP_NORM = 0.001
BETA_ONE = 0.9
BETA_TWO = 0.95
ADAM_EPS = 1e-08
DECAY = 0.01
RATES = (0.2, 0.05, 1.0, 0.15)

BF = jnp.bfloat16
F32 = jnp.float32
MESH = pl.DeviceIdType.MESH
FULL_SLOT = {0: 0, 1: 1, 4: 2}
HALF_SLOT = {2: 0, 3: 1}


def nt_dot(a, b):
    return lax.dot_general(a, b, (((1,), (1,)), ((), ())), preferred_element_type=F32)


def nn_dot(a, b):
    return jnp.dot(a, b, preferred_element_type=F32)


def beside(rows):
    return jnp.concatenate(rows, axis=1)


def lane_of(shape):
    return lax.broadcasted_iota(jnp.int32, shape, len(shape) - 1)


def from_left(x, by):
    return jnp.where(lane_of(x.shape) < by, 0.0, pltpu.roll(x, by, x.ndim - 1))


def from_right(x, by):
    return jnp.where(
        lane_of(x.shape) >= LANES - by, 0.0, pltpu.roll(x, LANES - by, x.ndim - 1)
    )


def pair_sum(x):
    even = lane_of(x.shape) % 2 == 0
    last = x.ndim - 1
    return x + jnp.where(even, pltpu.roll(x, LANES - 1, last), pltpu.roll(x, 1, last))


def drows(x):
    count = x.shape[0]
    return 0.5 * (pltpu.roll(x, count - 1, 0) - pltpu.roll(x, 1, 0))


def dcols(x):
    return 0.5 * (from_right(x, 1) - from_left(x, 1))


def nsum(x):
    count = x.shape[0]
    return (
        pltpu.roll(x, count - 1, 0) + pltpu.roll(x, 1, 0) + from_right(x, 1) + from_left(x, 1)
    )


def project(vr, vc, grid):
    div = grid * (drows(vr) + dcols(vc))
    press = -0.25 * div
    for sweep in range(JACOBI - 1):
        press = grid * (0.25 * (nsum(press) - div))
    return vr - drows(press), vc - dcols(press)


def sublanes(x):
    return jnp.sum(x.reshape(x.shape[0] // 8, 8, LANES), axis=0)


def group_rows(x):
    return jnp.sum(x.reshape(GROUPS, CH // GROUPS, LANES), axis=1)


def spread(x):
    return jnp.concatenate(
        [jnp.broadcast_to(x[g : g + 1], (CH // GROUPS, LANES)) for g in range(GROUPS)], axis=0
    )


def train_kernel(
    ranks,
    vel,
    tgt,
    meta,
    wf,
    wb,
    w0f,
    w0b,
    norms,
    headf,
    headb,
    bias,
    gw,
    gw0,
    gnorm,
    ghead,
    misc,
    u_ext,
    t_own,
    m_own,
    opened,
    grid_mask,
    s0,
    s0b,
    q_ext,
    u_kept,
    w_ext,
    u_bar,
    frows,
    taps,
    h1,
    skip,
    pooled,
    h3,
    h4,
    xh_full,
    xh_half,
    inv_kept,
    zbuf,
    skip_bar,
    half_bar,
    sg,
    sgh,
    edges,
    g_halo,
    coef,
    acc,
    st_send,
    st_recv,
    in_send,
    in_recv,
    in_local,
    halo_send,
    halo_recv,
    st_ss,
    st_rs,
):
    quarter = ranks // 4
    parts = ranks // 2
    tile = vel.shape[2]
    rows = 2 * tile
    half = rows // 2
    batch_at = lax.axis_index("batch")
    row_at = lax.axis_index("rows")
    core = lax.rem(batch_at, 2)
    plane = batch_at - core
    sample = row_at // quarter
    part = 2 * lax.rem(row_at, quarter) + core

    def owner(which, piece):
        return (plane + lax.rem(piece, 2), which * quarter + piece // 2)

    u_ext[...] = jnp.zeros_like(u_ext)
    q_ext[...] = jnp.zeros_like(q_ext)
    w_ext[...] = jnp.zeros_like(w_ext)
    g_halo[...] = jnp.zeros_like(g_halo)
    for kept, count in ((h1, rows), (skip, rows), (pooled, half), (h3, half), (h4, half)):
        for t in range(STEPS):
            kept[t, 0] = jnp.zeros((CH, LANES), BF)
            kept[t, count + 1] = jnp.zeros((CH, LANES), BF)

    barrier = pltpu.get_barrier_semaphore()
    members = 2 * ranks
    mine = core * ranks + row_at

    def greet(d, carry):
        other = lax.rem(mine + d, members)
        pl.semaphore_signal(
            barrier,
            inc=1,
            device_id=(plane + other // ranks, lax.rem(other, ranks)),
            device_id_type=MESH,
        )
        return carry

    lax.fori_loop(1, members, greet, 0)
    pl.semaphore_wait(barrier, members - 1)

    def incoming(place):
        at = pl.ds(pl.multiple_of(EDGE + place * tile, 8), tile)
        here = pl.ds(pl.multiple_of(place * tile, 8), tile)
        return u_ext.at[:, at, :], t_own.at[:, :, here, :], m_own.at[place]

    place = lax.rem(row_at, 2)
    for j in range(2):
        to_batch, to_row = owner(2 * core + j, row_at // 2)
        stays = (to_batch == batch_at) & (to_row == row_at)
        for k, (src, dst) in enumerate(zip((vel.at[j], tgt.at[j], meta.at[j]), incoming(place))):

            @pl.when(stays)
            def _():
                pltpu.make_async_copy(src, dst, in_local.at[k]).start()

            @pl.when(jnp.logical_not(stays))
            def _():
                pltpu.make_async_remote_copy(
                    src_ref=src,
                    dst_ref=dst,
                    send_sem=in_send.at[j, k],
                    recv_sem=in_recv.at[place, k],
                    device_id=(to_batch, to_row),
                    device_id_type=MESH,
                ).start()

    for j in range(2):
        to_batch, to_row = owner(2 * core + j, row_at // 2)
        stays = (to_batch == batch_at) & (to_row == row_at)
        for k, src in enumerate((vel.at[j], tgt.at[j], meta.at[j])):

            @pl.when(stays)
            def _():
                pltpu.make_async_copy(src, src, in_local.at[k]).wait()

            @pl.when(jnp.logical_not(stays))
            def _():
                pltpu.make_async_copy(src, src, in_send.at[j, k]).wait()

    for i in range(2):
        from_batch = plane + sample // 2
        from_row = 2 * part + i
        stays = (from_batch == batch_at) & (from_row == row_at)
        for k, dst in enumerate(incoming(i)):

            @pl.when(jnp.logical_not(stays))
            def _():
                pltpu.make_async_copy(dst, dst, in_recv.at[i, k]).wait()

    has_prev = part > 0
    has_next = part < parts - 1
    prev_id = owner(sample, jnp.maximum(part - 1, 0))
    next_id = owner(sample, jnp.minimum(part + 1, parts - 1))

    def halo_copies(slot, low_src, high_src, top_dst, bottom_dst):
        to_prev = pltpu.make_async_remote_copy(
            src_ref=low_src,
            dst_ref=bottom_dst,
            send_sem=halo_send.at[slot, 0],
            recv_sem=halo_recv.at[slot, 0],
            device_id=prev_id,
            device_id_type=MESH,
        )
        to_next = pltpu.make_async_remote_copy(
            src_ref=high_src,
            dst_ref=top_dst,
            send_sem=halo_send.at[slot, 1],
            recv_sem=halo_recv.at[slot, 1],
            device_id=next_id,
            device_id_type=MESH,
        )
        return to_prev, to_next

    def halo_start(*args):
        to_prev, to_next = halo_copies(*args)

        @pl.when(has_prev)
        def _():
            to_prev.start()

        @pl.when(has_next)
        def _():
            to_next.start()

    def halo_wait(*args):
        to_prev, to_next = halo_copies(*args)

        @pl.when(has_prev)
        def _():
            to_prev.wait_send()
            to_next.wait_recv()

        @pl.when(has_next)
        def _():
            to_next.wait_send()
            to_prev.wait_recv()

    def ext_halo(slot, ref):
        args = (
            slot,
            ref.at[:, pl.ds(EDGE, EDGE), :],
            ref.at[:, pl.ds(rows, EDGE), :],
            ref.at[:, pl.ds(0, EDGE), :],
            ref.at[:, pl.ds(rows + EDGE, EDGE), :],
        )
        halo_start(*args)
        halo_wait(*args)

    def group_totals(slot, first, second):
        local = jnp.concatenate([group_rows(first), group_rows(second)], axis=0)
        st_send[slot] = local
        copies = []
        for d in range(1, parts):
            copies.append(
                pltpu.make_async_remote_copy(
                    src_ref=st_send.at[slot],
                    dst_ref=st_recv.at[slot, d - 1],
                    send_sem=st_ss.at[slot, d - 1],
                    recv_sem=st_rs.at[slot, d - 1],
                    device_id=owner(sample, lax.rem(part + d, parts)),
                    device_id_type=MESH,
                )
            )
        for copy in copies:
            copy.start()
        total = local
        for d, copy in enumerate(copies):
            copy.wait()
            total = total + st_recv[slot, d]
        total = jnp.broadcast_to(jnp.sum(total, axis=1, keepdims=True), total.shape)
        return total[:GROUPS], total[GROUPS:]

    ext = rows + 2 * EDGE
    row_is = lax.broadcasted_iota(jnp.int32, (ext, LANES), 0) - EDGE + part * rows
    inside_grid = ((row_is >= 0) & (row_is < parts * rows)).astype(F32)
    row_f = row_is.astype(F32)
    col_f = lane_of((ext, LANES)).astype(F32)
    covered = jnp.zeros((ext, LANES), F32)
    facts = m_own[0]
    for b in range(2):
        bounds = [facts[2 + 4 * b + k : 3 + 4 * b + k] for k in range(4)]
        inside = (
            (row_f >= bounds[0])
            & (row_f < bounds[1])
            & (col_f >= bounds[2])
            & (col_f < bounds[3])
        )
        covered = jnp.maximum(covered, inside.astype(F32))
    grid_mask[...] = inside_grid
    opened[...] = inside_grid * (1.0 - covered)
    own = pl.ds(EDGE, rows)
    misc[...] = jnp.zeros_like(misc)
    live_slots = (facts[0:1] > 0.5).astype(F32) + (facts[1:2] > 0.5).astype(F32)
    misc[1] = sublanes(opened[own, :] * live_slots)
    gw[...] = jnp.zeros_like(gw)
    gw0[...] = jnp.zeros_like(gw0)
    gnorm[...] = jnp.zeros_like(gnorm)
    ghead[...] = jnp.zeros_like(ghead)
    s0[...] = jnp.zeros_like(s0)
    frows[...] = jnp.zeros_like(frows)
    u_bar[...] = jnp.zeros_like(u_bar)

    ext_halo(10, u_ext)

    for kx in range(3):
        field = opened[...]
        s0[:, 3 * kx + 2, :] = (from_left(field, 1), field, from_right(field, 1))[kx]

    def put_shifted(dst, at, x, by, order):
        copies = (from_left(x, by), x, from_right(x, by))
        for place_at, which in enumerate(order):
            dst[at, place_at * CH : (place_at + 1) * CH, :] = copies[which].astype(BF)

    FORWARD = (0, 1, 2)
    BACKWARD = (2, 1, 0)

    def spread_halo(dst, lines, count, by, order):
        for at, line in ((0, lines[0]), (count + 1, lines[1])):
            put_shifted(dst, at, line.astype(F32), by, order)

    def for_blocks(count, size, body):
        size = min(size, count)

        def step(i, carry):
            body(pl.multiple_of(i * size, size), size)
            return carry

        lax.fori_loop(0, count // size, step, 0)

    def channel_blocks():
        return [slice(16 * c, 16 * c + 16) for c in range(CH // 16)]

    def make_norm(layer, t, sums, squares, count):
        size = CH // GROUPS * count * LANES * parts
        mean = sums / size
        inverse = lax.rsqrt(squares / size - mean * mean + EPS_NORM)
        coef[0] = spread(inverse)
        coef[1] = spread(-mean * inverse)
        coef[2] = norms[0, layer]
        coef[3] = norms[1, layer]
        inv_kept[t, layer] = coef[0]

    def activate(z, c):
        xhat = z * coef[0, c] + coef[1, c]
        n = xhat * coef[2, c] + coef[3, c]
        return xhat, n * (0.5 * jnp.tanh(0.5 * n) + 0.5)

    def conv_sums(count, size, rows_of):
        size = min(size, count)
        zero = jnp.zeros((CH, LANES), F32)

        def step(i, carry):
            sums, squares = carry
            base = pl.multiple_of(i * size, size)
            for j, z in enumerate(rows_of(base, size)):
                zbuf[base + j] = z
                sums = sums + z
                squares = squares + z * z
            return sums, squares

        return lax.fori_loop(0, count // size, step, (zero, zero))

    def tap_rows(y, j, at):
        return y[at * CH : (at + 1) * CH, j * LANES : (j + 1) * LANES]

    def conv_of(src, layer):
        def rows_of(base, size):
            y = nn_dot(wf[layer], beside([src[base + j] for j in range(size + 2)]))
            return [
                tap_rows(y, j, 0) + tap_rows(y, j + 1, 1) + tap_rows(y, j + 2, 2)
                for j in range(size)
            ]

        return rows_of

    def conv_last(base, size):
        y = nn_dot(wf[4], beside([sg[base + j] for j in range(size + 2)]))
        low = base // 2
        x = nn_dot(wf[3], beside([sgh[low + j] for j in range(size // 2 + 2)]))
        result = []
        for j in range(size):
            z = tap_rows(y, j, 0) + tap_rows(y, j + 1, 1) + tap_rows(y, j + 2, 2)
            for ky in range(3):
                z = z + tap_rows(x, (j + ky - 1) // 2 + 1, ky)
            result.append(z)
        return result

    def finish_plain(t, layer, count, kept, xh, xh_at, dst, by, slot):
        def edge(which, line):
            xhat, h = activate(zbuf[line], slice(0, CH))
            edges[slot, which] = h.astype(BF)

        edge(0, 0)
        edge(1, count - 1)
        args = (slot, edges.at[slot, 0], edges.at[slot, 1], kept.at[t, 0], kept.at[t, count + 1])
        halo_start(*args)

        def block(base, size):
            for c in channel_blocks():
                xhat, h = activate(zbuf[pl.ds(base, size), c, :], c)
                xh[xh_at, t, pl.ds(base, size), c, :] = xhat.astype(BF)
                low = h.astype(BF)
                kept[t, pl.ds(base + 1, size), c, :] = low
                at = pl.ds(base + 1, size)
                dst[at, c, :] = from_left(h, by).astype(BF)
                dst[at, slice(CH + c.start, CH + c.stop), :] = low
                dst[at, slice(2 * CH + c.start, 2 * CH + c.stop), :] = from_right(h, by).astype(BF)

        for_blocks(count, 8, block)
        halo_wait(*args)
        spread_halo(dst, (kept[t, 0], kept[t, count + 1]), count, by, FORWARD)

    def pool_of(first, second):
        pair = first.astype(BF).astype(F32) + second.astype(BF).astype(F32)
        return 0.25 * pair_sum(pair)

    def finish_skip(t):
        def edge(which, line):
            xhat, first = activate(zbuf[line], slice(0, CH))
            xhat, second = activate(zbuf[line + 1], slice(0, CH))
            edges[1, which] = (first, second)[which].astype(BF)
            edges[2, which] = pool_of(first, second).astype(BF)

        edge(0, 0)
        edge(1, rows - 2)
        skip_args = (1, edges.at[1, 0], edges.at[1, 1], skip.at[t, 0], skip.at[t, rows + 1])
        pool_args = (2, edges.at[2, 0], edges.at[2, 1], pooled.at[t, 0], pooled.at[t, half + 1])
        halo_start(*pool_args)
        halo_start(*skip_args)

        def block(base, size):
            for c in channel_blocks():
                xhat, h = activate(zbuf[pl.ds(base, size), c, :], c)
                xh_full[1, t, pl.ds(base, size), c, :] = xhat.astype(BF)
                low = h.astype(BF)
                at = pl.ds(base + 1, size)
                skip[t, at, c, :] = low
                sg[at, c, :] = from_left(h, 1).astype(BF)
                sg[at, slice(CH + c.start, CH + c.stop), :] = low
                sg[at, slice(2 * CH + c.start, 2 * CH + c.stop), :] = from_right(h, 1).astype(BF)
                pairs = low.astype(F32).reshape(size // 2, 2, 16, LANES)
                mean = 0.25 * pair_sum(pairs[:, 0] + pairs[:, 1])
                at = pl.ds(base // 2 + 1, size // 2)
                small = mean.astype(BF)
                pooled[t, at, c, :] = small
                sgh[at, c, :] = from_left(mean, 2).astype(BF)
                sgh[at, slice(CH + c.start, CH + c.stop), :] = small
                sgh[at, slice(2 * CH + c.start, 2 * CH + c.stop), :] = from_right(mean, 2).astype(BF)

        for_blocks(rows, 8, block)
        halo_wait(*pool_args)
        halo_wait(*skip_args)
        spread_halo(sgh, (pooled[t, 0], pooled[t, half + 1]), half, 2, FORWARD)
        spread_halo(sg, (skip[t, 0], skip[t, rows + 1]), rows, 1, FORWARD)

    def finish_last(t):
        def block(base, size):
            lows = []
            for c in channel_blocks():
                xhat, h = activate(zbuf[pl.ds(base, size), c, :], c)
                xh_full[2, t, pl.ds(base, size), c, :] = xhat.astype(BF)
                lows.append(h.astype(BF))
            low = jnp.concatenate(lows, axis=1)
            force = nn_dot(headf[...], beside([low[j] for j in range(size)]))
            for j in range(size):
                frows[base + j] = force[:, j * LANES : (j + 1) * LANES]

        for_blocks(rows, 8, block)

    def forward_step(t, carry):
        for c in range(2):
            field = u_ext[c]
            for kx, moved in enumerate((from_left(field, 1), field, from_right(field, 1))):
                s0[:, 3 * kx + c, :] = moved
        s0b[t] = s0[...].astype(BF)

        def first_rows(base, size):
            x = beside(
                [s0b[t, pl.ds(base + EDGE - 1 + j, 3)].reshape(48, LANES) for j in range(size)]
            )
            z = nn_dot(w0f[...], x)
            return [z[:, j * LANES : (j + 1) * LANES] for j in range(size)]

        make_norm(0, t, *group_totals(0, *conv_sums(rows, 16, first_rows)), rows)
        finish_plain(t, 0, rows, h1, xh_full, 0, sg, 1, 0)
        make_norm(1, t, *group_totals(1, *conv_sums(rows, 16, conv_of(sg, 0))), rows)
        finish_skip(t)
        make_norm(2, t, *group_totals(2, *conv_sums(half, 16, conv_of(sgh, 1))), half)
        finish_plain(t, 2, half, h3, xh_half, 0, sgh, 2, 3)
        make_norm(3, t, *group_totals(3, *conv_sums(half, 16, conv_of(sgh, 2))), half)
        finish_plain(t, 3, half, h4, xh_half, 1, sgh, 1, 4)
        make_norm(4, t, *group_totals(4, *conv_sums(rows, 16, conv_last)), rows)
        finish_last(t)

        for c in range(2):
            force = frows[:, c, :] + bias[c]
            q_ext[t, c, own, :] = (u_ext[c, own, :] + DT_FORCE * force) * opened[own, :]
        ext_halo(11, q_ext.at[t])
        qr, qc = q_ext[t, 0], q_ext[t, 1]
        grid = grid_mask[...]
        vr = grid * (qr - DT_ADV * (qr * drows(qr) + qc * dcols(qr)))
        vc = grid * (qc - DT_ADV * (qr * drows(qc) + qc * dcols(qc)))
        facts = m_own[0]
        at = (t + 1).astype(F32)
        for c, moved in enumerate(project(vr, vc, grid)):
            u_ext[c] = opened[...] * moved
            u_now = u_ext[c, own, :]
            u_kept[t, c] = u_now
            for k in range(2):
                live = (facts[k : k + 1] == at).astype(F32)
                miss = u_now - t_own[k, c]
                misc[0] += sublanes(live * opened[own, :] * miss * miss)
        return carry

    lax.fori_loop(0, STEPS, forward_step, 0)

    def bar_block(layer, xh, xh_at, t, base, size, c, h_bar):
        xhat = xh[xh_at, t, pl.ds(base, size), c, :].astype(F32)
        n = xhat * norms[0, layer, c] + norms[1, layer, c]
        sig = 0.5 * jnp.tanh(0.5 * n) + 0.5
        n_bar = h_bar * (sig * (1.0 + n * (1.0 - sig)))
        zbuf[pl.ds(base, size), c, :] = n_bar
        acc[0, c, :] += jnp.sum(n_bar, axis=0)
        acc[1, c, :] += jnp.sum(n_bar * xhat, axis=0)
        return n * sig

    def first_pass(layer, t, count, xh, xh_at, h_bar_of):
        acc[...] = jnp.zeros_like(acc)

        def block(base, size):
            for c in channel_blocks():
                bar_block(layer, xh, xh_at, t, base, size, c, h_bar_of(base, size, c))

        for_blocks(count, 8, block)

    def first_pass_last(t):
        acc[...] = jnp.zeros_like(acc)

        def block(base, size):
            low = beside([frows[base + j].astype(BF) for j in range(size)])
            h_bar = nn_dot(headb[...], low)
            lows = []
            for c in channel_blocks():
                bar = jnp.stack(
                    [h_bar[c, j * LANES : (j + 1) * LANES] for j in range(size)], axis=0
                )
                h = bar_block(4, xh_full, 2, t, base, size, c, bar)
                lows.append(h.astype(BF))
            h = jnp.concatenate(lows, axis=1)
            ghead[...] += nt_dot(low, beside([h[j] for j in range(size)]))

        for_blocks(rows, 8, block)

    def second_pass(layer, t, count, xh, xh_at, dst, by):
        gain = norms[0, layer]
        sums, cross = acc[0], acc[1]
        gnorm[0, layer] += cross
        gnorm[1, layer] += sums
        size_all = CH // GROUPS * count * LANES * parts
        total, total_cross = group_totals(5 + layer, gain * sums, gain * cross)
        inverse = inv_kept[t, layer]
        coef[0] = gain * inverse
        coef[1] = -inverse * spread(total_cross / size_all)
        coef[2] = -inverse * spread(total / size_all)

        def z_bar(at, c):
            xhat = xh[xh_at, t, at, c, :].astype(F32)
            return zbuf[at, c, :] * coef[0, c] + xhat * coef[1, c] + coef[2, c]

        slot = 5 + layer
        for which, line in enumerate((0, count - 1)):
            edges[slot, which] = z_bar(line, slice(0, CH)).astype(BF)
        args = (
            slot,
            edges.at[slot, 0],
            edges.at[slot, 1],
            g_halo.at[layer, 0],
            g_halo.at[layer, 1],
        )
        halo_start(*args)

        def block(base, size):
            at = pl.ds(base + 1, size)
            for c in channel_blocks():
                z = z_bar(pl.ds(base, size), c)
                dst[at, slice(CH + c.start, CH + c.stop), :] = z.astype(BF)
                if by:
                    dst[at, c, :] = from_right(z, by).astype(BF)
                    right = slice(2 * CH + c.start, 2 * CH + c.stop)
                    dst[at, right, :] = from_left(z, by).astype(BF)

        for_blocks(count, 8, block)
        halo_wait(*args)
        if by:
            spread_halo(dst, (g_halo[layer, 0], g_halo[layer, 1]), count, by, BACKWARD)
        else:
            dst[0, CH : 2 * CH, :] = g_halo[layer, 0]
            dst[count + 1, CH : 2 * CH, :] = g_halo[layer, 1]

    def bar_rows(weight, g, size):
        y = nn_dot(weight, g)
        return [
            tap_rows(y, j + 2, 0) + tap_rows(y, j + 1, 1) + tap_rows(y, j, 2) for j in range(size)
        ]

    def products(t, layer, count, src, kept, out):
        def block(base, size):
            g = beside([src[base + j] for j in range(size + 2)])
            for j, bar in enumerate(bar_rows(wb[layer], g, size)):
                out[base + j] = bar
            h = beside([kept[t, pl.ds(base + j, 3)].reshape(3 * CH, LANES) for j in range(size)])
            gw[layer] += nt_dot(g[:, LANES : (size + 1) * LANES], h)

        for_blocks(count, 16, block)

    def products_last(t):
        def block(base, size):
            g = beside([sg[base + j] for j in range(size + 2)])
            inner = g[:, LANES : (size + 1) * LANES]
            low = base // 2
            for j, bar in enumerate(bar_rows(wb[4], g, size)):
                skip_bar[base + j] = bar
            ups = bar_rows(wb[3], g, size)
            for j in range(size // 2):
                half_bar[low + j] = pair_sum(ups[2 * j] + ups[2 * j + 1])
            h = beside([skip[t, pl.ds(base + j, 3)].reshape(3 * CH, LANES) for j in range(size)])
            gw[4] += nt_dot(inner, h)
            up = beside(
                [
                    jnp.concatenate([h4[t, low + (j + ky - 1) // 2 + 1] for ky in range(3)], axis=0)
                    for j in range(size)
                ]
            )
            gw[3] += nt_dot(inner, up)

        for_blocks(rows, 16, block)

    def products_first(t):
        def block(base, size):
            g = beside([sg[base + j, CH : 2 * CH, :] for j in range(size)])
            y = nn_dot(w0b[...], g)
            for j in range(size):
                taps[base + j] = y[:, j * LANES : (j + 1) * LANES]

        for_blocks(rows, 16, block)
        g = beside([sg[rows + j, CH : 2 * CH, :] for j in range(2)])
        y = nn_dot(w0b[...], g)
        for j in range(2):
            taps[rows + j] = y[:, j * LANES : (j + 1) * LANES]

        def weights(base, size):
            g = beside([sg[base + 1 + j, CH : 2 * CH, :] for j in range(size)])
            x = beside(
                [s0b[t, pl.ds(base + EDGE - 1 + j, 3)].reshape(48, LANES) for j in range(size)]
            )
            gw0[...] += nt_dot(g, x)

        for_blocks(rows, 16, weights)

    def backward_step(i, carry):
        t = STEPS - 1 - i
        facts = m_own[0]
        at = (t + 1).astype(F32)
        open_own = opened[own, :]
        for c in range(2):
            pull = jnp.zeros((rows, LANES), F32)
            for k in range(2):
                live = (facts[k : k + 1] == at).astype(F32)
                pull = pull + live * (u_kept[t, c] - t_own[k, c])
            w_ext[c, own, :] = open_own * (u_bar[c] + 2.0 * open_own * pull)
        ext_halo(12, w_ext)
        grid = grid_mask[...]
        gr, gc = project(w_ext[0], w_ext[1], grid)
        gr, gc = grid * gr, grid * gc
        qr, qc = q_ext[t, 0], q_ext[t, 1]
        bar_r = gr + DT_ADV * (
            drows(gr * qr) + dcols(gr * qc) - (gr * drows(qr) + gc * drows(qc))
        )
        bar_c = gc + DT_ADV * (
            drows(gc * qr) + dcols(gc * qc) - (gr * dcols(qr) + gc * dcols(qc))
        )
        for c, bar in enumerate((bar_r, bar_c)):
            passed = opened[...] * bar
            q_ext[t, c] = passed
            passed = q_ext[t, c, own, :]
            u_bar[c] = passed
            force_bar = DT_FORCE * passed
            misc[2 + c] += sublanes(force_bar)
            frows[:, c, :] = force_bar
        for c in range(2, 16):
            frows[:, c, :] = jnp.zeros((rows, LANES), F32)

        first_pass_last(t)
        second_pass(4, t, rows, xh_full, 2, sg, 1)
        products_last(t)
        first_pass(3, t, half, xh_half, 1, lambda b, s, c: half_bar[pl.ds(b, s), c, :])
        second_pass(3, t, half, xh_half, 1, sgh, 2)
        products(t, 2, half, sgh, h3, half_bar)
        first_pass(2, t, half, xh_half, 0, lambda b, s, c: half_bar[pl.ds(b, s), c, :])
        second_pass(2, t, half, xh_half, 0, sgh, 2)
        products(t, 1, half, sgh, pooled, half_bar)

        def skip_total(base, size, c):
            bars = skip_bar[pl.ds(base, size), c, :].reshape(size // 2, 2, 16, LANES)
            small = half_bar[pl.ds(base // 2, size // 2), c, :]
            return (bars + 0.25 * small[:, None]).reshape(size, 16, LANES)

        first_pass(1, t, rows, xh_full, 1, skip_total)
        second_pass(1, t, rows, xh_full, 1, sg, 1)
        products(t, 0, rows, sg, h1, skip_bar)
        first_pass(0, t, rows, xh_full, 0, lambda b, s, c: skip_bar[pl.ds(b, s), c, :])
        second_pass(0, t, rows, xh_full, 0, sg, 0)
        products_first(t)
        for c in range(2):
            columns = []
            for kx in range(3):
                total = jnp.zeros((rows, LANES), F32)
                for ky in range(3):
                    total = total + taps[pl.ds(2 - ky, rows), 16 * ky + 3 * kx + c, :]
                columns.append(total)
            u_bar[c] += from_right(columns[0], 1) + columns[1] + from_left(columns[2], 1)
        return carry

    lax.fori_loop(0, STEPS, backward_step, 0)


def train(velocity, targets, meta, wf, wb, w0f, w0b, norms, headf, headb, bias):
    ranks = lax.axis_size("rows")
    parts = ranks // 2
    tile = velocity.shape[2]
    rows, half, ext = 2 * tile, tile, 2 * tile + 2 * EDGE
    vmem = pl.BlockSpec(memory_space=pltpu.VMEM)

    def kept(count):
        return pltpu.VMEM((STEPS, count + 2, CH, LANES), BF)

    args = (velocity, targets, meta, wf, wb, w0f, w0b, norms, headf, headb, bias)
    return pl.pallas_call(
        functools.partial(train_kernel, ranks),
        out_shape=(
            jax.ShapeDtypeStruct((LAYERS + 1, 3 * CH, 3 * CH), F32),
            jax.ShapeDtypeStruct((CH, 48), F32),
            jax.ShapeDtypeStruct((2, LAYERS + 1, CH, LANES), F32),
            jax.ShapeDtypeStruct((16, CH), F32),
            jax.ShapeDtypeStruct((4, 8, LANES), F32),
        ),
        in_specs=[vmem] * len(args),
        out_specs=(vmem,) * 5,
        scratch_shapes=[
            pltpu.VMEM((2, ext, LANES), F32),
            pltpu.VMEM((2, 2, rows, LANES), F32),
            pltpu.VMEM((2, 16, LANES), F32),
            pltpu.VMEM((ext, LANES), F32),
            pltpu.VMEM((ext, LANES), F32),
            pltpu.VMEM((ext, 16, LANES), F32),
            pltpu.VMEM((STEPS, ext, 16, LANES), BF),
            pltpu.VMEM((STEPS, 2, ext, LANES), F32),
            pltpu.VMEM((STEPS, 2, rows, LANES), F32),
            pltpu.VMEM((2, ext, LANES), F32),
            pltpu.VMEM((2, rows, LANES), F32),
            pltpu.VMEM((rows, 16, LANES), F32),
            pltpu.VMEM((rows + 2, 48, LANES), F32),
            kept(rows),
            kept(rows),
            kept(half),
            kept(half),
            kept(half),
            pltpu.VMEM((3, STEPS, rows, CH, LANES), BF),
            pltpu.VMEM((2, STEPS, half, CH, LANES), BF),
            pltpu.VMEM((STEPS, LAYERS + 1, CH, LANES), F32),
            pltpu.VMEM((rows, CH, LANES), F32),
            pltpu.VMEM((rows, CH, LANES), F32),
            pltpu.VMEM((half, CH, LANES), F32),
            pltpu.VMEM((rows + 2, 3 * CH, LANES), BF),
            pltpu.VMEM((half + 2, 3 * CH, LANES), BF),
            pltpu.VMEM((10, 2, CH, LANES), BF),
            pltpu.VMEM((LAYERS + 1, 2, CH, LANES), BF),
            pltpu.VMEM((4, CH, LANES), F32),
            pltpu.VMEM((2, CH, LANES), F32),
            pltpu.VMEM((10, 16, LANES), F32),
            pltpu.VMEM((10, parts - 1, 16, LANES), F32),
            pltpu.SemaphoreType.DMA((2, 3)),
            pltpu.SemaphoreType.DMA((2, 3)),
            pltpu.SemaphoreType.DMA((3,)),
            pltpu.SemaphoreType.DMA((13, 2)),
            pltpu.SemaphoreType.DMA((13, 2)),
            pltpu.SemaphoreType.DMA((10, parts - 1)),
            pltpu.SemaphoreType.DMA((10, parts - 1)),
        ],
        compiler_params=pltpu.CompilerParams(
            collective_id=0, has_side_effects=True, vmem_limit_bytes=60 * 2**20
        ),
        name="train",
    )(*args)


def shards(
    velocity,
    targets,
    keyframes,
    boxes,
    w_in,
    w_mid,
    norm_params,
    head_params,
    m_in,
    m_mid,
    m_norm,
    m_head,
    v_in,
    v_mid,
    v_norm,
    v_head,
):
    samples = velocity.shape[0]
    facts = jnp.concatenate(
        [keyframes, boxes.reshape(samples, 8), jnp.zeros((samples, 6), jnp.int32)], axis=1
    ).astype(F32)
    meta = jnp.broadcast_to(facts[:, :, None], (samples, 16, LANES))
    mid = w_mid.reshape(LAYERS + 1, 3, 3, CH, CH)
    wf = jnp.transpose(mid, (0, 1, 3, 2, 4)).reshape(LAYERS + 1, 3 * CH, 3 * CH).astype(BF)
    wb = jnp.transpose(mid, (0, 1, 4, 2, 3)).reshape(LAYERS + 1, 3 * CH, 3 * CH).astype(BF)
    first = jnp.transpose(w_in, (0, 2, 3, 1)).reshape(CH, 3, 9)
    w0f = jnp.pad(first, ((0, 0), (0, 0), (0, 7))).reshape(CH, 48).astype(BF)
    norms = jnp.broadcast_to(norm_params[..., None], norm_params.shape + (LANES,))
    headf = jnp.pad(head_params[:, :CH], ((0, 14), (0, 0))).astype(BF)
    bias = jnp.broadcast_to(head_params[:, CH:, None], (2, 1, LANES))
    gw, gw0, gnorm, ghead, misc = train(
        velocity, targets, meta, wf, wb, w0f, w0f.T, norms, headf, headf.T, bias
    )
    halves = jnp.array([1.0, 0.5, 0.5, 1.0, 1.0], F32)
    g_mid = jnp.transpose(
        gw.reshape(LAYERS + 1, 3, CH, 3, CH) * halves[:, None, None, None, None], (0, 3, 1, 2, 4)
    ).reshape(w_mid.shape)
    g_in = jnp.transpose(gw0.reshape(CH, 3, 16)[:, :, :9].reshape(CH, 3, 3, 3), (0, 3, 1, 2))
    layer_halves = jnp.array([1.0, 1.0, 0.5, 0.5, 1.0], F32)
    g_norm = jnp.sum(gnorm, axis=-1) * layer_halves[None, :, None]
    sums = jnp.sum(misc, axis=(1, 2))
    g_head = jnp.concatenate([ghead[:2], sums[2:4, None]], axis=1)
    grads_in, grads_mid, grads_norm, grads_head, totals = lax.psum(
        (g_in, g_mid, g_norm, g_head, sums[:2]), ("batch", "rows")
    )
    loss_sum, count = totals[0], totals[1]
    grads = tuple(g / count for g in (grads_in, grads_mid, grads_norm, grads_head))
    params = (w_in, w_mid, norm_params, head_params)
    norm = jnp.sqrt(sum((jnp.sum(g * g) for g in grads)))
    scale = jnp.minimum(1.0, CLIP_NORM / norm)
    new_w, new_m, new_v = ([], [], [])
    for weight, moment, second, g, rate in zip(
        params, (m_in, m_mid, m_norm, m_head), (v_in, v_mid, v_norm, v_head), grads, RATES
    ):
        g = g * scale
        moment_new = BETA_ONE * moment + (1 - BETA_ONE) * g
        second_new = BETA_TWO * second + (1 - BETA_TWO) * g * g
        mhat = moment_new / (1 - BETA_ONE**STEP_NUM)
        vhat = second_new / (1 - BETA_TWO**STEP_NUM)
        new_w.append(weight - rate * (mhat / (jnp.sqrt(vhat) + ADAM_EPS) + DECAY * weight))
        new_m.append(moment_new)
        new_v.append(second_new)
    return (
        *new_w,
        *new_m,
        *new_v,
        new_w[0].astype(BF),
        new_w[1].astype(BF),
        new_w[3].astype(BF),
        loss_sum,
        count,
        norm,
    )


def solution(mesh):
    return jax.shard_map(
        shards,
        mesh=mesh,
        in_specs=(
            P("batch", None, "rows", None),
            P("batch", None, None, "rows", None),
            P("batch", None),
            P("batch", None, None),
        )
        + (P(),) * 12,
        out_specs=(P(),) * 18,
        check_vma=False,
    )
```

```python
import functools

import jax
import jax.numpy as jnp
from jax import lax
from jax.experimental import pallas as pl
from jax.experimental.pallas import tpu as pltpu
from jax.sharding import PartitionSpec as P

CH = 64
GROUPS = 8
LAYERS = 4
STEPS = 4
JACOBI = 4
STEP_NUM = 10
LANES = 128
EDGE = 8

EPS_NORM = 1e-05
DT_FORCE = 0.5
DT_ADV = 0.2
CLIP_NORM = 0.001
BETA_ONE = 0.9
BETA_TWO = 0.95
ADAM_EPS = 1e-08
DECAY = 0.01
RATES = (0.2, 0.05, 1.0, 0.15)

BF = jnp.bfloat16
F32 = jnp.float32
MESH = pl.DeviceIdType.MESH
FULL_SLOT = {0: 0, 1: 1, 4: 2}
HALF_SLOT = {2: 0, 3: 1}


def nt_dot(a, b):
    return lax.dot_general(a, b, (((1,), (1,)), ((), ())), preferred_element_type=F32)


def nn_dot(a, b):
    return jnp.dot(a, b, preferred_element_type=F32)


def beside(rows):
    return jnp.concatenate(rows, axis=1)


def lane_of(shape):
    return lax.broadcasted_iota(jnp.int32, shape, len(shape) - 1)


def from_left(x, by):
    return jnp.where(lane_of(x.shape) < by, 0.0, pltpu.roll(x, by, x.ndim - 1))


def from_right(x, by):
    return jnp.where(
        lane_of(x.shape) >= LANES - by, 0.0, pltpu.roll(x, LANES - by, x.ndim - 1)
    )


def pair_sum(x):
    even = lane_of(x.shape) % 2 == 0
    last = x.ndim - 1
    return x + jnp.where(even, pltpu.roll(x, LANES - 1, last), pltpu.roll(x, 1, last))


def drows(x):
    count = x.shape[0]
    return 0.5 * (pltpu.roll(x, count - 1, 0) - pltpu.roll(x, 1, 0))


def dcols(x):
    return 0.5 * (from_right(x, 1) - from_left(x, 1))


def nsum(x):
    count = x.shape[0]
    return (
        pltpu.roll(x, count - 1, 0) + pltpu.roll(x, 1, 0) + from_right(x, 1) + from_left(x, 1)
    )


def project(vr, vc, grid):
    div = grid * (drows(vr) + dcols(vc))
    press = -0.25 * div
    for sweep in range(JACOBI - 1):
        press = grid * (0.25 * (nsum(press) - div))
    return vr - drows(press), vc - dcols(press)


def sublanes(x):
    return jnp.sum(x.reshape(x.shape[0] // 8, 8, LANES), axis=0)


def group_rows(x):
    return jnp.sum(x.reshape(GROUPS, CH // GROUPS, LANES), axis=1)


def spread(x):
    return jnp.concatenate(
        [jnp.broadcast_to(x[g : g + 1], (CH // GROUPS, LANES)) for g in range(GROUPS)], axis=0
    )


def train_kernel(
    ranks,
    planes,
    vel,
    tgt,
    meta,
    wf,
    wb,
    w0f,
    w0b,
    norms,
    headf,
    headb,
    bias,
    g_all,
    scalars,
    gw,
    gw0,
    gnorm,
    ghead,
    misc,
    u_ext,
    t_own,
    m_own,
    opened,
    grid_mask,
    s0,
    s0b,
    q_ext,
    u_kept,
    w_ext,
    u_bar,
    frows,
    taps,
    h1,
    skip,
    pooled,
    h3,
    h4,
    xh_full,
    xh_half,
    inv_kept,
    zbuf,
    skip_bar,
    half_bar,
    sg,
    sgh,
    edges,
    g_halo,
    coef,
    acc,
    st_send,
    st_recv,
    g_send,
    p_recv,
    z_send,
    z_recv,
    m_plane,
    m_line,
    in_send,
    in_recv,
    in_local,
    halo_send,
    halo_recv,
    st_ss,
    st_rs,
    p_ss,
    p_rs,
    z_ss,
    z_rs,
):
    quarter = ranks // 4
    parts = ranks // 2
    tile = vel.shape[2]
    rows = 2 * tile
    half = rows // 2
    batch_at = lax.axis_index("batch")
    row_at = lax.axis_index("rows")
    core = lax.rem(batch_at, 2)
    plane = batch_at - core
    sample = row_at // quarter
    part = 2 * lax.rem(row_at, quarter) + core

    def owner(which, piece):
        return (plane + lax.rem(piece, 2), which * quarter + piece // 2)

    u_ext[...] = jnp.zeros_like(u_ext)
    q_ext[...] = jnp.zeros_like(q_ext)
    w_ext[...] = jnp.zeros_like(w_ext)
    g_halo[...] = jnp.zeros_like(g_halo)
    for kept, count in ((h1, rows), (skip, rows), (pooled, half), (h3, half), (h4, half)):
        for t in range(STEPS):
            kept[t, 0] = jnp.zeros((CH, LANES), BF)
            kept[t, count + 1] = jnp.zeros((CH, LANES), BF)

    barrier = pltpu.get_barrier_semaphore()
    members = 2 * ranks
    mine = core * ranks + row_at

    def plane_id(d):
        other = lax.rem(mine + d, members)
        return (plane + other // ranks, lax.rem(other, ranks))

    def greet(d, carry):
        pl.semaphore_signal(barrier, inc=1, device_id=plane_id(d), device_id_type=MESH)
        return carry

    lax.fori_loop(1, members, greet, 0)
    level = batch_at // 2

    def line_id(d):
        return (2 * lax.rem(level + d, planes) + core, row_at)

    def greet_line(d, carry):
        pl.semaphore_signal(barrier, inc=1, device_id=line_id(d), device_id_type=MESH)
        return carry

    lax.fori_loop(1, planes, greet_line, 0)
    pl.semaphore_wait(barrier, members + planes - 2)

    def incoming(place):
        at = pl.ds(pl.multiple_of(EDGE + place * tile, 8), tile)
        here = pl.ds(pl.multiple_of(place * tile, 8), tile)
        return u_ext.at[:, at, :], t_own.at[:, :, here, :], m_own.at[place]

    place = lax.rem(row_at, 2)
    for j in range(2):
        to_batch, to_row = owner(2 * core + j, row_at // 2)
        stays = (to_batch == batch_at) & (to_row == row_at)
        for k, (src, dst) in enumerate(zip((vel.at[j], tgt.at[j], meta.at[j]), incoming(place))):

            @pl.when(stays)
            def _():
                pltpu.make_async_copy(src, dst, in_local.at[k]).start()

            @pl.when(jnp.logical_not(stays))
            def _():
                pltpu.make_async_remote_copy(
                    src_ref=src,
                    dst_ref=dst,
                    send_sem=in_send.at[j, k],
                    recv_sem=in_recv.at[place, k],
                    device_id=(to_batch, to_row),
                    device_id_type=MESH,
                ).start()

    for j in range(2):
        to_batch, to_row = owner(2 * core + j, row_at // 2)
        stays = (to_batch == batch_at) & (to_row == row_at)
        for k, src in enumerate((vel.at[j], tgt.at[j], meta.at[j])):

            @pl.when(stays)
            def _():
                pltpu.make_async_copy(src, src, in_local.at[k]).wait()

            @pl.when(jnp.logical_not(stays))
            def _():
                pltpu.make_async_copy(src, src, in_send.at[j, k]).wait()

    for i in range(2):
        from_batch = plane + sample // 2
        from_row = 2 * part + i
        stays = (from_batch == batch_at) & (from_row == row_at)
        for k, dst in enumerate(incoming(i)):

            @pl.when(jnp.logical_not(stays))
            def _():
                pltpu.make_async_copy(dst, dst, in_recv.at[i, k]).wait()

    has_prev = part > 0
    has_next = part < parts - 1
    prev_id = owner(sample, jnp.maximum(part - 1, 0))
    next_id = owner(sample, jnp.minimum(part + 1, parts - 1))

    def halo_copies(slot, low_src, high_src, top_dst, bottom_dst):
        to_prev = pltpu.make_async_remote_copy(
            src_ref=low_src,
            dst_ref=bottom_dst,
            send_sem=halo_send.at[slot, 0],
            recv_sem=halo_recv.at[slot, 0],
            device_id=prev_id,
            device_id_type=MESH,
        )
        to_next = pltpu.make_async_remote_copy(
            src_ref=high_src,
            dst_ref=top_dst,
            send_sem=halo_send.at[slot, 1],
            recv_sem=halo_recv.at[slot, 1],
            device_id=next_id,
            device_id_type=MESH,
        )
        return to_prev, to_next

    def halo_start(*args):
        to_prev, to_next = halo_copies(*args)

        @pl.when(has_prev)
        def _():
            to_prev.start()

        @pl.when(has_next)
        def _():
            to_next.start()

    def halo_wait(*args):
        to_prev, to_next = halo_copies(*args)

        @pl.when(has_prev)
        def _():
            to_prev.wait_send()
            to_next.wait_recv()

        @pl.when(has_next)
        def _():
            to_next.wait_send()
            to_prev.wait_recv()

    def ext_halo(slot, ref):
        args = (
            slot,
            ref.at[:, pl.ds(EDGE, EDGE), :],
            ref.at[:, pl.ds(rows, EDGE), :],
            ref.at[:, pl.ds(0, EDGE), :],
            ref.at[:, pl.ds(rows + EDGE, EDGE), :],
        )
        halo_start(*args)
        halo_wait(*args)

    def group_totals(slot, first, second):
        local = jnp.concatenate([group_rows(first), group_rows(second)], axis=0)
        st_send[slot] = local
        copies = []
        for d in range(1, parts):
            copies.append(
                pltpu.make_async_remote_copy(
                    src_ref=st_send.at[slot],
                    dst_ref=st_recv.at[slot, d - 1],
                    send_sem=st_ss.at[slot, d - 1],
                    recv_sem=st_rs.at[slot, d - 1],
                    device_id=owner(sample, lax.rem(part + d, parts)),
                    device_id_type=MESH,
                )
            )
        for copy in copies:
            copy.start()
        total = local
        for d, copy in enumerate(copies):
            copy.wait()
            total = total + st_recv[slot, d]
        total = jnp.broadcast_to(jnp.sum(total, axis=1, keepdims=True), total.shape)
        return total[:GROUPS], total[GROUPS:]

    ext = rows + 2 * EDGE
    row_is = lax.broadcasted_iota(jnp.int32, (ext, LANES), 0) - EDGE + part * rows
    inside_grid = ((row_is >= 0) & (row_is < parts * rows)).astype(F32)
    row_f = row_is.astype(F32)
    col_f = lane_of((ext, LANES)).astype(F32)
    covered = jnp.zeros((ext, LANES), F32)
    facts = m_own[0]
    for b in range(2):
        bounds = [facts[2 + 4 * b + k : 3 + 4 * b + k] for k in range(4)]
        inside = (
            (row_f >= bounds[0])
            & (row_f < bounds[1])
            & (col_f >= bounds[2])
            & (col_f < bounds[3])
        )
        covered = jnp.maximum(covered, inside.astype(F32))
    grid_mask[...] = inside_grid
    opened[...] = inside_grid * (1.0 - covered)
    own = pl.ds(EDGE, rows)
    misc[...] = jnp.zeros_like(misc)
    live_slots = (facts[0:1] > 0.5).astype(F32) + (facts[1:2] > 0.5).astype(F32)
    misc[1] = sublanes(opened[own, :] * live_slots)
    gw[...] = jnp.zeros_like(gw)
    gw0[...] = jnp.zeros_like(gw0)
    gnorm[...] = jnp.zeros_like(gnorm)
    ghead[...] = jnp.zeros_like(ghead)
    s0[...] = jnp.zeros_like(s0)
    frows[...] = jnp.zeros_like(frows)
    u_bar[...] = jnp.zeros_like(u_bar)

    ext_halo(10, u_ext)

    for kx in range(3):
        field = opened[...]
        s0[:, 3 * kx + 2, :] = (from_left(field, 1), field, from_right(field, 1))[kx]

    def put_shifted(dst, at, x, by, order):
        copies = (from_left(x, by), x, from_right(x, by))
        for place_at, which in enumerate(order):
            dst[at, place_at * CH : (place_at + 1) * CH, :] = copies[which].astype(BF)

    FORWARD = (0, 1, 2)
    BACKWARD = (2, 1, 0)

    def spread_halo(dst, lines, count, by, order):
        for at, line in ((0, lines[0]), (count + 1, lines[1])):
            put_shifted(dst, at, line.astype(F32), by, order)

    def for_blocks(count, size, body):
        size = min(size, count)

        def step(i, carry):
            body(pl.multiple_of(i * size, size), size)
            return carry

        lax.fori_loop(0, count // size, step, 0)

    def channel_blocks():
        return [slice(16 * c, 16 * c + 16) for c in range(CH // 16)]

    def make_norm(layer, t, sums, squares, count):
        size = CH // GROUPS * count * LANES * parts
        mean = sums / size
        inverse = lax.rsqrt(squares / size - mean * mean + EPS_NORM)
        coef[0] = spread(inverse)
        coef[1] = spread(-mean * inverse)
        coef[2] = norms[0, layer]
        coef[3] = norms[1, layer]
        inv_kept[t, layer] = coef[0]

    def activate(z, c):
        xhat = z * coef[0, c] + coef[1, c]
        n = xhat * coef[2, c] + coef[3, c]
        return xhat, n * (0.5 * jnp.tanh(0.5 * n) + 0.5)

    def conv_sums(count, size, rows_of):
        size = min(size, count)
        zero = jnp.zeros((CH, LANES), F32)

        def step(i, carry):
            sums, squares = carry
            base = pl.multiple_of(i * size, size)
            for j, z in enumerate(rows_of(base, size)):
                zbuf[base + j] = z
                sums = sums + z
                squares = squares + z * z
            return sums, squares

        return lax.fori_loop(0, count // size, step, (zero, zero))

    def tap_rows(y, j, at):
        return y[at * CH : (at + 1) * CH, j * LANES : (j + 1) * LANES]

    def conv_of(src, layer):
        def rows_of(base, size):
            y = nn_dot(wf[layer], beside([src[base + j] for j in range(size + 2)]))
            return [
                tap_rows(y, j, 0) + tap_rows(y, j + 1, 1) + tap_rows(y, j + 2, 2)
                for j in range(size)
            ]

        return rows_of

    def conv_last(base, size):
        y = nn_dot(wf[4], beside([sg[base + j] for j in range(size + 2)]))
        low = base // 2
        x = nn_dot(wf[3], beside([sgh[low + j] for j in range(size // 2 + 2)]))
        result = []
        for j in range(size):
            z = tap_rows(y, j, 0) + tap_rows(y, j + 1, 1) + tap_rows(y, j + 2, 2)
            for ky in range(3):
                z = z + tap_rows(x, (j + ky - 1) // 2 + 1, ky)
            result.append(z)
        return result

    def finish_plain(t, layer, count, kept, xh, xh_at, dst, by, slot):
        def edge(which, line):
            xhat, h = activate(zbuf[line], slice(0, CH))
            edges[slot, which] = h.astype(BF)

        edge(0, 0)
        edge(1, count - 1)
        args = (slot, edges.at[slot, 0], edges.at[slot, 1], kept.at[t, 0], kept.at[t, count + 1])
        halo_start(*args)

        def block(base, size):
            for c in channel_blocks():
                xhat, h = activate(zbuf[pl.ds(base, size), c, :], c)
                xh[xh_at, t, pl.ds(base, size), c, :] = xhat.astype(BF)
                low = h.astype(BF)
                kept[t, pl.ds(base + 1, size), c, :] = low
                at = pl.ds(base + 1, size)
                dst[at, c, :] = from_left(h, by).astype(BF)
                dst[at, slice(CH + c.start, CH + c.stop), :] = low
                dst[at, slice(2 * CH + c.start, 2 * CH + c.stop), :] = from_right(h, by).astype(BF)

        for_blocks(count, 8, block)
        halo_wait(*args)
        spread_halo(dst, (kept[t, 0], kept[t, count + 1]), count, by, FORWARD)

    def pool_of(first, second):
        pair = first.astype(BF).astype(F32) + second.astype(BF).astype(F32)
        return 0.25 * pair_sum(pair)

    def finish_skip(t):
        def edge(which, line):
            xhat, first = activate(zbuf[line], slice(0, CH))
            xhat, second = activate(zbuf[line + 1], slice(0, CH))
            edges[1, which] = (first, second)[which].astype(BF)
            edges[2, which] = pool_of(first, second).astype(BF)

        edge(0, 0)
        edge(1, rows - 2)
        skip_args = (1, edges.at[1, 0], edges.at[1, 1], skip.at[t, 0], skip.at[t, rows + 1])
        pool_args = (2, edges.at[2, 0], edges.at[2, 1], pooled.at[t, 0], pooled.at[t, half + 1])
        halo_start(*pool_args)
        halo_start(*skip_args)

        def block(base, size):
            for c in channel_blocks():
                xhat, h = activate(zbuf[pl.ds(base, size), c, :], c)
                xh_full[1, t, pl.ds(base, size), c, :] = xhat.astype(BF)
                low = h.astype(BF)
                at = pl.ds(base + 1, size)
                skip[t, at, c, :] = low
                sg[at, c, :] = from_left(h, 1).astype(BF)
                sg[at, slice(CH + c.start, CH + c.stop), :] = low
                sg[at, slice(2 * CH + c.start, 2 * CH + c.stop), :] = from_right(h, 1).astype(BF)
                pairs = low.astype(F32).reshape(size // 2, 2, 16, LANES)
                mean = 0.25 * pair_sum(pairs[:, 0] + pairs[:, 1])
                at = pl.ds(base // 2 + 1, size // 2)
                small = mean.astype(BF)
                pooled[t, at, c, :] = small
                sgh[at, c, :] = from_left(mean, 2).astype(BF)
                sgh[at, slice(CH + c.start, CH + c.stop), :] = small
                sgh[at, slice(2 * CH + c.start, 2 * CH + c.stop), :] = from_right(mean, 2).astype(BF)

        for_blocks(rows, 8, block)
        halo_wait(*pool_args)
        halo_wait(*skip_args)
        spread_halo(sgh, (pooled[t, 0], pooled[t, half + 1]), half, 2, FORWARD)
        spread_halo(sg, (skip[t, 0], skip[t, rows + 1]), rows, 1, FORWARD)

    def finish_last(t):
        def block(base, size):
            lows = []
            for c in channel_blocks():
                xhat, h = activate(zbuf[pl.ds(base, size), c, :], c)
                xh_full[2, t, pl.ds(base, size), c, :] = xhat.astype(BF)
                lows.append(h.astype(BF))
            low = jnp.concatenate(lows, axis=1)
            force = nn_dot(headf[...], beside([low[j] for j in range(size)]))
            for j in range(size):
                frows[base + j] = force[:, j * LANES : (j + 1) * LANES]

        for_blocks(rows, 8, block)

    def forward_step(t, carry):
        for c in range(2):
            field = u_ext[c]
            for kx, moved in enumerate((from_left(field, 1), field, from_right(field, 1))):
                s0[:, 3 * kx + c, :] = moved
        s0b[t] = s0[...].astype(BF)

        def first_rows(base, size):
            x = beside(
                [s0b[t, pl.ds(base + EDGE - 1 + j, 3)].reshape(48, LANES) for j in range(size)]
            )
            z = nn_dot(w0f[...], x)
            return [z[:, j * LANES : (j + 1) * LANES] for j in range(size)]

        make_norm(0, t, *group_totals(0, *conv_sums(rows, 16, first_rows)), rows)
        finish_plain(t, 0, rows, h1, xh_full, 0, sg, 1, 0)
        make_norm(1, t, *group_totals(1, *conv_sums(rows, 16, conv_of(sg, 0))), rows)
        finish_skip(t)
        make_norm(2, t, *group_totals(2, *conv_sums(half, 16, conv_of(sgh, 1))), half)
        finish_plain(t, 2, half, h3, xh_half, 0, sgh, 2, 3)
        make_norm(3, t, *group_totals(3, *conv_sums(half, 16, conv_of(sgh, 2))), half)
        finish_plain(t, 3, half, h4, xh_half, 1, sgh, 1, 4)
        make_norm(4, t, *group_totals(4, *conv_sums(rows, 16, conv_last)), rows)
        finish_last(t)

        for c in range(2):
            force = frows[:, c, :] + bias[c]
            q_ext[t, c, own, :] = (u_ext[c, own, :] + DT_FORCE * force) * opened[own, :]
        ext_halo(11, q_ext.at[t])
        qr, qc = q_ext[t, 0], q_ext[t, 1]
        grid = grid_mask[...]
        vr = grid * (qr - DT_ADV * (qr * drows(qr) + qc * dcols(qr)))
        vc = grid * (qc - DT_ADV * (qr * drows(qc) + qc * dcols(qc)))
        facts = m_own[0]
        at = (t + 1).astype(F32)
        for c, moved in enumerate(project(vr, vc, grid)):
            u_ext[c] = opened[...] * moved
            u_now = u_ext[c, own, :]
            u_kept[t, c] = u_now
            for k in range(2):
                live = (facts[k : k + 1] == at).astype(F32)
                miss = u_now - t_own[k, c]
                misc[0] += sublanes(live * opened[own, :] * miss * miss)
        return carry

    lax.fori_loop(0, STEPS, forward_step, 0)

    def bar_block(layer, xh, xh_at, t, base, size, c, h_bar):
        xhat = xh[xh_at, t, pl.ds(base, size), c, :].astype(F32)
        n = xhat * norms[0, layer, c] + norms[1, layer, c]
        sig = 0.5 * jnp.tanh(0.5 * n) + 0.5
        n_bar = h_bar * (sig * (1.0 + n * (1.0 - sig)))
        zbuf[pl.ds(base, size), c, :] = n_bar
        acc[0, c, :] += jnp.sum(n_bar, axis=0)
        acc[1, c, :] += jnp.sum(n_bar * xhat, axis=0)
        return n * sig

    def first_pass(layer, t, count, xh, xh_at, h_bar_of):
        acc[...] = jnp.zeros_like(acc)

        def block(base, size):
            for c in channel_blocks():
                bar_block(layer, xh, xh_at, t, base, size, c, h_bar_of(base, size, c))

        for_blocks(count, 8, block)

    def first_pass_last(t):
        acc[...] = jnp.zeros_like(acc)

        def block(base, size):
            low = beside([frows[base + j].astype(BF) for j in range(size)])
            h_bar = nn_dot(headb[...], low)
            lows = []
            for c in channel_blocks():
                bar = jnp.stack(
                    [h_bar[c, j * LANES : (j + 1) * LANES] for j in range(size)], axis=0
                )
                h = bar_block(4, xh_full, 2, t, base, size, c, bar)
                lows.append(h.astype(BF))
            h = jnp.concatenate(lows, axis=1)
            ghead[...] += nt_dot(beside([h[j] for j in range(size)]), low)

        for_blocks(rows, 8, block)

    def second_pass(layer, t, count, xh, xh_at, dst, by):
        gain = norms[0, layer]
        sums, cross = acc[0], acc[1]
        gnorm[0, layer] += cross
        gnorm[1, layer] += sums
        size_all = CH // GROUPS * count * LANES * parts
        total, total_cross = group_totals(5 + layer, gain * sums, gain * cross)
        inverse = inv_kept[t, layer]
        coef[0] = gain * inverse
        coef[1] = -inverse * spread(total_cross / size_all)
        coef[2] = -inverse * spread(total / size_all)

        def z_bar(at, c):
            xhat = xh[xh_at, t, at, c, :].astype(F32)
            return zbuf[at, c, :] * coef[0, c] + xhat * coef[1, c] + coef[2, c]

        slot = 5 + layer
        for which, line in enumerate((0, count - 1)):
            edges[slot, which] = z_bar(line, slice(0, CH)).astype(BF)
        args = (
            slot,
            edges.at[slot, 0],
            edges.at[slot, 1],
            g_halo.at[layer, 0],
            g_halo.at[layer, 1],
        )
        halo_start(*args)

        def block(base, size):
            at = pl.ds(base + 1, size)
            for c in channel_blocks():
                z = z_bar(pl.ds(base, size), c)
                dst[at, slice(CH + c.start, CH + c.stop), :] = z.astype(BF)
                if by:
                    dst[at, c, :] = from_right(z, by).astype(BF)
                    right = slice(2 * CH + c.start, 2 * CH + c.stop)
                    dst[at, right, :] = from_left(z, by).astype(BF)

        for_blocks(count, 8, block)
        halo_wait(*args)
        if by:
            spread_halo(dst, (g_halo[layer, 0], g_halo[layer, 1]), count, by, BACKWARD)
        else:
            dst[0, CH : 2 * CH, :] = g_halo[layer, 0]
            dst[count + 1, CH : 2 * CH, :] = g_halo[layer, 1]

    def bar_rows(weight, g, size):
        y = nn_dot(weight, g)
        return [
            tap_rows(y, j + 2, 0) + tap_rows(y, j + 1, 1) + tap_rows(y, j, 2) for j in range(size)
        ]

    def products(t, layer, count, src, kept, out):
        def block(base, size):
            g = beside([src[base + j] for j in range(size + 2)])
            for j, bar in enumerate(bar_rows(wb[layer], g, size)):
                out[base + j] = bar
            h = beside([kept[t, pl.ds(base + j, 3)].reshape(3 * CH, LANES) for j in range(size)])
            gw[layer * 3 * CH : (layer + 1) * 3 * CH, :] += nt_dot(
                g[:, LANES : (size + 1) * LANES], h
            )

        for_blocks(count, 16, block)

    def products_last(t):
        def block(base, size):
            g = beside([sg[base + j] for j in range(size + 2)])
            inner = g[:, LANES : (size + 1) * LANES]
            low = base // 2
            for j, bar in enumerate(bar_rows(wb[4], g, size)):
                skip_bar[base + j] = bar
            ups = bar_rows(wb[3], g, size)
            for j in range(size // 2):
                half_bar[low + j] = pair_sum(ups[2 * j] + ups[2 * j + 1])
            h = beside([skip[t, pl.ds(base + j, 3)].reshape(3 * CH, LANES) for j in range(size)])
            gw[4 * 3 * CH : 5 * 3 * CH, :] += nt_dot(inner, h)
            up = beside(
                [
                    jnp.concatenate([h4[t, low + (j + ky - 1) // 2 + 1] for ky in range(3)], axis=0)
                    for j in range(size)
                ]
            )
            gw[3 * 3 * CH : 4 * 3 * CH, :] += nt_dot(inner, up)

        for_blocks(rows, 16, block)

    def products_first(t):
        def block(base, size):
            g = beside([sg[base + j, CH : 2 * CH, :] for j in range(size)])
            y = nn_dot(w0b[...], g)
            for j in range(size):
                taps[base + j] = y[:, j * LANES : (j + 1) * LANES]

        for_blocks(rows, 16, block)
        g = beside([sg[rows + j, CH : 2 * CH, :] for j in range(2)])
        y = nn_dot(w0b[...], g)
        for j in range(2):
            taps[rows + j] = y[:, j * LANES : (j + 1) * LANES]

        def weights(base, size):
            g = beside([sg[base + 1 + j, CH : 2 * CH, :] for j in range(size)])
            x = beside(
                [s0b[t, pl.ds(base + EDGE - 1 + j, 3)].reshape(48, LANES) for j in range(size)]
            )
            gw0[...] += nt_dot(g, x)

        for_blocks(rows, 16, weights)

    def backward_step(i, carry):
        t = STEPS - 1 - i
        facts = m_own[0]
        at = (t + 1).astype(F32)
        open_own = opened[own, :]
        for c in range(2):
            pull = jnp.zeros((rows, LANES), F32)
            for k in range(2):
                live = (facts[k : k + 1] == at).astype(F32)
                pull = pull + live * (u_kept[t, c] - t_own[k, c])
            w_ext[c, own, :] = open_own * (u_bar[c] + 2.0 * open_own * pull)
        ext_halo(12, w_ext)
        grid = grid_mask[...]
        gr, gc = project(w_ext[0], w_ext[1], grid)
        gr, gc = grid * gr, grid * gc
        qr, qc = q_ext[t, 0], q_ext[t, 1]
        bar_r = gr + DT_ADV * (
            drows(gr * qr) + dcols(gr * qc) - (gr * drows(qr) + gc * drows(qc))
        )
        bar_c = gc + DT_ADV * (
            drows(gc * qr) + dcols(gc * qc) - (gr * dcols(qr) + gc * dcols(qc))
        )
        for c, bar in enumerate((bar_r, bar_c)):
            passed = opened[...] * bar
            q_ext[t, c] = passed
            passed = q_ext[t, c, own, :]
            u_bar[c] = passed
            force_bar = DT_FORCE * passed
            misc[2 + c] += sublanes(force_bar)
            frows[:, c, :] = force_bar
        for c in range(2, 16):
            frows[:, c, :] = jnp.zeros((rows, LANES), F32)

        first_pass_last(t)
        second_pass(4, t, rows, xh_full, 2, sg, 1)
        products_last(t)
        first_pass(3, t, half, xh_half, 1, lambda b, s, c: half_bar[pl.ds(b, s), c, :])
        second_pass(3, t, half, xh_half, 1, sgh, 2)
        products(t, 2, half, sgh, h3, half_bar)
        first_pass(2, t, half, xh_half, 0, lambda b, s, c: half_bar[pl.ds(b, s), c, :])
        second_pass(2, t, half, xh_half, 0, sgh, 2)
        products(t, 1, half, sgh, pooled, half_bar)

        def skip_total(base, size, c):
            bars = skip_bar[pl.ds(base, size), c, :].reshape(size // 2, 2, 16, LANES)
            small = half_bar[pl.ds(base // 2, size // 2), c, :]
            return (bars + 0.25 * small[:, None]).reshape(size, 16, LANES)

        first_pass(1, t, rows, xh_full, 1, skip_total)
        second_pass(1, t, rows, xh_full, 1, sg, 1)
        products(t, 0, rows, sg, h1, skip_bar)
        first_pass(0, t, rows, xh_full, 0, lambda b, s, c: skip_bar[pl.ds(b, s), c, :])
        second_pass(0, t, rows, xh_full, 0, sg, 0)
        products_first(t)
        for c in range(2):
            columns = []
            for kx in range(3):
                total = jnp.zeros((rows, LANES), F32)
                for ky in range(3):
                    total = total + taps[pl.ds(2 - ky, rows), 16 * ky + 3 * kx + c, :]
                columns.append(total)
            u_bar[c] += from_right(columns[0], 1) + columns[1] + from_left(columns[2], 1)
        return carry

    lax.fori_loop(0, STEPS, backward_step, 0)

    mid_rows = (LAYERS + 1) * 3 * CH
    gw[3 * CH : 9 * CH, :] = 0.5 * gw[3 * CH : 9 * CH, :]
    lane = lane_of((CH, 3 * CH))
    rest = jnp.concatenate([gw0[...], jnp.zeros((CH, 3 * CH - 48), F32)], axis=1)
    for which in range(2):
        for layer in range(LAYERS + 1):
            column = jnp.sum(gnorm[which, layer], axis=1, keepdims=True)
            if layer in HALF_SLOT:
                column = 0.5 * column
            rest = jnp.where(lane == 48 + 5 * which + layer, column, rest)
    for c in range(2):
        rest = jnp.where(lane == 58 + c, ghead[:, c : c + 1], rest)
    gw[mid_rows : mid_rows + CH, :] = rest
    g_send[...] = gw[...].astype(BF)
    chunk = gw.shape[0] // members
    piece = chunk // planes

    def chunk_at(which):
        return pl.ds(pl.multiple_of(which * chunk, 16), chunk)

    def piece_at(which):
        return pl.ds(pl.multiple_of(which * piece, 16), piece)

    def part_at(which):
        return pl.ds(pl.multiple_of(mine * chunk + which * piece, 16), piece)

    m_plane[mine] = jnp.concatenate(
        [jnp.sum(misc[k], axis=0, keepdims=True) for k in range(4)] + [jnp.zeros((4, LANES), F32)],
        axis=0,
    )

    def plane_copies(d):
        other = lax.rem(mine + d, members)
        source = lax.rem(mine + members - d, members)
        sends = [
            (g_send.at[chunk_at(other)], p_recv.at[mine], p_ss.at[0, d], p_rs.at[0, mine]),
            (m_plane.at[mine], m_plane.at[mine], p_ss.at[1, d], p_rs.at[1, mine]),
        ]
        lands = [
            (p_recv.at[source], p_rs.at[0, source]),
            (m_plane.at[source], p_rs.at[1, source]),
        ]
        return plane_id(d), sends, lands

    def line_copies(d):
        other = lax.rem(level + d, planes)
        source = lax.rem(level + planes - d, planes)
        sends = [
            (z_send.at[piece_at(other)], z_recv.at[level], z_ss.at[0, d], z_rs.at[0, level]),
            (m_line.at[level], m_line.at[level], z_ss.at[1, d], z_rs.at[1, level]),
        ]
        lands = [
            (z_recv.at[source], z_rs.at[0, source]),
            (m_line.at[source], z_rs.at[1, source]),
        ]
        return line_id(d), sends, lands

    def line_gather(d):
        source = lax.rem(level + planes - d, planes)
        sends = [(g_all.at[part_at(level)], g_all.at[part_at(level)], z_ss.at[2, d], z_rs.at[2, level])]
        lands = [(g_all.at[part_at(source)], z_rs.at[2, source])]
        return line_id(d), sends, lands

    def plane_gather(d):
        source = lax.rem(mine + members - d, members)
        sends = [(g_all.at[chunk_at(mine)], g_all.at[chunk_at(mine)], p_ss.at[2, d], p_rs.at[2, mine])]
        lands = [(g_all.at[chunk_at(source)], p_rs.at[2, source])]
        return plane_id(d), sends, lands

    def exchange(copies, count):
        def start(d, carry):
            peer, sends, lands = copies(d)
            for src, dst, sent, landed in sends:
                pltpu.make_async_remote_copy(
                    src_ref=src,
                    dst_ref=dst,
                    send_sem=sent,
                    recv_sem=landed,
                    device_id=peer,
                    device_id_type=MESH,
                ).start()
            return carry

        def finish(d, carry):
            peer, sends, lands = copies(d)
            for src, dst, sent, landed in sends:
                pltpu.make_async_copy(src, src, sent).wait()
            for dst, landed in lands:
                pltpu.make_async_copy(dst, dst, landed).wait()
            return carry

        lax.fori_loop(1, count, start, 0)
        lax.fori_loop(1, count, finish, 0)

    exchange(plane_copies, members)
    own_chunk = chunk_at(mine)

    def add_chunk(d, carry):
        gw[own_chunk, :] += p_recv[lax.rem(mine + d, members)].astype(F32)
        return carry

    lax.fori_loop(1, members, add_chunk, 0)
    z_send[...] = gw[own_chunk, :].astype(BF)
    m_line[level] = lax.fori_loop(
        0, members, lambda k, total: total + m_plane[k], jnp.zeros((8, LANES), F32)
    )
    exchange(line_copies, planes)

    def add_piece(d, total):
        return total + z_recv[lax.rem(level + d, planes)].astype(F32)

    total = lax.fori_loop(1, planes, add_piece, gw[part_at(level), :])
    g_all[part_at(level), :] = total.astype(BF)
    exchange(line_gather, planes)
    exchange(plane_gather, members)

    totals = lax.fori_loop(
        0, planes, lambda k, total: total + m_line[k], jnp.zeros((8, LANES), F32)
    )
    totals = jnp.broadcast_to(jnp.sum(totals, axis=1, keepdims=True), (8, LANES))

    def squares(i, total):
        at = pl.ds(pl.multiple_of(i * 64, 64), 64)
        block = g_all[at, :].astype(F32)
        return total + jnp.sum((block * block).reshape(8, 8, 3 * CH), axis=0)

    square = lax.fori_loop(0, gw.shape[0] // 64, squares, jnp.zeros((8, 3 * CH), F32))
    square = jnp.sum(jnp.sum(square, axis=0, keepdims=True), axis=1, keepdims=True)
    count = totals[1:2]
    raw = square + totals[2:3] * totals[2:3] + totals[3:4] * totals[3:4]
    norm = jnp.sqrt(raw) / count
    factor = jnp.minimum(1.0, CLIP_NORM / norm) / count
    scalars[...] = jnp.concatenate([totals[:4], norm, factor, totals[6:]], axis=0)


def train(velocity, targets, meta, wf, wb, w0f, w0b, norms, headf, headb, bias):
    ranks = lax.axis_size("rows")
    planes = lax.axis_size("batch") // 2
    members = 2 * ranks
    unit = 16 * members * planes
    lines = -(-((LAYERS + 1) * 3 * CH + CH) // unit) * unit
    chunk = lines // members
    parts = ranks // 2
    tile = velocity.shape[2]
    rows, half, ext = 2 * tile, tile, 2 * tile + 2 * EDGE
    vmem = pl.BlockSpec(memory_space=pltpu.VMEM)

    def kept(count):
        return pltpu.VMEM((STEPS, count + 2, CH, LANES), BF)

    args = (velocity, targets, meta, wf, wb, w0f, w0b, norms, headf, headb, bias)
    return pl.pallas_call(
        functools.partial(train_kernel, ranks, planes),
        out_shape=(
            jax.ShapeDtypeStruct((lines, 3 * CH), BF),
            jax.ShapeDtypeStruct((8, LANES), F32),
        ),
        in_specs=[vmem] * len(args),
        out_specs=(vmem,) * 2,
        scratch_shapes=[
            pltpu.VMEM((lines, 3 * CH), F32),
            pltpu.VMEM((CH, 48), F32),
            pltpu.VMEM((2, LAYERS + 1, CH, LANES), F32),
            pltpu.VMEM((CH, 16), F32),
            pltpu.VMEM((4, 8, LANES), F32),
            pltpu.VMEM((2, ext, LANES), F32),
            pltpu.VMEM((2, 2, rows, LANES), F32),
            pltpu.VMEM((2, 16, LANES), F32),
            pltpu.VMEM((ext, LANES), F32),
            pltpu.VMEM((ext, LANES), F32),
            pltpu.VMEM((ext, 16, LANES), F32),
            pltpu.VMEM((STEPS, ext, 16, LANES), BF),
            pltpu.VMEM((STEPS, 2, ext, LANES), F32),
            pltpu.VMEM((STEPS, 2, rows, LANES), F32),
            pltpu.VMEM((2, ext, LANES), F32),
            pltpu.VMEM((2, rows, LANES), F32),
            pltpu.VMEM((rows, 16, LANES), F32),
            pltpu.VMEM((rows + 2, 48, LANES), F32),
            kept(rows),
            kept(rows),
            kept(half),
            kept(half),
            kept(half),
            pltpu.VMEM((3, STEPS, rows, CH, LANES), BF),
            pltpu.VMEM((2, STEPS, half, CH, LANES), BF),
            pltpu.VMEM((STEPS, LAYERS + 1, CH, LANES), F32),
            pltpu.VMEM((rows, CH, LANES), F32),
            pltpu.VMEM((rows, CH, LANES), F32),
            pltpu.VMEM((half, CH, LANES), F32),
            pltpu.VMEM((rows + 2, 3 * CH, LANES), BF),
            pltpu.VMEM((half + 2, 3 * CH, LANES), BF),
            pltpu.VMEM((10, 2, CH, LANES), BF),
            pltpu.VMEM((LAYERS + 1, 2, CH, LANES), BF),
            pltpu.VMEM((4, CH, LANES), F32),
            pltpu.VMEM((2, CH, LANES), F32),
            pltpu.VMEM((10, 16, LANES), F32),
            pltpu.VMEM((10, parts - 1, 16, LANES), F32),
            pltpu.VMEM((lines, 3 * CH), BF),
            pltpu.VMEM((members, chunk, 3 * CH), BF),
            pltpu.VMEM((chunk, 3 * CH), BF),
            pltpu.VMEM((planes, chunk // planes, 3 * CH), BF),
            pltpu.VMEM((members, 8, LANES), F32),
            pltpu.VMEM((planes, 8, LANES), F32),
            pltpu.SemaphoreType.DMA((2, 3)),
            pltpu.SemaphoreType.DMA((2, 3)),
            pltpu.SemaphoreType.DMA((3,)),
            pltpu.SemaphoreType.DMA((13, 2)),
            pltpu.SemaphoreType.DMA((13, 2)),
            pltpu.SemaphoreType.DMA((10, parts - 1)),
            pltpu.SemaphoreType.DMA((10, parts - 1)),
            pltpu.SemaphoreType.DMA((3, members)),
            pltpu.SemaphoreType.DMA((3, members)),
            pltpu.SemaphoreType.DMA((3, planes)),
            pltpu.SemaphoreType.DMA((3, planes)),
        ],
        compiler_params=pltpu.CompilerParams(
            collective_id=0, has_side_effects=True, vmem_limit_bytes=60 * 2**20
        ),
        name="train",
    )(*args)


def shards(
    velocity,
    targets,
    keyframes,
    boxes,
    w_in,
    w_mid,
    norm_params,
    head_params,
    m_in,
    m_mid,
    m_norm,
    m_head,
    v_in,
    v_mid,
    v_norm,
    v_head,
):
    samples = velocity.shape[0]
    facts = jnp.concatenate(
        [keyframes, boxes.reshape(samples, 8), jnp.zeros((samples, 6), jnp.int32)], axis=1
    ).astype(F32)
    meta = jnp.broadcast_to(facts[:, :, None], (samples, 16, LANES))
    mid = w_mid.reshape(LAYERS + 1, 3, 3, CH, CH)
    wf = jnp.transpose(mid, (0, 1, 3, 2, 4)).reshape(LAYERS + 1, 3 * CH, 3 * CH).astype(BF)
    wb = jnp.transpose(mid, (0, 1, 4, 2, 3)).reshape(LAYERS + 1, 3 * CH, 3 * CH).astype(BF)
    first = jnp.transpose(w_in, (0, 2, 3, 1)).reshape(CH, 3, 9)
    w0f = jnp.pad(first, ((0, 0), (0, 0), (0, 7))).reshape(CH, 48).astype(BF)
    norms = jnp.broadcast_to(norm_params[..., None], norm_params.shape + (LANES,))
    headf = jnp.pad(head_params[:, :CH], ((0, 14), (0, 0))).astype(BF)
    bias = jnp.broadcast_to(head_params[:, CH:, None], (2, 1, LANES))
    g_all, scalars = train(
        velocity, targets, meta, wf, wb, w0f, w0f.T, norms, headf, headf.T, bias
    )
    loss_sum, count, norm, factor = scalars[0, 0], scalars[1, 0], scalars[4, 0], scalars[5, 0]
    mid_rows = (LAYERS + 1) * 3 * CH
    g_mid = jnp.transpose(
        g_all[:mid_rows].reshape(LAYERS + 1, 3, CH, 3, CH), (0, 3, 1, 2, 4)
    ).reshape(w_mid.shape)
    rest = g_all[mid_rows : mid_rows + CH].astype(F32)
    g_in = rest[:, :48].reshape(CH, 3, 16)[:, :, :9].reshape(CH, 3, 3, 3)
    g_in = jnp.transpose(g_in, (0, 3, 1, 2))
    g_norm = rest[:, 48:58].T.reshape(norm_params.shape)
    g_head = jnp.concatenate([rest[:, 58:60].T, scalars[2:4, :1]], axis=1)
    grads = (g_in, g_mid, g_norm, g_head)
    params = (w_in, w_mid, norm_params, head_params)
    new_w, new_m, new_v = ([], [], [])
    for weight, moment, second, g, rate in zip(
        params, (m_in, m_mid, m_norm, m_head), (v_in, v_mid, v_norm, v_head), grads, RATES
    ):
        g = g.astype(F32) * factor
        moment_new = BETA_ONE * moment + (1 - BETA_ONE) * g
        second_new = BETA_TWO * second + (1 - BETA_TWO) * g * g
        mhat = moment_new / (1 - BETA_ONE**STEP_NUM)
        vhat = second_new / (1 - BETA_TWO**STEP_NUM)
        new_w.append(weight - rate * (mhat / (jnp.sqrt(vhat) + ADAM_EPS) + DECAY * weight))
        new_m.append(moment_new)
        new_v.append(second_new)
    return (
        *new_w,
        *new_m,
        *new_v,
        new_w[0].astype(BF),
        new_w[1].astype(BF),
        new_w[3].astype(BF),
        loss_sum,
        count,
        norm,
    )


def solution(mesh):
    return jax.shard_map(
        shards,
        mesh=mesh,
        in_specs=(
            P("batch", None, "rows", None),
            P("batch", None, None, "rows", None),
            P("batch", None),
            P("batch", None, None),
        )
        + (P(),) * 12,
        out_specs=(P(),) * 18,
        check_vma=False,
    )
```

```python
import functools

import jax
import jax.numpy as jnp
from jax import lax
from jax.experimental import pallas as pl
from jax.experimental.pallas import tpu as pltpu
from jax.sharding import PartitionSpec as P

CH = 64
GROUPS = 8
LAYERS = 4
STEPS = 4
JACOBI = 4
STEP_NUM = 10
LANES = 128
EDGE = 8

EPS_NORM = 1e-05
DT_FORCE = 0.5
DT_ADV = 0.2
CLIP_NORM = 0.001
BETA_ONE = 0.9
BETA_TWO = 0.95
ADAM_EPS = 1e-08
DECAY = 0.01
RATES = (0.2, 0.05, 1.0, 0.15)

BF = jnp.bfloat16
F32 = jnp.float32
MESH = pl.DeviceIdType.MESH
FULL_SLOT = {0: 0, 1: 1, 4: 2}
HALF_SLOT = {2: 0, 3: 1}
ACT_LINES = 32
CONV_LINES = 32
BAR_LINES = 16
SUM_LINES = 32


def nt_dot(a, b):
    return lax.dot_general(a, b, (((1,), (1,)), ((), ())), preferred_element_type=F32)


def nn_dot(a, b):
    return jnp.dot(a, b, preferred_element_type=F32)


def beside(rows):
    return jnp.concatenate(rows, axis=1)


def lane_of(shape):
    return lax.broadcasted_iota(jnp.int32, shape, len(shape) - 1)


def from_left(x, by):
    return jnp.where(lane_of(x.shape) < by, jnp.zeros((), x.dtype), pltpu.roll(x, by, x.ndim - 1))


def from_right(x, by):
    moved = pltpu.roll(x, LANES - by, x.ndim - 1)
    return jnp.where(lane_of(x.shape) >= LANES - by, jnp.zeros((), x.dtype), moved)


def pair_sum(x):
    even = lane_of(x.shape) % 2 == 0
    last = x.ndim - 1
    return x + jnp.where(even, pltpu.roll(x, LANES - 1, last), pltpu.roll(x, 1, last))


def drows(x):
    count = x.shape[0]
    return 0.5 * (pltpu.roll(x, count - 1, 0) - pltpu.roll(x, 1, 0))


def dcols(x):
    return 0.5 * (from_right(x, 1) - from_left(x, 1))


def nsum(x):
    count = x.shape[0]
    return (
        pltpu.roll(x, count - 1, 0) + pltpu.roll(x, 1, 0) + from_right(x, 1) + from_left(x, 1)
    )


def project(vr, vc, grid):
    div = grid * (drows(vr) + dcols(vc))
    press = -0.25 * div
    for sweep in range(JACOBI - 1):
        press = grid * (0.25 * (nsum(press) - div))
    return vr - drows(press), vc - dcols(press)


def sublanes(x):
    return jnp.sum(x.reshape(x.shape[0] // 8, 8, LANES), axis=0)


def group_rows(x):
    return jnp.sum(x.reshape(GROUPS, CH // GROUPS, LANES), axis=1)


def spread(x):
    return jnp.concatenate(
        [jnp.broadcast_to(x[g : g + 1], (CH // GROUPS, LANES)) for g in range(GROUPS)], axis=0
    )


def train_kernel(
    ranks,
    planes,
    keys,
    boxes,
    vel,
    tgt,
    w_in,
    w_mid,
    norm_params,
    head,
    g_all,
    scalars,
    meta,
    wf,
    wb,
    w0f,
    w0b,
    norms,
    headf,
    headb,
    bias,
    lines,
    wide,
    small,
    gw,
    gw0,
    gnorm,
    ghead,
    misc,
    u_ext,
    t_own,
    m_own,
    opened,
    grid_mask,
    s0,
    s0b,
    q_ext,
    u_kept,
    w_ext,
    u_bar,
    frows,
    taps,
    h1,
    skip,
    pooled,
    h3,
    h4,
    xh_full,
    xh_half,
    inv_kept,
    zbuf,
    skip_bar,
    sg,
    sgh,
    edges,
    g_halo,
    pool_mat,
    coef,
    acc,
    st_send,
    st_recv,
    g_send,
    p_recv,
    z_send,
    z_recv,
    m_plane,
    m_line,
    in_send,
    in_recv,
    in_local,
    halo_send,
    halo_recv,
    st_ss,
    st_rs,
    p_ss,
    p_rs,
    z_ss,
    z_rs,
):
    quarter = ranks // 4
    parts = ranks // 2
    tile = vel.shape[2]
    rows = 2 * tile
    half = rows // 2
    batch_at = lax.axis_index("batch")
    row_at = lax.axis_index("rows")
    core = lax.rem(batch_at, 2)
    plane = batch_at - core
    sample = row_at // quarter
    part = 2 * lax.rem(row_at, quarter) + core

    def owner(which, piece):
        return (plane + lax.rem(piece, 2), which * quarter + piece // 2)

    u_ext[...] = jnp.zeros_like(u_ext)
    q_ext[...] = jnp.zeros_like(q_ext)
    w_ext[...] = jnp.zeros_like(w_ext)
    g_halo[...] = jnp.zeros_like(g_halo)
    for kept, count in ((h1, rows), (skip, rows), (pooled, half), (h3, half), (h4, half)):
        for t in range(STEPS):
            kept[t, 0] = jnp.zeros((CH, LANES), BF)
            kept[t, count + 1] = jnp.zeros((CH, LANES), BF)

    barrier = pltpu.get_barrier_semaphore()
    members = 2 * ranks
    mine = core * ranks + row_at

    def plane_id(d):
        other = lax.rem(mine + d, members)
        return (plane + other // ranks, lax.rem(other, ranks))

    def greet(d, carry):
        pl.semaphore_signal(barrier, inc=1, device_id=plane_id(d), device_id_type=MESH)
        return carry

    lax.fori_loop(1, members, greet, 0)
    level = batch_at // 2

    def line_id(d):
        return (2 * lax.rem(level + d, planes) + core, row_at)

    def greet_line(d, carry):
        pl.semaphore_signal(barrier, inc=1, device_id=line_id(d), device_id_type=MESH)
        return carry

    lax.fori_loop(1, planes, greet_line, 0)

    line_is = lax.broadcasted_iota(jnp.int32, (16, LANES), 0)
    for j in range(2):
        values = [keys[j, k] for k in range(2)]
        values += [boxes[j, b, k] for b in range(2) for k in range(4)]
        facts = jnp.zeros((16, LANES), F32)
        for k, value in enumerate(values):
            facts = jnp.where(line_is == k, value.astype(F32), facts)
        meta[j] = facts

    pl.semaphore_wait(barrier, members + planes - 2)

    def incoming(place):
        at = pl.ds(pl.multiple_of(EDGE + place * tile, 8), tile)
        here = pl.ds(pl.multiple_of(place * tile, 8), tile)
        return u_ext.at[:, at, :], t_own.at[:, :, here, :], m_own.at[place]

    place = lax.rem(row_at, 2)
    for j in range(2):
        to_batch, to_row = owner(2 * core + j, row_at // 2)
        stays = (to_batch == batch_at) & (to_row == row_at)
        for k, (src, dst) in enumerate(zip((vel.at[j], tgt.at[j], meta.at[j]), incoming(place))):

            @pl.when(stays)
            def _():
                pltpu.make_async_copy(src, dst, in_local.at[k]).start()

            @pl.when(jnp.logical_not(stays))
            def _():
                pltpu.make_async_remote_copy(
                    src_ref=src,
                    dst_ref=dst,
                    send_sem=in_send.at[j, k],
                    recv_sem=in_recv.at[place, k],
                    device_id=(to_batch, to_row),
                    device_id_type=MESH,
                ).start()

    low_lanes = lane_of((CH // 2, LANES)) < CH
    for ky in range(3):
        for kx in range(3):
            for a in range(CH // 2):
                lines[kx, a, : LAYERS + 1, :] = w_mid[3 * ky + kx, :, a * LANES : (a + 1) * LANES]
        for k in range(LAYERS + 1):
            left, mid, right = (lines[kx, :, k, :] for kx in range(3))
            slab = 3 * k + ky
            even, odd = pl.ds(0, CH // 2, 2), pl.ds(1, CH // 2, 2)
            wide[0, slab, even, :] = jnp.where(low_lanes, left, pltpu.roll(mid, CH, 1))
            wide[0, slab, odd, :] = jnp.where(low_lanes, pltpu.roll(left, CH, 1), mid)
            wide[1, slab, even, :] = right
            wide[1, slab, odd, :] = pltpu.roll(right, CH, 1)
    low_lanes = lane_of((CH, LANES)) < CH
    for k in range(LAYERS + 1):
        for ky in range(3):
            slab = 3 * k + ky
            at = slice(ky * CH, (ky + 1) * CH)
            first, last = wide[0, slab], wide[1, slab]
            wf[k, at, :] = jnp.concatenate([first, last[:, :CH]], axis=1).astype(BF)
            turned = jnp.concatenate([first, last], axis=0).T
            left, mid = turned[:CH], turned[CH:]
            first = jnp.where(low_lanes, left, pltpu.roll(mid, CH, 1))
            last = pltpu.roll(left, CH, 1)
            wb[k, at, :] = jnp.concatenate([first, last[:, :CH]], axis=1).astype(BF)
    small[...] = jnp.zeros_like(small)
    for ch in range(3):
        for ky in range(3):
            taps_in = w_in[ch, ky]
            taps_in = jnp.concatenate([taps_in, jnp.zeros_like(taps_in)], axis=1)
            small[pl.ds(16 * ky + ch, 3, 3), :] = taps_in
    for layer in range(LAYERS + 1):
        pair = norm_params[layer]
        small[48 + 2 * layer : 50 + 2 * layer, :] = jnp.concatenate(
            [pair, jnp.zeros_like(pair)], axis=1
        )
    pair = head[:, :CH]
    small[64:66, :] = jnp.concatenate([pair, jnp.zeros_like(pair)], axis=1)
    w0b[...] = small[:48, :CH].astype(BF)
    headf[...] = small[64:80, :CH].astype(BF)
    turned = small[...].T[:CH]
    w0f[...] = turned[:, :48].astype(BF)
    headb[...] = turned[:, 64:80].astype(BF)
    for which in range(2):
        for layer in range(LAYERS + 1):
            at = 48 + 2 * layer + which
            norms[which, layer] = jnp.broadcast_to(turned[:, at : at + 1], (CH, LANES))
        bias[which] = jnp.broadcast_to(head[which : which + 1, CH : CH + 1], (1, LANES))

    for j in range(2):
        to_batch, to_row = owner(2 * core + j, row_at // 2)
        stays = (to_batch == batch_at) & (to_row == row_at)
        for k, src in enumerate((vel.at[j], tgt.at[j], meta.at[j])):

            @pl.when(stays)
            def _():
                pltpu.make_async_copy(src, src, in_local.at[k]).wait()

            @pl.when(jnp.logical_not(stays))
            def _():
                pltpu.make_async_copy(src, src, in_send.at[j, k]).wait()

    for i in range(2):
        from_batch = plane + sample // 2
        from_row = 2 * part + i
        stays = (from_batch == batch_at) & (from_row == row_at)
        for k, dst in enumerate(incoming(i)):

            @pl.when(jnp.logical_not(stays))
            def _():
                pltpu.make_async_copy(dst, dst, in_recv.at[i, k]).wait()

    has_prev = part > 0
    has_next = part < parts - 1
    prev_id = owner(sample, jnp.maximum(part - 1, 0))
    next_id = owner(sample, jnp.minimum(part + 1, parts - 1))

    def halo_copies(slot, low_src, high_src, top_dst, bottom_dst):
        to_prev = pltpu.make_async_remote_copy(
            src_ref=low_src,
            dst_ref=bottom_dst,
            send_sem=halo_send.at[slot, 0],
            recv_sem=halo_recv.at[slot, 0],
            device_id=prev_id,
            device_id_type=MESH,
        )
        to_next = pltpu.make_async_remote_copy(
            src_ref=high_src,
            dst_ref=top_dst,
            send_sem=halo_send.at[slot, 1],
            recv_sem=halo_recv.at[slot, 1],
            device_id=next_id,
            device_id_type=MESH,
        )
        return to_prev, to_next

    def halo_start(*args):
        to_prev, to_next = halo_copies(*args)

        @pl.when(has_prev)
        def _():
            to_prev.start()

        @pl.when(has_next)
        def _():
            to_next.start()

    def halo_wait(*args):
        to_prev, to_next = halo_copies(*args)

        @pl.when(has_prev)
        def _():
            to_prev.wait_send()
            to_next.wait_recv()

        @pl.when(has_next)
        def _():
            to_next.wait_send()
            to_prev.wait_recv()

    def ext_halo(slot, ref):
        args = (
            slot,
            ref.at[:, pl.ds(EDGE, EDGE), :],
            ref.at[:, pl.ds(rows, EDGE), :],
            ref.at[:, pl.ds(0, EDGE), :],
            ref.at[:, pl.ds(rows + EDGE, EDGE), :],
        )
        halo_start(*args)
        halo_wait(*args)

    def group_copies(slot):
        return [
            pltpu.make_async_remote_copy(
                src_ref=st_send.at[slot],
                dst_ref=st_recv.at[slot, d - 1],
                send_sem=st_ss.at[slot, d - 1],
                recv_sem=st_rs.at[slot, d - 1],
                device_id=owner(sample, lax.rem(part + d, parts)),
                device_id_type=MESH,
            )
            for d in range(1, parts)
        ]

    def group_start(slot, first, second):
        st_send[slot] = jnp.concatenate([group_rows(first), group_rows(second)], axis=0)
        for copy in group_copies(slot):
            copy.start()

    def group_finish(slot):
        total = st_send[slot]
        for d, copy in enumerate(group_copies(slot)):
            copy.wait()
            total = total + st_recv[slot, d]
        total = jnp.broadcast_to(jnp.sum(total, axis=1, keepdims=True), total.shape)
        return total[:GROUPS], total[GROUPS:]

    ext = rows + 2 * EDGE
    row_is = lax.broadcasted_iota(jnp.int32, (ext, LANES), 0) - EDGE + part * rows
    inside_grid = ((row_is >= 0) & (row_is < parts * rows)).astype(F32)
    row_f = row_is.astype(F32)
    col_f = lane_of((ext, LANES)).astype(F32)
    covered = jnp.zeros((ext, LANES), F32)
    facts = m_own[0]
    for b in range(2):
        bounds = [facts[2 + 4 * b + k : 3 + 4 * b + k] for k in range(4)]
        inside = (
            (row_f >= bounds[0])
            & (row_f < bounds[1])
            & (col_f >= bounds[2])
            & (col_f < bounds[3])
        )
        covered = jnp.maximum(covered, inside.astype(F32))
    grid_mask[...] = inside_grid
    opened[...] = inside_grid * (1.0 - covered)
    own = pl.ds(EDGE, rows)
    misc[...] = jnp.zeros_like(misc)
    live_slots = (facts[0:1] > 0.5).astype(F32) + (facts[1:2] > 0.5).astype(F32)
    misc[1] = sublanes(opened[own, :] * live_slots)
    gw[...] = jnp.zeros_like(gw)
    gw0[...] = jnp.zeros_like(gw0)
    gnorm[...] = jnp.zeros_like(gnorm)
    ghead[...] = jnp.zeros_like(ghead)
    s0[...] = jnp.zeros_like(s0)
    frows[...] = jnp.zeros_like(frows)
    u_bar[...] = jnp.zeros_like(u_bar)

    ext_halo(10, u_ext)

    source = lax.broadcasted_iota(jnp.int32, pool_mat.shape, 0) % LANES
    target = lane_of(pool_mat.shape)
    column = target % LANES + 2 * (target // LANES - 1)
    pool_mat[...] = jnp.where(source // 2 == (column + 2) // 2 - 1, 0.25, 0.0).astype(BF)

    for kx in range(3):
        field = opened[...]
        s0[:, 3 * kx + 2, :] = (from_left(field, 1), field, from_right(field, 1))[kx]

    def put_shifted(dst, at, c, x, by, order):
        copies = (from_left(x, by), x, from_right(x, by))
        for place_at, which in enumerate(order):
            dst[at, slice(place_at * CH + c.start, place_at * CH + c.stop), :] = copies[which]

    FORWARD = (0, 1, 2)
    BACKWARD = (2, 1, 0)

    def spread_halo(dst, lines, count, by, order):
        for at, line in ((0, lines[0]), (count + 1, lines[1])):
            put_shifted(dst, at, slice(0, CH), line, by, order)

    def for_blocks(count, size, body):
        size = min(size, count)

        def step(i, carry):
            body(pl.multiple_of(i * size, size), size)
            return carry

        lax.fori_loop(0, count // size, step, 0)

    def channel_blocks():
        return [slice(16 * c, 16 * c + 16) for c in range(CH // 16)]

    def make_norm(layer, t, sums, squares, count):
        group_start(layer, sums, squares)
        sums, squares = group_finish(layer)
        size = CH // GROUPS * count * LANES * parts
        mean = sums / size
        inverse = lax.rsqrt(squares / size - mean * mean + EPS_NORM)
        scale = spread(inverse)
        inv_kept[t, layer] = scale
        scale = 0.5 * scale * norms[0, layer]
        coef[0] = scale
        coef[1] = 0.5 * norms[1, layer] - spread(mean) * scale

    def activate(z, c):
        n = z * coef[0, c] + coef[1, c]
        return n, n * jnp.tanh(n) + n

    def conv_sums(count, size, rows_of):
        size = min(size, count)
        zero = jnp.zeros((CH, LANES), F32)

        def step(i, carry):
            sums, squares = carry
            base = pl.multiple_of(i * size, size)
            for j, z in enumerate(rows_of(base, size)):
                zbuf[base + j] = z
                sums = sums + z
                squares = squares + z * z
            return sums, squares

        return lax.fori_loop(0, count // size, step, (zero, zero))

    def tap_rows(y, j, at):
        return y[at * CH : (at + 1) * CH, j * LANES : (j + 1) * LANES]

    def conv_of(src, layer):
        def rows_of(base, size):
            y = nn_dot(wf[layer], beside([src[base + j] for j in range(size + 2)]))
            return [
                tap_rows(y, j, 0) + tap_rows(y, j + 1, 1) + tap_rows(y, j + 2, 2)
                for j in range(size)
            ]

        return rows_of

    def conv_last(base, size):
        y = nn_dot(wf[4], beside([sg[base + j] for j in range(size + 2)]))
        low = base // 2
        x = nn_dot(wf[3], beside([sgh[low + j] for j in range(size // 2 + 2)]))
        result = []
        for j in range(size):
            z = tap_rows(y, j, 0) + tap_rows(y, j + 1, 1) + tap_rows(y, j + 2, 2)
            for ky in range(3):
                z = z + tap_rows(x, (j + ky - 1) // 2 + 1, ky)
            result.append(z)
        return result

    def finish_plain(t, layer, count, kept, xh, xh_at, dst, by, slot):
        for which, line in enumerate((0, count - 1)):
            edges[slot, which] = activate(zbuf[line], slice(0, CH))[1].astype(BF)
        args = (slot, edges.at[slot, 0], edges.at[slot, 1], kept.at[t, 0], kept.at[t, count + 1])
        halo_start(*args)

        def block(base, size):
            at = pl.ds(base + 1, size)
            for c in channel_blocks():
                n, h = activate(zbuf[pl.ds(base, size), c, :], c)
                xh[xh_at, t, pl.ds(base, size), c, :] = n.astype(BF)
                low = h.astype(BF)
                kept[t, at, c, :] = low
                put_shifted(dst, at, c, low, by, FORWARD)

        for_blocks(count, ACT_LINES, block)
        halo_wait(*args)
        spread_halo(dst, (kept[t, 0], kept[t, count + 1]), count, by, FORWARD)

    def pool_pairs(low, size):
        pairs = jnp.concatenate(
            [beside([low[2 * j], low[2 * j + 1]]) for j in range(size // 2)], axis=0
        )
        return nn_dot(pairs, pool_mat[...]).astype(BF).reshape(size // 2, CH, 3 * LANES)

    def finish_skip(t):
        for which, line in enumerate((0, rows - 2)):
            low = activate(zbuf[pl.ds(line, 2)], slice(0, CH))[1].astype(BF)
            edges[1, which] = low[which]
            edges[2, which] = pool_pairs(low, 2)[0, :, LANES : 2 * LANES]
        skip_args = (1, edges.at[1, 0], edges.at[1, 1], skip.at[t, 0], skip.at[t, rows + 1])
        pool_args = (2, edges.at[2, 0], edges.at[2, 1], pooled.at[t, 0], pooled.at[t, half + 1])
        halo_start(*pool_args)
        halo_start(*skip_args)

        def block(base, size):
            at = pl.ds(base + 1, size)
            lows = []
            for c in channel_blocks():
                n, h = activate(zbuf[pl.ds(base, size), c, :], c)
                xh_full[1, t, pl.ds(base, size), c, :] = n.astype(BF)
                low = h.astype(BF)
                skip[t, at, c, :] = low
                put_shifted(sg, at, c, low, 1, FORWARD)
                lows.append(low)
            small = pool_pairs(jnp.concatenate(lows, axis=1), size)
            at = pl.ds(base // 2 + 1, size // 2)
            pooled[t, at] = small[:, :, LANES : 2 * LANES]
            for k in range(3):
                sgh[at, k * CH : (k + 1) * CH, :] = small[:, :, k * LANES : (k + 1) * LANES]

        for_blocks(rows, ACT_LINES, block)
        halo_wait(*pool_args)
        halo_wait(*skip_args)
        spread_halo(sgh, (pooled[t, 0], pooled[t, half + 1]), half, 2, FORWARD)
        spread_halo(sg, (skip[t, 0], skip[t, rows + 1]), rows, 1, FORWARD)

    def finish_last(t):
        def block(base, size):
            lows = []
            for c in channel_blocks():
                n, h = activate(zbuf[pl.ds(base, size), c, :], c)
                xh_full[2, t, pl.ds(base, size), c, :] = n.astype(BF)
                lows.append(h.astype(BF))
            low = jnp.concatenate(lows, axis=1)
            force = nn_dot(headf[...], beside([low[j] for j in range(size)]))
            for j in range(size):
                frows[base + j] = force[:, j * LANES : (j + 1) * LANES]

        for_blocks(rows, ACT_LINES, block)

    def forward_step(t, carry):
        for c in range(2):
            field = u_ext[c]
            for kx, moved in enumerate((from_left(field, 1), field, from_right(field, 1))):
                s0[:, 3 * kx + c, :] = moved
        s0b[t] = s0[...].astype(BF)

        def first_rows(base, size):
            x = beside(
                [s0b[t, pl.ds(base + EDGE - 1 + j, 3)].reshape(48, LANES) for j in range(size)]
            )
            z = nn_dot(w0f[...], x)
            return [z[:, j * LANES : (j + 1) * LANES] for j in range(size)]

        make_norm(0, t, *conv_sums(rows, CONV_LINES, first_rows), rows)
        finish_plain(t, 0, rows, h1, xh_full, 0, sg, 1, 0)
        make_norm(1, t, *conv_sums(rows, CONV_LINES, conv_of(sg, 0)), rows)
        finish_skip(t)
        make_norm(2, t, *conv_sums(half, CONV_LINES, conv_of(sgh, 1)), half)
        finish_plain(t, 2, half, h3, xh_half, 0, sgh, 2, 3)
        make_norm(3, t, *conv_sums(half, CONV_LINES, conv_of(sgh, 2)), half)
        finish_plain(t, 3, half, h4, xh_half, 1, sgh, 1, 4)
        make_norm(4, t, *conv_sums(rows, CONV_LINES, conv_last), rows)
        finish_last(t)

        for c in range(2):
            force = frows[:, c, :] + bias[c]
            q_ext[t, c, own, :] = (u_ext[c, own, :] + DT_FORCE * force) * opened[own, :]
        ext_halo(11, q_ext.at[t])
        qr, qc = q_ext[t, 0], q_ext[t, 1]
        grid = grid_mask[...]
        vr = grid * (qr - DT_ADV * (qr * drows(qr) + qc * dcols(qr)))
        vc = grid * (qc - DT_ADV * (qr * drows(qc) + qc * dcols(qc)))
        facts = m_own[0]
        at = (t + 1).astype(F32)
        for c, moved in enumerate(project(vr, vc, grid)):
            u_ext[c] = opened[...] * moved
            u_now = u_ext[c, own, :]
            u_kept[t, c] = u_now
            for k in range(2):
                live = (facts[k : k + 1] == at).astype(F32)
                miss = u_now - t_own[k, c]
                misc[0] += sublanes(live * opened[own, :] * miss * miss)
        return carry

    lax.fori_loop(0, STEPS, forward_step, 0)

    def bar_block(xh, xh_at, t, base, size, c, h_bar):
        n = xh[xh_at, t, pl.ds(base, size), c, :].astype(F32)
        bend = jnp.tanh(n)
        moved = n * bend
        n_bar = h_bar * ((1.0 + bend) * ((1.0 + n) - moved))
        zbuf[pl.ds(base, size), c, :] = n_bar
        acc[0, c, :] += jnp.sum(n_bar, axis=0)
        acc[1, c, :] += jnp.sum(n_bar * n, axis=0)
        return n + moved

    def clear_sums():
        acc[...] = jnp.zeros_like(acc)

    def first_pass_last(t):
        clear_sums()

        def block(base, size):
            low = beside([frows[base + j].astype(BF) for j in range(size)])
            h_bar = nn_dot(headb[...], low)
            bars = jnp.stack([h_bar[:, j * LANES : (j + 1) * LANES] for j in range(size)], axis=0)
            lows = [
                bar_block(xh_full, 2, t, base, size, c, bars[:, c, :]).astype(BF)
                for c in channel_blocks()
            ]
            h = jnp.concatenate(lows, axis=1)
            ghead[...] += nt_dot(beside([h[j] for j in range(size)]), low)

        for_blocks(rows, BAR_LINES, block)

    def sums_start(layer):
        gain = norms[0, layer]
        sums = 0.5 * acc[0]
        cross = (acc[1] - norms[1, layer] * sums) / gain
        group_start(5 + layer, gain * sums, gain * cross)
        gnorm[0, layer] += cross
        gnorm[1, layer] += sums

    def second_pass(layer, t, count, xh, xh_at, dst, by):
        size_all = CH // GROUPS * count * LANES * parts
        total, total_cross = group_finish(5 + layer)
        inverse = inv_kept[t, layer]
        gain = norms[0, layer]
        slope = inverse * spread(total_cross / size_all) / gain
        coef[0] = 0.5 * gain * inverse
        coef[1] = -2.0 * slope
        coef[2] = norms[1, layer] * slope - inverse * spread(total / size_all)

        def z_bar(at, c):
            n = xh[xh_at, t, at, c, :].astype(F32)
            return (zbuf[at, c, :] * coef[0, c] + n * coef[1, c] + coef[2, c]).astype(BF)

        slot = 5 + layer
        for which, line in enumerate((0, count - 1)):
            edges[slot, which] = z_bar(line, slice(0, CH))
        args = (
            slot,
            edges.at[slot, 0],
            edges.at[slot, 1],
            g_halo.at[layer, 0],
            g_halo.at[layer, 1],
        )
        halo_start(*args)

        def block(base, size):
            at = pl.ds(base + 1, size)
            for c in channel_blocks():
                z = z_bar(pl.ds(base, size), c)
                if by:
                    put_shifted(dst, at, c, z, by, BACKWARD)
                else:
                    dst[at, slice(CH + c.start, CH + c.stop), :] = z

        for_blocks(count, ACT_LINES, block)
        halo_wait(*args)
        if by:
            spread_halo(dst, (g_halo[layer, 0], g_halo[layer, 1]), count, by, BACKWARD)
        else:
            dst[0, CH : 2 * CH, :] = g_halo[layer, 0]
            dst[count + 1, CH : 2 * CH, :] = g_halo[layer, 1]

    def bar_rows(weight, g, size):
        y = nn_dot(weight, g)
        return [
            tap_rows(y, j + 2, 0) + tap_rows(y, j + 1, 1) + tap_rows(y, j, 2) for j in range(size)
        ]

    def bars_of(layer, count, src, then):
        clear_sums()

        def block(base, size):
            g = beside([src[base + j] for j in range(size + 2)])
            then(base, size, jnp.stack(bar_rows(wb[layer], g, size), axis=0))

        for_blocks(count, BAR_LINES, block)

    def weight_sums(at, t, count, src, kept):
        def block(base, size):
            g = beside([src[base + 1 + j] for j in range(size)])
            h = beside([kept[t, pl.ds(base + j, 3)].reshape(3 * CH, LANES) for j in range(size)])
            gw[at * 3 * CH : (at + 1) * 3 * CH, :] += nt_dot(g, h)

        for_blocks(count, SUM_LINES, block)

    def bars_last(t):
        clear_sums()

        def block(base, size):
            g = beside([sg[base + j] for j in range(size + 2)])
            for j, bar in enumerate(bar_rows(wb[4], g, size)):
                skip_bar[base + j] = bar
            ups = bar_rows(wb[3], g, size)
            low = base // 2
            bars = jnp.stack(
                [pair_sum(ups[2 * j] + ups[2 * j + 1]) for j in range(size // 2)], axis=0
            )
            for c in channel_blocks():
                bar_block(xh_half, 1, t, low, size // 2, c, bars[:, c, :])

        for_blocks(rows, BAR_LINES, block)

    def weight_sums_last(t):
        def block(base, size):
            g = beside([sg[base + 1 + j] for j in range(size)])
            low = base // 2
            h = beside([skip[t, pl.ds(base + j, 3)].reshape(3 * CH, LANES) for j in range(size)])
            gw[4 * 3 * CH : 5 * 3 * CH, :] += nt_dot(g, h)
            up = beside(
                [
                    jnp.concatenate([h4[t, low + (j + ky - 1) // 2 + 1] for ky in range(3)], axis=0)
                    for j in range(size)
                ]
            )
            gw[3 * 3 * CH : 4 * 3 * CH, :] += nt_dot(g, up)

        for_blocks(rows, SUM_LINES, block)

    def taps_first():
        def block(base, size):
            g = beside([sg[base + j, CH : 2 * CH, :] for j in range(size)])
            y = nn_dot(w0b[...], g)
            for j in range(size):
                taps[base + j] = y[:, j * LANES : (j + 1) * LANES]

        for_blocks(rows, SUM_LINES, block)
        g = beside([sg[rows + j, CH : 2 * CH, :] for j in range(2)])
        y = nn_dot(w0b[...], g)
        for j in range(2):
            taps[rows + j] = y[:, j * LANES : (j + 1) * LANES]

    def weight_sums_first(t):
        def weights(base, size):
            g = beside([sg[base + 1 + j, CH : 2 * CH, :] for j in range(size)])
            x = beside(
                [s0b[t, pl.ds(base + EDGE - 1 + j, 3)].reshape(48, LANES) for j in range(size)]
            )
            gw0[...] += nt_dot(g, x)

        for_blocks(rows, SUM_LINES, weights)

    def w_args():
        return (
            12,
            w_ext.at[:, pl.ds(EDGE, EDGE), :],
            w_ext.at[:, pl.ds(rows, EDGE), :],
            w_ext.at[:, pl.ds(0, EDGE), :],
            w_ext.at[:, pl.ds(rows + EDGE, EDGE), :],
        )

    def pull_start(t):
        facts = m_own[0]
        at = (t + 1).astype(F32)
        open_own = opened[own, :]
        for c in range(2):
            pull = jnp.zeros((rows, LANES), F32)
            for k in range(2):
                live = (facts[k : k + 1] == at).astype(F32)
                pull = pull + live * (u_kept[t, c] - t_own[k, c])
            w_ext[c, own, :] = open_own * (u_bar[c] + 2.0 * open_own * pull)
        halo_start(*w_args())

    def backward_step(i, carry):
        t = STEPS - 1 - i
        halo_wait(*w_args())
        grid = grid_mask[...]
        gr, gc = project(w_ext[0], w_ext[1], grid)
        gr, gc = grid * gr, grid * gc
        qr, qc = q_ext[t, 0], q_ext[t, 1]
        bar_r = gr + DT_ADV * (
            drows(gr * qr) + dcols(gr * qc) - (gr * drows(qr) + gc * drows(qc))
        )
        bar_c = gc + DT_ADV * (
            drows(gc * qr) + dcols(gc * qc) - (gr * dcols(qr) + gc * dcols(qc))
        )
        for c, bar in enumerate((bar_r, bar_c)):
            passed = opened[...] * bar
            q_ext[t, c] = passed
            passed = q_ext[t, c, own, :]
            u_bar[c] = passed
            force_bar = DT_FORCE * passed
            misc[2 + c] += sublanes(force_bar)
            frows[:, c, :] = force_bar
        for c in range(2, 16):
            frows[:, c, :] = jnp.zeros((rows, LANES), F32)

        first_pass_last(t)
        sums_start(4)
        second_pass(4, t, rows, xh_full, 2, sg, 1)
        bars_last(t)
        sums_start(3)
        weight_sums_last(t)
        second_pass(3, t, half, xh_half, 1, sgh, 2)

        def into_two(base, size, bars):
            for c in channel_blocks():
                bar_block(xh_half, 0, t, base, size, c, bars[:, c, :])

        bars_of(2, half, sgh, into_two)
        sums_start(2)
        weight_sums(2, t, half, sgh, h3)
        second_pass(2, t, half, xh_half, 0, sgh, 2)

        def into_one(base, size, bars):
            at = pl.multiple_of(2 * base, 2)
            for c in channel_blocks():
                direct = skip_bar[pl.ds(at, 2 * size), c, :].reshape(size, 2, 16, LANES)
                total = (direct + 0.25 * bars[:, None, c, :]).reshape(2 * size, 16, LANES)
                bar_block(xh_full, 1, t, at, 2 * size, c, total)

        bars_of(1, half, sgh, into_one)
        sums_start(1)
        weight_sums(1, t, half, sgh, pooled)
        second_pass(1, t, rows, xh_full, 1, sg, 1)

        def into_zero(base, size, bars):
            for c in channel_blocks():
                bar_block(xh_full, 0, t, base, size, c, bars[:, c, :])

        bars_of(0, rows, sg, into_zero)
        sums_start(0)
        weight_sums(0, t, rows, sg, h1)
        second_pass(0, t, rows, xh_full, 0, sg, 0)
        taps_first()
        for c in range(2):
            columns = []
            for kx in range(3):
                total = jnp.zeros((rows, LANES), F32)
                for ky in range(3):
                    total = total + taps[pl.ds(2 - ky, rows), 16 * ky + 3 * kx + c, :]
                columns.append(total)
            u_bar[c] += from_right(columns[0], 1) + columns[1] + from_left(columns[2], 1)

        @pl.when(t > 0)
        def _():
            pull_start(t - 1)

        weight_sums_first(t)
        return carry

    pull_start(jnp.int32(STEPS - 1))
    lax.fori_loop(0, STEPS, backward_step, 0)

    mid_rows = (LAYERS + 1) * 3 * CH
    gw[3 * CH : 9 * CH, :] = 0.5 * gw[3 * CH : 9 * CH, :]
    lane = lane_of((CH, 3 * CH))
    rest = jnp.concatenate([gw0[...], jnp.zeros((CH, 3 * CH - 48), F32)], axis=1)
    for which in range(2):
        for layer in range(LAYERS + 1):
            column = jnp.sum(gnorm[which, layer], axis=1, keepdims=True)
            if layer in HALF_SLOT:
                column = 0.5 * column
            rest = jnp.where(lane == 48 + 5 * which + layer, column, rest)
    for c in range(2):
        rest = jnp.where(lane == 58 + c, ghead[:, c : c + 1], rest)
    gw[mid_rows : mid_rows + CH, :] = rest
    g_send[...] = gw[...].astype(BF)
    chunk = gw.shape[0] // members
    piece = chunk // planes

    def chunk_at(which):
        return pl.ds(pl.multiple_of(which * chunk, 16), chunk)

    def piece_at(which):
        return pl.ds(pl.multiple_of(which * piece, 16), piece)

    def part_at(which):
        return pl.ds(pl.multiple_of(mine * chunk + which * piece, 16), piece)

    m_plane[mine] = jnp.concatenate(
        [jnp.sum(misc[k], axis=0, keepdims=True) for k in range(4)] + [jnp.zeros((4, LANES), F32)],
        axis=0,
    )

    def plane_copies(d):
        other = lax.rem(mine + d, members)
        source = lax.rem(mine + members - d, members)
        sends = [
            (g_send.at[chunk_at(other)], p_recv.at[mine], p_ss.at[0, d], p_rs.at[0, mine]),
            (m_plane.at[mine], m_plane.at[mine], p_ss.at[1, d], p_rs.at[1, mine]),
        ]
        lands = [
            (p_recv.at[source], p_rs.at[0, source]),
            (m_plane.at[source], p_rs.at[1, source]),
        ]
        return plane_id(d), sends, lands

    def line_copies(d):
        other = lax.rem(level + d, planes)
        source = lax.rem(level + planes - d, planes)
        sends = [
            (z_send.at[piece_at(other)], z_recv.at[level], z_ss.at[0, d], z_rs.at[0, level]),
            (m_line.at[level], m_line.at[level], z_ss.at[1, d], z_rs.at[1, level]),
        ]
        lands = [
            (z_recv.at[source], z_rs.at[0, source]),
            (m_line.at[source], z_rs.at[1, source]),
        ]
        return line_id(d), sends, lands

    def line_gather(d):
        source = lax.rem(level + planes - d, planes)
        sends = [(g_all.at[part_at(level)], g_all.at[part_at(level)], z_ss.at[2, d], z_rs.at[2, level])]
        lands = [(g_all.at[part_at(source)], z_rs.at[2, source])]
        return line_id(d), sends, lands

    def plane_gather(d):
        source = lax.rem(mine + members - d, members)
        sends = [(g_all.at[chunk_at(mine)], g_all.at[chunk_at(mine)], p_ss.at[2, d], p_rs.at[2, mine])]
        lands = [(g_all.at[chunk_at(source)], p_rs.at[2, source])]
        return plane_id(d), sends, lands

    def exchange(copies, count):
        def start(d, carry):
            peer, sends, lands = copies(d)
            for src, dst, sent, landed in sends:
                pltpu.make_async_remote_copy(
                    src_ref=src,
                    dst_ref=dst,
                    send_sem=sent,
                    recv_sem=landed,
                    device_id=peer,
                    device_id_type=MESH,
                ).start()
            return carry

        def finish(d, carry):
            peer, sends, lands = copies(d)
            for src, dst, sent, landed in sends:
                pltpu.make_async_copy(src, src, sent).wait()
            for dst, landed in lands:
                pltpu.make_async_copy(dst, dst, landed).wait()
            return carry

        lax.fori_loop(1, count, start, 0)
        lax.fori_loop(1, count, finish, 0)

    exchange(plane_copies, members)
    own_chunk = chunk_at(mine)

    def add_chunk(d, carry):
        gw[own_chunk, :] += p_recv[lax.rem(mine + d, members)].astype(F32)
        return carry

    lax.fori_loop(1, members, add_chunk, 0)
    z_send[...] = gw[own_chunk, :].astype(BF)
    m_line[level] = lax.fori_loop(
        0, members, lambda k, total: total + m_plane[k], jnp.zeros((8, LANES), F32)
    )
    exchange(line_copies, planes)

    def add_piece(d, total):
        return total + z_recv[lax.rem(level + d, planes)].astype(F32)

    total = lax.fori_loop(1, planes, add_piece, gw[part_at(level), :])
    g_all[part_at(level), :] = total.astype(BF)
    exchange(line_gather, planes)
    exchange(plane_gather, members)

    totals = lax.fori_loop(
        0, planes, lambda k, total: total + m_line[k], jnp.zeros((8, LANES), F32)
    )
    totals = jnp.broadcast_to(jnp.sum(totals, axis=1, keepdims=True), (8, LANES))

    def squares(i, total):
        at = pl.ds(pl.multiple_of(i * 64, 64), 64)
        block = g_all[at, :].astype(F32)
        return total + jnp.sum((block * block).reshape(8, 8, 3 * CH), axis=0)

    square = lax.fori_loop(0, gw.shape[0] // 64, squares, jnp.zeros((8, 3 * CH), F32))
    square = jnp.sum(jnp.sum(square, axis=0, keepdims=True), axis=1, keepdims=True)
    count = totals[1:2]
    raw = square + totals[2:3] * totals[2:3] + totals[3:4] * totals[3:4]
    norm = jnp.sqrt(raw) / count
    factor = jnp.minimum(1.0, CLIP_NORM / norm) / count
    scalars[...] = jnp.concatenate([totals[:4], norm, factor, totals[6:]], axis=0)


def train(keyframes, boxes, velocity, targets, w_in, w_mid, norm_params, head_params):
    ranks = lax.axis_size("rows")
    planes = lax.axis_size("batch") // 2
    members = 2 * ranks
    unit = 16 * members * planes
    lines = -(-((LAYERS + 1) * 3 * CH + CH) // unit) * unit
    chunk = lines // members
    parts = ranks // 2
    tile = velocity.shape[2]
    rows, half, ext = 2 * tile, tile, 2 * tile + 2 * EDGE
    vmem = pl.BlockSpec(memory_space=pltpu.VMEM)

    def kept(count):
        return pltpu.VMEM((STEPS, count + 2, CH, LANES), BF)

    smem = pl.BlockSpec(memory_space=pltpu.SMEM)
    args = (keyframes, boxes, velocity, targets, w_in, w_mid, norm_params, head_params)
    return pl.pallas_call(
        functools.partial(train_kernel, ranks, planes),
        out_shape=(
            jax.ShapeDtypeStruct((lines, 3 * CH), BF),
            jax.ShapeDtypeStruct((8, LANES), F32),
        ),
        in_specs=[smem] * 2 + [vmem] * 6,
        out_specs=(vmem,) * 2,
        scratch_shapes=[
            pltpu.VMEM((2, 16, LANES), F32),
            pltpu.VMEM((LAYERS + 1, 3 * CH, 3 * CH), BF),
            pltpu.VMEM((LAYERS + 1, 3 * CH, 3 * CH), BF),
            pltpu.VMEM((CH, 48), BF),
            pltpu.VMEM((48, CH), BF),
            pltpu.VMEM((2, LAYERS + 1, CH, LANES), F32),
            pltpu.VMEM((16, CH), BF),
            pltpu.VMEM((CH, 16), BF),
            pltpu.VMEM((2, 1, LANES), F32),
            pltpu.VMEM((3, CH // 2, 8, LANES), F32),
            pltpu.VMEM((2, 3 * (LAYERS + 1), CH, LANES), F32),
            pltpu.VMEM((LANES, LANES), F32),
            pltpu.VMEM((lines, 3 * CH), F32),
            pltpu.VMEM((CH, 48), F32),
            pltpu.VMEM((2, LAYERS + 1, CH, LANES), F32),
            pltpu.VMEM((CH, 16), F32),
            pltpu.VMEM((4, 8, LANES), F32),
            pltpu.VMEM((2, ext, LANES), F32),
            pltpu.VMEM((2, 2, rows, LANES), F32),
            pltpu.VMEM((2, 16, LANES), F32),
            pltpu.VMEM((ext, LANES), F32),
            pltpu.VMEM((ext, LANES), F32),
            pltpu.VMEM((ext, 16, LANES), F32),
            pltpu.VMEM((STEPS, ext, 16, LANES), BF),
            pltpu.VMEM((STEPS, 2, ext, LANES), F32),
            pltpu.VMEM((STEPS, 2, rows, LANES), F32),
            pltpu.VMEM((2, ext, LANES), F32),
            pltpu.VMEM((2, rows, LANES), F32),
            pltpu.VMEM((rows, 16, LANES), F32),
            pltpu.VMEM((rows + 2, 48, LANES), F32),
            kept(rows),
            kept(rows),
            kept(half),
            kept(half),
            kept(half),
            pltpu.VMEM((3, STEPS, rows, CH, LANES), BF),
            pltpu.VMEM((2, STEPS, half, CH, LANES), BF),
            pltpu.VMEM((STEPS, LAYERS + 1, CH, LANES), F32),
            pltpu.VMEM((rows, CH, LANES), F32),
            pltpu.VMEM((rows, CH, LANES), F32),
            pltpu.VMEM((rows + 2, 3 * CH, LANES), BF),
            pltpu.VMEM((half + 2, 3 * CH, LANES), BF),
            pltpu.VMEM((10, 2, CH, LANES), BF),
            pltpu.VMEM((LAYERS + 1, 2, CH, LANES), BF),
            pltpu.VMEM((2 * LANES, 3 * LANES), BF),
            pltpu.VMEM((3, CH, LANES), F32),
            pltpu.VMEM((2, CH, LANES), F32),
            pltpu.VMEM((10, 16, LANES), F32),
            pltpu.VMEM((10, parts - 1, 16, LANES), F32),
            pltpu.VMEM((lines, 3 * CH), BF),
            pltpu.VMEM((members, chunk, 3 * CH), BF),
            pltpu.VMEM((chunk, 3 * CH), BF),
            pltpu.VMEM((planes, chunk // planes, 3 * CH), BF),
            pltpu.VMEM((members, 8, LANES), F32),
            pltpu.VMEM((planes, 8, LANES), F32),
            pltpu.SemaphoreType.DMA((2, 3)),
            pltpu.SemaphoreType.DMA((2, 3)),
            pltpu.SemaphoreType.DMA((3,)),
            pltpu.SemaphoreType.DMA((13, 2)),
            pltpu.SemaphoreType.DMA((13, 2)),
            pltpu.SemaphoreType.DMA((10, parts - 1)),
            pltpu.SemaphoreType.DMA((10, parts - 1)),
            pltpu.SemaphoreType.DMA((3, members)),
            pltpu.SemaphoreType.DMA((3, members)),
            pltpu.SemaphoreType.DMA((3, planes)),
            pltpu.SemaphoreType.DMA((3, planes)),
        ],
        compiler_params=pltpu.CompilerParams(
            collective_id=0, has_side_effects=True, vmem_limit_bytes=60 * 2**20
        ),
        name="train",
    )(*args)


def adam_kernel(g_all, scalars, *refs):
    olds = [refs[3 * k : 3 * k + 3] for k in range(4)]
    news = [refs[12 + 3 * k : 15 + 3 * k] for k in range(4)]
    low_in, low_mid, low_head, wide, turned, lines = refs[24:]
    factor = scalars[5:6, :]
    at_step = pl.program_id(0)

    def update(which, at, g, low=None):
        weight, moment, second = (ref[at] for ref in olds[which])
        moment = BETA_ONE * moment + (1 - BETA_ONE) * g
        second = BETA_TWO * second + (1 - BETA_TWO) * g * g
        mhat = moment / (1 - BETA_ONE**STEP_NUM)
        vhat = second / (1 - BETA_TWO**STEP_NUM)
        change = mhat / (jnp.sqrt(vhat) + ADAM_EPS) + DECAY * weight
        weight = weight - RATES[which] * change
        for ref, value in zip(news[which], (weight, moment, second)):
            ref[at] = value
        if low is not None:
            low[at] = weight.astype(BF)

    mid_rows = (LAYERS + 1) * 3 * CH

    @pl.when(at_step == 0)
    def _():
        wide[0] = g_all[:mid_rows, :LANES].astype(F32) * factor
        tail = g_all[:mid_rows, LANES:].astype(F32) * factor[:, :CH]
        wide[1] = jnp.concatenate([tail, jnp.zeros_like(tail)], axis=1)
        rest = g_all[mid_rows : mid_rows + CH, :LANES].astype(F32) * factor
        rest = jnp.concatenate([rest, jnp.zeros_like(rest)], axis=0)
        turned[...] = rest.T
        for ch in range(3):
            for ky in range(3):
                g = turned[pl.ds(16 * ky + ch, 3, 3), :]
                update(0, (ch, ky), g[:, :CH], low_in)
        for layer in range(LAYERS + 1):
            g = turned[pl.ds(48 + layer, 2, LAYERS + 1), :]
            update(2, (layer,), g[:, :CH])
        bias = scalars[2:4, :] * factor
        g = jnp.where(lax.broadcasted_iota(jnp.int32, (2, LANES), 1) < CH, turned[58:60, :], bias)
        update(3, (slice(None),), g[:, : CH + 1], low_head)

    low_lanes = lax.broadcasted_iota(jnp.int32, (CH // 2, LANES), 1) < CH
    for ky in range(3):

        @pl.when(at_step == ky)
        def _():
            for k in range(LAYERS + 1):
                for kx in range(3):
                    base = k * 3 * CH + kx * CH
                    even = wide[ky // 2, pl.ds(base, CH // 2, 2), :]
                    odd = wide[ky // 2, pl.ds(base + 1, CH // 2, 2), :]
                    if ky % 2:
                        even = pltpu.roll(even, CH, 1)
                    else:
                        odd = pltpu.roll(odd, CH, 1)
                    lines[kx, :, k, :] = jnp.where(low_lanes, even, odd)

    for kx in range(3):
        g = jnp.concatenate(
            [lines[kx, a, : LAYERS + 1, :] for a in range(CH // 2)], axis=1
        )
        update(1, (kx,), g, low_mid)


def adam(g_all, scalars, params, moments, seconds):
    shapes = [w.shape for w in params]
    whole = lambda shape: pl.BlockSpec(shape, lambda i: (0,) * len(shape))
    mid = pl.BlockSpec((3,) + shapes[1][1:], lambda i: (i, 0, 0))
    spec = lambda k: mid if k == 1 else whole(shapes[k])
    states = [x for group in zip(params, moments, seconds) for x in group]
    lows = (0, 1, 3)
    return pl.pallas_call(
        adam_kernel,
        grid=(3,),
        out_shape=tuple(jax.ShapeDtypeStruct(x.shape, F32) for x in states)
        + tuple(jax.ShapeDtypeStruct(shapes[k], BF) for k in lows),
        in_specs=[whole(g_all.shape), whole(scalars.shape)] + [spec(k // 3) for k in range(12)],
        out_specs=tuple(spec(k // 3) for k in range(12)) + tuple(spec(k) for k in lows),
        scratch_shapes=[
            pltpu.VMEM((2, (LAYERS + 1) * 3 * CH, LANES), F32),
            pltpu.VMEM((LANES, LANES), F32),
            pltpu.VMEM((3, CH // 2, 8, LANES), F32),
        ],
        compiler_params=pltpu.CompilerParams(vmem_limit_bytes=40 * 2**20),
        name="adam",
    )(g_all, scalars, *states)


def in_order(group):
    first, mid, norm, head = group
    return (
        jnp.transpose(first, (1, 2, 3, 0)),
        jnp.transpose(mid, (1, 0, 2)),
        jnp.transpose(norm, (1, 0, 2)),
        head,
    )


def out_of_order(group):
    first, mid, norm, head = group
    return (
        jnp.transpose(first, (3, 0, 1, 2)),
        jnp.transpose(mid, (1, 0, 2)),
        jnp.transpose(norm, (1, 0, 2)),
        head,
    )


def shards(
    velocity,
    targets,
    keyframes,
    boxes,
    w_in,
    w_mid,
    norm_params,
    head_params,
    m_in,
    m_mid,
    m_norm,
    m_head,
    v_in,
    v_mid,
    v_norm,
    v_head,
):
    params = in_order((w_in, w_mid, norm_params, head_params))
    moments = in_order((m_in, m_mid, m_norm, m_head))
    seconds = in_order((v_in, v_mid, v_norm, v_head))
    g_all, scalars = train(keyframes, boxes, velocity, targets, *params)
    result = adam(g_all, scalars, params, moments, seconds)
    new_w, new_m, new_v = (out_of_order(result[k:12:3]) for k in range(3))
    low_in, low_mid, low_head = result[12:]
    return (
        *new_w,
        *new_m,
        *new_v,
        jnp.transpose(low_in, (3, 0, 1, 2)),
        jnp.transpose(low_mid, (1, 0, 2)),
        low_head,
        scalars[0, 0],
        scalars[1, 0],
        scalars[4, 0],
    )


def solution(mesh):
    return jax.shard_map(
        shards,
        mesh=mesh,
        in_specs=(
            P("batch", None, "rows", None),
            P("batch", None, None, "rows", None),
            P("batch", None),
            P("batch", None, None),
        )
        + (P(),) * 12,
        out_specs=(P(),) * 18,
        check_vma=False,
    )
```

```python
import functools

import jax
import jax.numpy as jnp
from jax import lax
from jax.experimental import pallas as pl
from jax.experimental.pallas import tpu as pltpu
from jax.sharding import PartitionSpec as P

CH = 64
GROUPS = 8
LAYERS = 4
STEPS = 4
JACOBI = 4
STEP_NUM = 10
LANES = 128
EDGE = 8

EPS_NORM = 1e-05
DT_FORCE = 0.5
DT_ADV = 0.2
CLIP_NORM = 0.001
BETA_ONE = 0.9
BETA_TWO = 0.95
ADAM_EPS = 1e-08
DECAY = 0.01
RATES = (0.2, 0.05, 1.0, 0.15)

BF = jnp.bfloat16
F32 = jnp.float32
MESH = pl.DeviceIdType.MESH
FULL_SLOT = {0: 0, 1: 1, 4: 2}
HALF_SLOT = {2: 0, 3: 1}
ACT_LINES = 64
CONV_LINES = 64
BAR_LINES = 32
SUM_LINES = 64


def nt_dot(a, b):
    return lax.dot_general(a, b, (((1,), (1,)), ((), ())), preferred_element_type=F32)


def nn_dot(a, b):
    return jnp.dot(a, b, preferred_element_type=F32)


def beside(rows):
    return jnp.concatenate(rows, axis=1)


def lane_of(shape):
    return lax.broadcasted_iota(jnp.int32, shape, len(shape) - 1)


def from_left(x, by):
    return jnp.where(lane_of(x.shape) < by, jnp.zeros((), x.dtype), pltpu.roll(x, by, x.ndim - 1))


def from_right(x, by):
    moved = pltpu.roll(x, LANES - by, x.ndim - 1)
    return jnp.where(lane_of(x.shape) >= LANES - by, jnp.zeros((), x.dtype), moved)


def pair_sum(x):
    even = lane_of(x.shape) % 2 == 0
    last = x.ndim - 1
    return x + jnp.where(even, pltpu.roll(x, LANES - 1, last), pltpu.roll(x, 1, last))


def drows(x):
    count = x.shape[0]
    return 0.5 * (pltpu.roll(x, count - 1, 0) - pltpu.roll(x, 1, 0))


def dcols(x):
    return 0.5 * (from_right(x, 1) - from_left(x, 1))


def nsum(x):
    count = x.shape[0]
    return (
        pltpu.roll(x, count - 1, 0) + pltpu.roll(x, 1, 0) + from_right(x, 1) + from_left(x, 1)
    )


def project(vr, vc, grid):
    div = grid * (drows(vr) + dcols(vc))
    press = -0.25 * div
    for sweep in range(JACOBI - 1):
        press = grid * (0.25 * (nsum(press) - div))
    return vr - drows(press), vc - dcols(press)


def sublanes(x):
    return jnp.sum(x.reshape(x.shape[0] // 8, 8, LANES), axis=0)


def group_rows(x):
    return jnp.sum(x.reshape(GROUPS, CH // GROUPS, LANES), axis=1)


def spread(x):
    return jnp.concatenate(
        [jnp.broadcast_to(x[g : g + 1], (CH // GROUPS, LANES)) for g in range(GROUPS)], axis=0
    )


def gradient_lines(members):
    groups = ((0,), (1, 2), (3, 4))
    chunks, starts, at = [], [], []
    start = 0
    for group in groups:
        place = start
        for layer in group:
            at.append(place)
            place += 3 * CH
        chunk = -(-(place - start) // (16 * members)) * 16
        starts.append(start)
        chunks.append(chunk)
        start += chunk * members
    return starts, chunks, at, start


def train_kernel(
    ranks,
    planes,
    keys,
    boxes,
    vel,
    tgt,
    w_in,
    w_mid,
    norm_params,
    head,
    g_all,
    small_out,
    scalars,
    meta,
    wf,
    wb,
    w0f,
    w0b,
    norms,
    headf,
    headb,
    bias,
    lines,
    wide,
    small,
    gw,
    gw0,
    gnorm,
    ghead,
    misc,
    u_ext,
    t_own,
    m_own,
    opened,
    grid_mask,
    s0,
    s0b,
    q_ext,
    u_kept,
    w_ext,
    u_bar,
    frows,
    taps,
    h1,
    skip,
    pooled,
    h3,
    h4,
    xh_full,
    xh_half,
    inv_kept,
    zbuf,
    skip_bar,
    sg,
    sgh,
    edges,
    g_halo,
    pool_mat,
    coef,
    acc,
    st_send,
    st_recv,
    g_send,
    p_recv,
    z_recv,
    m_plane,
    m_line,
    in_send,
    in_recv,
    in_local,
    halo_send,
    halo_recv,
    st_ss,
    st_rs,
    p_ss,
    p_rs,
    z_ss,
    z_rs,
):
    quarter = ranks // 4
    parts = ranks // 2
    tile = vel.shape[2]
    rows = 2 * tile
    half = rows // 2
    batch_at = lax.axis_index("batch")
    row_at = lax.axis_index("rows")
    core = lax.rem(batch_at, 2)
    plane = batch_at - core
    sample = row_at // quarter
    part = 2 * lax.rem(row_at, quarter) + core

    def owner(which, piece):
        return (plane + lax.rem(piece, 2), which * quarter + piece // 2)

    u_ext[...] = jnp.zeros_like(u_ext)
    q_ext[...] = jnp.zeros_like(q_ext)
    w_ext[...] = jnp.zeros_like(w_ext)
    g_halo[...] = jnp.zeros_like(g_halo)
    for kept, count in ((h1, rows), (skip, rows), (pooled, half), (h3, half), (h4, half)):
        for t in range(STEPS):
            kept[t, 0] = jnp.zeros((CH, LANES), BF)
            kept[t, count + 1] = jnp.zeros((CH, LANES), BF)

    barrier = pltpu.get_barrier_semaphore()
    members = 2 * ranks
    starts, chunks, line_at, all_lines = gradient_lines(members)
    offsets = [sum(chunks[:k]) for k in range(3)]
    mine = core * ranks + row_at

    def plane_id(d):
        other = lax.rem(mine + d, members)
        return (plane + other // ranks, lax.rem(other, ranks))

    def greet(d, carry):
        pl.semaphore_signal(barrier, inc=1, device_id=plane_id(d), device_id_type=MESH)
        return carry

    lax.fori_loop(1, members, greet, 0)
    level = batch_at // 2

    def line_id(d):
        return (2 * lax.rem(level + d, planes) + core, row_at)

    def greet_line(d, carry):
        pl.semaphore_signal(barrier, inc=1, device_id=line_id(d), device_id_type=MESH)
        return carry

    lax.fori_loop(1, planes, greet_line, 0)

    line_is = lax.broadcasted_iota(jnp.int32, (16, LANES), 0)
    for j in range(2):
        values = [keys[j, k] for k in range(2)]
        values += [boxes[j, b, k] for b in range(2) for k in range(4)]
        facts = jnp.zeros((16, LANES), F32)
        for k, value in enumerate(values):
            facts = jnp.where(line_is == k, value.astype(F32), facts)
        meta[j] = facts

    low_lanes = lane_of((CH // 2, LANES)) < CH
    for ky in range(3):
        for kx in range(3):
            for a in range(CH // 2):
                lines[kx, a, : LAYERS + 1, :] = w_mid[3 * ky + kx, :, a * LANES : (a + 1) * LANES]
        for k in range(LAYERS + 1):
            left, mid, right = (lines[kx, :, k, :] for kx in range(3))
            slab = 3 * k + ky
            even, odd = pl.ds(0, CH // 2, 2), pl.ds(1, CH // 2, 2)
            wide[0, slab, even, :] = jnp.where(low_lanes, left, pltpu.roll(mid, CH, 1))
            wide[0, slab, odd, :] = jnp.where(low_lanes, pltpu.roll(left, CH, 1), mid)
            wide[1, slab, even, :] = right
            wide[1, slab, odd, :] = pltpu.roll(right, CH, 1)
    low_lanes = lane_of((CH, LANES)) < CH
    for k in range(LAYERS + 1):
        for ky in range(3):
            slab = 3 * k + ky
            at = slice(ky * CH, (ky + 1) * CH)
            first, last = wide[0, slab], wide[1, slab]
            wf[k, at, :] = jnp.concatenate([first, last[:, :CH]], axis=1).astype(BF)
            turned = jnp.concatenate([first, last], axis=0).T
            left, mid = turned[:CH], turned[CH:]
            first = jnp.where(low_lanes, left, pltpu.roll(mid, CH, 1))
            last = pltpu.roll(left, CH, 1)
            wb[k, at, :] = jnp.concatenate([first, last[:, :CH]], axis=1).astype(BF)
    pl.semaphore_wait(barrier, members + planes - 2)

    def incoming(place):
        at = pl.ds(pl.multiple_of(EDGE + place * tile, 8), tile)
        here = pl.ds(pl.multiple_of(place * tile, 8), tile)
        return u_ext.at[:, at, :], t_own.at[:, :, here, :], m_own.at[place]

    place = lax.rem(row_at, 2)
    for j in range(2):
        to_batch, to_row = owner(2 * core + j, row_at // 2)
        stays = (to_batch == batch_at) & (to_row == row_at)
        for k, (src, dst) in enumerate(zip((vel.at[j], tgt.at[j], meta.at[j]), incoming(place))):

            @pl.when(stays)
            def _():
                pltpu.make_async_copy(src, dst, in_local.at[k]).start()

            @pl.when(jnp.logical_not(stays))
            def _():
                pltpu.make_async_remote_copy(
                    src_ref=src,
                    dst_ref=dst,
                    send_sem=in_send.at[j, k],
                    recv_sem=in_recv.at[place, k],
                    device_id=(to_batch, to_row),
                    device_id_type=MESH,
                ).start()

    small[...] = jnp.zeros_like(small)
    for ch in range(3):
        for ky in range(3):
            taps_in = w_in[ch, ky]
            taps_in = jnp.concatenate([taps_in, jnp.zeros_like(taps_in)], axis=1)
            small[pl.ds(16 * ky + ch, 3, 3), :] = taps_in
    for layer in range(LAYERS + 1):
        pair = norm_params[layer]
        small[48 + 2 * layer : 50 + 2 * layer, :] = jnp.concatenate(
            [pair, jnp.zeros_like(pair)], axis=1
        )
    pair = head[:, :CH]
    small[64:66, :] = jnp.concatenate([pair, jnp.zeros_like(pair)], axis=1)
    w0b[...] = small[:48, :CH].astype(BF)
    headf[...] = small[64:80, :CH].astype(BF)
    turned = small[...].T[:CH]
    w0f[...] = turned[:, :48].astype(BF)
    headb[...] = turned[:, 64:80].astype(BF)
    for which in range(2):
        for layer in range(LAYERS + 1):
            at = 48 + 2 * layer + which
            norms[which, layer] = jnp.broadcast_to(turned[:, at : at + 1], (CH, LANES))
        bias[which] = jnp.broadcast_to(head[which : which + 1, CH : CH + 1], (1, LANES))

    for j in range(2):
        to_batch, to_row = owner(2 * core + j, row_at // 2)
        stays = (to_batch == batch_at) & (to_row == row_at)
        for k, src in enumerate((vel.at[j], tgt.at[j], meta.at[j])):

            @pl.when(stays)
            def _():
                pltpu.make_async_copy(src, src, in_local.at[k]).wait()

            @pl.when(jnp.logical_not(stays))
            def _():
                pltpu.make_async_copy(src, src, in_send.at[j, k]).wait()

    for i in range(2):
        from_batch = plane + sample // 2
        from_row = 2 * part + i
        stays = (from_batch == batch_at) & (from_row == row_at)
        for k, dst in enumerate(incoming(i)):

            @pl.when(jnp.logical_not(stays))
            def _():
                pltpu.make_async_copy(dst, dst, in_recv.at[i, k]).wait()

    has_prev = part > 0
    has_next = part < parts - 1
    prev_id = owner(sample, jnp.maximum(part - 1, 0))
    next_id = owner(sample, jnp.minimum(part + 1, parts - 1))

    def halo_copies(slot, low_src, high_src, top_dst, bottom_dst):
        to_prev = pltpu.make_async_remote_copy(
            src_ref=low_src,
            dst_ref=bottom_dst,
            send_sem=halo_send.at[slot, 0],
            recv_sem=halo_recv.at[slot, 0],
            device_id=prev_id,
            device_id_type=MESH,
        )
        to_next = pltpu.make_async_remote_copy(
            src_ref=high_src,
            dst_ref=top_dst,
            send_sem=halo_send.at[slot, 1],
            recv_sem=halo_recv.at[slot, 1],
            device_id=next_id,
            device_id_type=MESH,
        )
        return to_prev, to_next

    def halo_start(*args):
        to_prev, to_next = halo_copies(*args)

        @pl.when(has_prev)
        def _():
            to_prev.start()

        @pl.when(has_next)
        def _():
            to_next.start()

    def halo_wait(*args):
        to_prev, to_next = halo_copies(*args)

        @pl.when(has_prev)
        def _():
            to_prev.wait_send()
            to_next.wait_recv()

        @pl.when(has_next)
        def _():
            to_next.wait_send()
            to_prev.wait_recv()

    def ext_halo(slot, ref):
        args = (
            slot,
            ref.at[:, pl.ds(EDGE, EDGE), :],
            ref.at[:, pl.ds(rows, EDGE), :],
            ref.at[:, pl.ds(0, EDGE), :],
            ref.at[:, pl.ds(rows + EDGE, EDGE), :],
        )
        halo_start(*args)
        halo_wait(*args)

    def group_copies(slot):
        return [
            pltpu.make_async_remote_copy(
                src_ref=st_send.at[slot],
                dst_ref=st_recv.at[slot, d - 1],
                send_sem=st_ss.at[slot, d - 1],
                recv_sem=st_rs.at[slot, d - 1],
                device_id=owner(sample, lax.rem(part + d, parts)),
                device_id_type=MESH,
            )
            for d in range(1, parts)
        ]

    def group_start(slot, first, second):
        st_send[slot] = jnp.concatenate([group_rows(first), group_rows(second)], axis=0)
        for copy in group_copies(slot):
            copy.start()

    def group_finish(slot):
        total = st_send[slot]
        for d, copy in enumerate(group_copies(slot)):
            copy.wait()
            total = total + st_recv[slot, d]
        total = jnp.broadcast_to(jnp.sum(total, axis=1, keepdims=True), total.shape)
        return total[:GROUPS], total[GROUPS:]

    ext = rows + 2 * EDGE
    row_is = lax.broadcasted_iota(jnp.int32, (ext, LANES), 0) - EDGE + part * rows
    inside_grid = ((row_is >= 0) & (row_is < parts * rows)).astype(F32)
    row_f = row_is.astype(F32)
    col_f = lane_of((ext, LANES)).astype(F32)
    covered = jnp.zeros((ext, LANES), F32)
    facts = m_own[0]
    for b in range(2):
        bounds = [facts[2 + 4 * b + k : 3 + 4 * b + k] for k in range(4)]
        inside = (
            (row_f >= bounds[0])
            & (row_f < bounds[1])
            & (col_f >= bounds[2])
            & (col_f < bounds[3])
        )
        covered = jnp.maximum(covered, inside.astype(F32))
    grid_mask[...] = inside_grid
    opened[...] = inside_grid * (1.0 - covered)
    own = pl.ds(EDGE, rows)
    misc[...] = jnp.zeros_like(misc)
    live_slots = (facts[0:1] > 0.5).astype(F32) + (facts[1:2] > 0.5).astype(F32)
    misc[1] = sublanes(opened[own, :] * live_slots)
    gw[...] = jnp.zeros_like(gw)
    gw0[...] = jnp.zeros_like(gw0)
    gnorm[...] = jnp.zeros_like(gnorm)
    ghead[...] = jnp.zeros_like(ghead)
    s0[...] = jnp.zeros_like(s0)
    frows[...] = jnp.zeros_like(frows)
    u_bar[...] = jnp.zeros_like(u_bar)

    ext_halo(10, u_ext)

    source = lax.broadcasted_iota(jnp.int32, pool_mat.shape, 0) % LANES
    target = lane_of(pool_mat.shape)
    column = target % LANES + 2 * (target // LANES - 1)
    pool_mat[...] = jnp.where(source // 2 == (column + 2) // 2 - 1, 0.25, 0.0).astype(BF)

    for kx in range(3):
        field = opened[...]
        s0[:, 3 * kx + 2, :] = (from_left(field, 1), field, from_right(field, 1))[kx]

    def put_shifted(dst, at, c, x, by, order):
        copies = (from_left(x, by), x, from_right(x, by))
        for place_at, which in enumerate(order):
            dst[at, slice(place_at * CH + c.start, place_at * CH + c.stop), :] = copies[which]

    FORWARD = (0, 1, 2)
    BACKWARD = (2, 1, 0)

    def spread_halo(dst, lines, count, by, order):
        for at, line in ((0, lines[0]), (count + 1, lines[1])):
            put_shifted(dst, at, slice(0, CH), line, by, order)

    def for_blocks(count, size, body):
        size = min(size, count)
        if size == count:
            body(0, size)
            return

        def step(i, carry):
            body(pl.multiple_of(i * size, size), size)
            return carry

        lax.fori_loop(0, count // size, step, 0)

    def channel_blocks():
        return [slice(16 * c, 16 * c + 16) for c in range(CH // 16)]

    def make_norm(layer, t, sums, squares, count):
        group_start(layer, sums, squares)
        sums, squares = group_finish(layer)
        size = CH // GROUPS * count * LANES * parts
        mean = sums / size
        inverse = lax.rsqrt(squares / size - mean * mean + EPS_NORM)
        scale = spread(inverse)
        inv_kept[t, layer] = scale
        scale = 0.5 * scale * norms[0, layer]
        coef[0] = scale
        coef[1] = 0.5 * norms[1, layer] - spread(mean) * scale

    def activate(z, c):
        n = z * coef[0, c] + coef[1, c]
        return n, n * jnp.tanh(n) + n

    def conv_sums(count, size, rows_of):
        size = min(size, count)
        zero = jnp.zeros((CH, LANES), F32)

        def step(i, carry):
            sums, squares = carry
            base = i * size
            for j, z in enumerate(rows_of(base, size)):
                zbuf[base + j] = z
                sums = sums + z
                squares = squares + z * z
            return sums, squares

        if size == count:
            return step(0, (zero, zero))
        return lax.fori_loop(0, count // size, step, (zero, zero))

    def tap_rows(y, j, at):
        return y[at * CH : (at + 1) * CH, j * LANES : (j + 1) * LANES]

    def conv_of(src, layer):
        def rows_of(base, size):
            y = nn_dot(wf[layer], beside([src[base + j] for j in range(size + 2)]))
            return [
                tap_rows(y, j, 0) + tap_rows(y, j + 1, 1) + tap_rows(y, j + 2, 2)
                for j in range(size)
            ]

        return rows_of

    def conv_last(base, size):
        y = nn_dot(wf[4], beside([sg[base + j] for j in range(size + 2)]))
        low = base // 2
        x = nn_dot(wf[3], beside([sgh[low + j] for j in range(size // 2 + 2)]))
        result = []
        for j in range(size):
            z = tap_rows(y, j, 0) + tap_rows(y, j + 1, 1) + tap_rows(y, j + 2, 2)
            for ky in range(3):
                z = z + tap_rows(x, (j + ky - 1) // 2 + 1, ky)
            result.append(z)
        return result

    def finish_plain(t, layer, count, kept, xh, xh_at, dst, by, slot):
        for which, line in enumerate((0, count - 1)):
            edges[slot, which] = activate(zbuf[line], slice(0, CH))[1].astype(BF)
        args = (slot, edges.at[slot, 0], edges.at[slot, 1], kept.at[t, 0], kept.at[t, count + 1])
        halo_start(*args)

        def block(base, size):
            at = pl.ds(base + 1, size)
            for c in channel_blocks():
                n, h = activate(zbuf[pl.ds(base, size), c, :], c)
                xh[xh_at, t, pl.ds(base, size), c, :] = n.astype(BF)
                low = h.astype(BF)
                kept[t, at, c, :] = low
                put_shifted(dst, at, c, low, by, FORWARD)

        for_blocks(count, ACT_LINES, block)
        halo_wait(*args)
        spread_halo(dst, (kept[t, 0], kept[t, count + 1]), count, by, FORWARD)

    def pool_pairs(low, size):
        pairs = jnp.concatenate(
            [beside([low[2 * j], low[2 * j + 1]]) for j in range(size // 2)], axis=0
        )
        return nn_dot(pairs, pool_mat[...]).astype(BF).reshape(size // 2, CH, 3 * LANES)

    def finish_skip(t):
        for which, line in enumerate((0, rows - 2)):
            low = activate(zbuf[pl.ds(line, 2)], slice(0, CH))[1].astype(BF)
            edges[1, which] = low[which]
            edges[2, which] = pool_pairs(low, 2)[0, :, LANES : 2 * LANES]
        skip_args = (1, edges.at[1, 0], edges.at[1, 1], skip.at[t, 0], skip.at[t, rows + 1])
        pool_args = (2, edges.at[2, 0], edges.at[2, 1], pooled.at[t, 0], pooled.at[t, half + 1])
        halo_start(*pool_args)
        halo_start(*skip_args)

        def block(base, size):
            at = pl.ds(base + 1, size)
            lows = []
            for c in channel_blocks():
                n, h = activate(zbuf[pl.ds(base, size), c, :], c)
                xh_full[1, t, pl.ds(base, size), c, :] = n.astype(BF)
                low = h.astype(BF)
                skip[t, at, c, :] = low
                put_shifted(sg, at, c, low, 1, FORWARD)
                lows.append(low)
            small = pool_pairs(jnp.concatenate(lows, axis=1), size)
            at = pl.ds(base // 2 + 1, size // 2)
            pooled[t, at] = small[:, :, LANES : 2 * LANES]
            for k in range(3):
                sgh[at, k * CH : (k + 1) * CH, :] = small[:, :, k * LANES : (k + 1) * LANES]

        for_blocks(rows, ACT_LINES, block)
        halo_wait(*pool_args)
        halo_wait(*skip_args)
        spread_halo(sgh, (pooled[t, 0], pooled[t, half + 1]), half, 2, FORWARD)
        spread_halo(sg, (skip[t, 0], skip[t, rows + 1]), rows, 1, FORWARD)

    def finish_last(t):
        def block(base, size):
            lows = []
            for c in channel_blocks():
                n, h = activate(zbuf[pl.ds(base, size), c, :], c)
                xh_full[2, t, pl.ds(base, size), c, :] = n.astype(BF)
                lows.append(h.astype(BF))
            low = jnp.concatenate(lows, axis=1)
            force = nn_dot(headf[...], beside([low[j] for j in range(size)]))
            for j in range(size):
                frows[base + j] = force[:, j * LANES : (j + 1) * LANES]

        for_blocks(rows, ACT_LINES, block)

    def forward_step(t, carry):
        for c in range(2):
            field = u_ext[c]
            for kx, moved in enumerate((from_left(field, 1), field, from_right(field, 1))):
                s0[:, 3 * kx + c, :] = moved
        s0b[t] = s0[...].astype(BF)

        def first_rows(base, size):
            x = beside(
                [s0b[t, pl.ds(base + EDGE - 1 + j, 3)].reshape(48, LANES) for j in range(size)]
            )
            z = nn_dot(w0f[...], x)
            return [z[:, j * LANES : (j + 1) * LANES] for j in range(size)]

        make_norm(0, t, *conv_sums(rows, CONV_LINES, first_rows), rows)
        finish_plain(t, 0, rows, h1, xh_full, 0, sg, 1, 0)
        make_norm(1, t, *conv_sums(rows, CONV_LINES, conv_of(sg, 0)), rows)
        finish_skip(t)
        make_norm(2, t, *conv_sums(half, CONV_LINES, conv_of(sgh, 1)), half)
        finish_plain(t, 2, half, h3, xh_half, 0, sgh, 2, 3)
        make_norm(3, t, *conv_sums(half, CONV_LINES, conv_of(sgh, 2)), half)
        finish_plain(t, 3, half, h4, xh_half, 1, sgh, 1, 4)
        make_norm(4, t, *conv_sums(rows, CONV_LINES, conv_last), rows)
        finish_last(t)

        for c in range(2):
            force = frows[:, c, :] + bias[c]
            q_ext[t, c, own, :] = (u_ext[c, own, :] + DT_FORCE * force) * opened[own, :]
        ext_halo(11, q_ext.at[t])
        qr, qc = q_ext[t, 0], q_ext[t, 1]
        grid = grid_mask[...]
        vr = grid * (qr - DT_ADV * (qr * drows(qr) + qc * dcols(qr)))
        vc = grid * (qc - DT_ADV * (qr * drows(qc) + qc * dcols(qc)))
        facts = m_own[0]
        at = (t + 1).astype(F32)
        for c, moved in enumerate(project(vr, vc, grid)):
            u_ext[c] = opened[...] * moved
            u_now = u_ext[c, own, :]
            u_kept[t, c] = u_now
            for k in range(2):
                live = (facts[k : k + 1] == at).astype(F32)
                miss = u_now - t_own[k, c]
                misc[0] += sublanes(live * opened[own, :] * miss * miss)
        return carry

    lax.fori_loop(0, STEPS, forward_step, 0)

    def bar_block(xh, xh_at, t, base, size, c, h_bar):
        n = xh[xh_at, t, pl.ds(base, size), c, :].astype(F32)
        bend = jnp.tanh(n)
        moved = n * bend
        n_bar = h_bar * ((1.0 + bend) * ((1.0 + n) - moved))
        zbuf[pl.ds(base, size), c, :] = n_bar
        acc[0, c, :] += jnp.sum(n_bar, axis=0)
        acc[1, c, :] += jnp.sum(n_bar * n, axis=0)
        return n + moved

    def clear_sums():
        acc[...] = jnp.zeros_like(acc)

    def first_pass_last(t):
        clear_sums()

        def block(base, size):
            low = beside([frows[base + j].astype(BF) for j in range(size)])
            h_bar = nn_dot(headb[...], low)
            bars = jnp.stack([h_bar[:, j * LANES : (j + 1) * LANES] for j in range(size)], axis=0)
            lows = [
                bar_block(xh_full, 2, t, base, size, c, bars[:, c, :]).astype(BF)
                for c in channel_blocks()
            ]
            h = jnp.concatenate(lows, axis=1)
            ghead[...] += nt_dot(beside([h[j] for j in range(size)]), low)

        for_blocks(rows, BAR_LINES, block)

    def sums_start(layer):
        gain = norms[0, layer]
        sums = 0.5 * acc[0]
        cross = (acc[1] - norms[1, layer] * sums) / gain
        group_start(5 + layer, gain * sums, gain * cross)
        gnorm[0, layer] += cross
        gnorm[1, layer] += sums

    def second_pass(layer, t, count, xh, xh_at, dst, by):
        size_all = CH // GROUPS * count * LANES * parts
        total, total_cross = group_finish(5 + layer)
        inverse = inv_kept[t, layer]
        gain = norms[0, layer]
        slope = inverse * spread(total_cross / size_all) / gain
        coef[0] = 0.5 * gain * inverse
        coef[1] = -2.0 * slope
        coef[2] = norms[1, layer] * slope - inverse * spread(total / size_all)

        def z_bar(at, c):
            n = xh[xh_at, t, at, c, :].astype(F32)
            return (zbuf[at, c, :] * coef[0, c] + n * coef[1, c] + coef[2, c]).astype(BF)

        slot = 5 + layer
        for which, line in enumerate((0, count - 1)):
            edges[slot, which] = z_bar(line, slice(0, CH))
        args = (
            slot,
            edges.at[slot, 0],
            edges.at[slot, 1],
            g_halo.at[layer, 0],
            g_halo.at[layer, 1],
        )
        halo_start(*args)

        def block(base, size):
            at = pl.ds(base + 1, size)
            for c in channel_blocks():
                z = z_bar(pl.ds(base, size), c)
                if by:
                    put_shifted(dst, at, c, z, by, BACKWARD)
                else:
                    dst[at, slice(CH + c.start, CH + c.stop), :] = z

        for_blocks(count, ACT_LINES, block)
        halo_wait(*args)
        if by:
            spread_halo(dst, (g_halo[layer, 0], g_halo[layer, 1]), count, by, BACKWARD)
        else:
            dst[0, CH : 2 * CH, :] = g_halo[layer, 0]
            dst[count + 1, CH : 2 * CH, :] = g_halo[layer, 1]

    def bar_rows(weight, g, size):
        y = nn_dot(weight, g)
        return [
            tap_rows(y, j + 2, 0) + tap_rows(y, j + 1, 1) + tap_rows(y, j, 2) for j in range(size)
        ]

    def bars_of(layer, count, src, then):
        clear_sums()

        def block(base, size):
            g = beside([src[base + j] for j in range(size + 2)])
            then(base, size, jnp.stack(bar_rows(wb[layer], g, size), axis=0))

        for_blocks(count, BAR_LINES, block)

    def weight_sums(at, t, count, src, kept):
        def block(base, size):
            g = beside([src[base + 1 + j] for j in range(size)])
            h = beside([kept[t, pl.ds(base + j, 3)].reshape(3 * CH, LANES) for j in range(size)])
            gw[line_at[at] : line_at[at] + 3 * CH, :] += nt_dot(g, h)

        for_blocks(count, SUM_LINES, block)

    def bars_last(t):
        clear_sums()

        def block(base, size):
            g = beside([sg[base + j] for j in range(size + 2)])
            for j, bar in enumerate(bar_rows(wb[4], g, size)):
                skip_bar[base + j] = bar
            ups = bar_rows(wb[3], g, size)
            low = base // 2
            bars = jnp.stack(
                [pair_sum(ups[2 * j] + ups[2 * j + 1]) for j in range(size // 2)], axis=0
            )
            for c in channel_blocks():
                bar_block(xh_half, 1, t, low, size // 2, c, bars[:, c, :])

        for_blocks(rows, BAR_LINES, block)

    def weight_sums_last(t):
        def block(base, size):
            g = beside([sg[base + 1 + j] for j in range(size)])
            low = base // 2
            h = beside([skip[t, pl.ds(base + j, 3)].reshape(3 * CH, LANES) for j in range(size)])
            gw[line_at[4] : line_at[4] + 3 * CH, :] += nt_dot(g, h)
            up = beside(
                [
                    jnp.concatenate([h4[t, low + (j + ky - 1) // 2 + 1] for ky in range(3)], axis=0)
                    for j in range(size)
                ]
            )
            gw[line_at[3] : line_at[3] + 3 * CH, :] += nt_dot(g, up)

        for_blocks(rows, SUM_LINES, block)

    def taps_first():
        def block(base, size):
            g = beside([sg[base + j, CH : 2 * CH, :] for j in range(size)])
            y = nn_dot(w0b[...], g)
            for j in range(size):
                taps[base + j] = y[:, j * LANES : (j + 1) * LANES]

        for_blocks(rows, SUM_LINES, block)
        g = beside([sg[rows + j, CH : 2 * CH, :] for j in range(2)])
        y = nn_dot(w0b[...], g)
        for j in range(2):
            taps[rows + j] = y[:, j * LANES : (j + 1) * LANES]

    def weight_sums_first(t):
        def weights(base, size):
            g = beside([sg[base + 1 + j, CH : 2 * CH, :] for j in range(size)])
            x = beside(
                [s0b[t, pl.ds(base + EDGE - 1 + j, 3)].reshape(48, LANES) for j in range(size)]
            )
            gw0[...] += nt_dot(g, x)

        for_blocks(rows, SUM_LINES, weights)

    def chunk_at(p, which):
        return pl.ds(pl.multiple_of(starts[p] + which * chunks[p], 16), chunks[p])

    def strip(p):
        return pl.ds(offsets[p], chunks[p])

    def exchange_start(copies, count, *args):
        def start(d, carry):
            src, dst, sent, landed, peer = copies(d, *args)[0]
            pltpu.make_async_remote_copy(
                src_ref=src,
                dst_ref=dst,
                send_sem=sent,
                recv_sem=landed,
                device_id=peer,
                device_id_type=MESH,
            ).start()
            return carry

        lax.fori_loop(1, count, start, 0)

    def exchange_finish(copies, count, *args):
        def finish(d, carry):
            (src, _, sent, _, _), (dst, landed) = copies(d, *args)
            pltpu.make_async_copy(src, src, sent).wait()
            pltpu.make_async_copy(dst, dst, landed).wait()
            return carry

        lax.fori_loop(1, count, finish, 0)

    def around(d, here, count):
        return lax.rem(here + d, count), lax.rem(here + count - d, count)

    def chunk_plane(d, p):
        other, source = around(d, mine, members)
        send = (g_send.at[chunk_at(p, other)], p_recv.at[mine, strip(p)])
        sems = (p_ss.at[p, d], p_rs.at[p, mine], plane_id(d))
        return send + sems, (p_recv.at[source, strip(p)], p_rs.at[p, source])

    def chunk_line(d, p):
        other, source = around(d, level, planes)
        block = z_recv.at[level, strip(p)]
        sems = (z_ss.at[p, d], z_rs.at[p, level], line_id(d))
        return (block, block) + sems, (z_recv.at[source, strip(p)], z_rs.at[p, source])

    def chunk_back(d, p):
        other, source = around(d, mine, members)
        block = g_all.at[chunk_at(p, mine)]
        sems = (p_ss.at[3 + p, d], p_rs.at[3 + p, mine], plane_id(d))
        return (block, block) + sems, (g_all.at[chunk_at(p, source)], p_rs.at[3 + p, source])

    def small_plane(d):
        other, source = around(d, mine, members)
        block = m_plane.at[mine]
        sems = (p_ss.at[6, d], p_rs.at[6, mine], plane_id(d))
        return (block, block) + sems, (m_plane.at[source], p_rs.at[6, source])

    def small_line(d):
        other, source = around(d, level, planes)
        block = m_line.at[level]
        sems = (z_ss.at[3, d], z_rs.at[3, level], line_id(d))
        return (block, block) + sems, (m_line.at[source], z_rs.at[3, source])

    def plane_start(p):
        at = slice(starts[p], starts[p] + chunks[p] * members)
        if p == 1:
            gw[at, :] = 0.5 * gw[at, :]
        g_send[at, :] = gw[at, :].astype(BF)
        exchange_start(chunk_plane, members, p)

    def plane_finish(p):
        exchange_finish(chunk_plane, members, p)

        def add(d, total):
            return total + p_recv[lax.rem(mine + d, members), strip(p), :].astype(F32)

        total = lax.fori_loop(1, members, add, gw[chunk_at(p, mine), :])
        z_recv[level, strip(p), :] = total.astype(BF)
        exchange_start(chunk_line, planes, p)

    def line_finish(p):
        exchange_finish(chunk_line, planes, p)

        def add(k, total):
            return total + z_recv[k, strip(p), :].astype(F32)

        total = lax.fori_loop(0, planes, add, jnp.zeros((chunks[p], 3 * CH), F32))
        g_all[chunk_at(p, mine), :] = total.astype(BF)
        exchange_start(chunk_back, members, p)

    def gather_finish(p):
        exchange_finish(chunk_back, members, p)

    def at_last(t, what, p):
        @pl.when(t == 0)
        def _():
            what(p)

    def w_args():
        return (
            12,
            w_ext.at[:, pl.ds(EDGE, EDGE), :],
            w_ext.at[:, pl.ds(rows, EDGE), :],
            w_ext.at[:, pl.ds(0, EDGE), :],
            w_ext.at[:, pl.ds(rows + EDGE, EDGE), :],
        )

    def pull_start(t):
        facts = m_own[0]
        at = (t + 1).astype(F32)
        open_own = opened[own, :]
        for c in range(2):
            pull = jnp.zeros((rows, LANES), F32)
            for k in range(2):
                live = (facts[k : k + 1] == at).astype(F32)
                pull = pull + live * (u_kept[t, c] - t_own[k, c])
            w_ext[c, own, :] = open_own * (u_bar[c] + 2.0 * open_own * pull)
        halo_start(*w_args())

    def backward_step(i, carry):
        t = STEPS - 1 - i
        halo_wait(*w_args())
        grid = grid_mask[...]
        gr, gc = project(w_ext[0], w_ext[1], grid)
        gr, gc = grid * gr, grid * gc
        qr, qc = q_ext[t, 0], q_ext[t, 1]
        bar_r = gr + DT_ADV * (
            drows(gr * qr) + dcols(gr * qc) - (gr * drows(qr) + gc * drows(qc))
        )
        bar_c = gc + DT_ADV * (
            drows(gc * qr) + dcols(gc * qc) - (gr * dcols(qr) + gc * dcols(qc))
        )
        for c, bar in enumerate((bar_r, bar_c)):
            passed = opened[...] * bar
            q_ext[t, c] = passed
            passed = q_ext[t, c, own, :]
            u_bar[c] = passed
            force_bar = DT_FORCE * passed
            misc[2 + c] += sublanes(force_bar)
            frows[:, c, :] = force_bar
        for c in range(2, 16):
            frows[:, c, :] = jnp.zeros((rows, LANES), F32)

        first_pass_last(t)
        sums_start(4)
        second_pass(4, t, rows, xh_full, 2, sg, 1)
        bars_last(t)
        sums_start(3)
        weight_sums_last(t)
        at_last(t, plane_start, 2)
        second_pass(3, t, half, xh_half, 1, sgh, 2)

        def into_two(base, size, bars):
            for c in channel_blocks():
                bar_block(xh_half, 0, t, base, size, c, bars[:, c, :])

        bars_of(2, half, sgh, into_two)
        sums_start(2)
        weight_sums(2, t, half, sgh, h3)
        second_pass(2, t, half, xh_half, 0, sgh, 2)

        def into_one(base, size, bars):
            at = 2 * base
            for c in channel_blocks():
                direct = skip_bar[pl.ds(at, 2 * size), c, :].reshape(size, 2, 16, LANES)
                total = (direct + 0.25 * bars[:, None, c, :]).reshape(2 * size, 16, LANES)
                bar_block(xh_full, 1, t, at, 2 * size, c, total)

        bars_of(1, half, sgh, into_one)
        sums_start(1)
        weight_sums(1, t, half, sgh, pooled)
        at_last(t, plane_finish, 2)
        at_last(t, plane_start, 1)
        second_pass(1, t, rows, xh_full, 1, sg, 1)

        def into_zero(base, size, bars):
            for c in channel_blocks():
                bar_block(xh_full, 0, t, base, size, c, bars[:, c, :])

        bars_of(0, rows, sg, into_zero)
        sums_start(0)
        weight_sums(0, t, rows, sg, h1)
        at_last(t, plane_start, 0)
        second_pass(0, t, rows, xh_full, 0, sg, 0)

        @pl.when(t > 0)
        def _():
            taps_first()
            for c in range(2):
                columns = []
                for kx in range(3):
                    total = jnp.zeros((rows, LANES), F32)
                    for ky in range(3):
                        total = total + taps[pl.ds(2 - ky, rows), 16 * ky + 3 * kx + c, :]
                    columns.append(total)
                u_bar[c] += from_right(columns[0], 1) + columns[1] + from_left(columns[2], 1)
            pull_start(t - 1)

        at_last(t, plane_finish, 1)
        weight_sums_first(t)
        at_last(t, line_finish, 2)
        return carry

    pull_start(jnp.int32(STEPS - 1))
    lax.fori_loop(0, STEPS, backward_step, 0)

    lane = lane_of((CH, CH))
    small_sums = jnp.concatenate([gw0[...], jnp.zeros((CH, CH - 48), F32)], axis=1)
    for which in range(2):
        for layer in range(LAYERS + 1):
            column = jnp.sum(gnorm[which, layer], axis=1, keepdims=True)
            if layer in HALF_SLOT:
                column = 0.5 * column
            small_sums = jnp.where(lane == 48 + 5 * which + layer, column, small_sums)
    for c in range(2):
        small_sums = jnp.where(lane == 58 + c, ghead[:, c : c + 1], small_sums)
    m_plane[mine] = jnp.concatenate(
        [jnp.sum(misc[k], axis=0, keepdims=True) for k in range(4)]
        + [jnp.zeros((4, LANES), F32), beside([small_sums[: CH // 2], small_sums[CH // 2 :]])],
        axis=0,
    )
    exchange_start(small_plane, members)
    plane_finish(0)
    line_finish(1)
    exchange_finish(small_plane, members)
    no_sums = jnp.zeros(m_line.shape[1:], F32)
    m_line[level] = lax.fori_loop(0, members, lambda k, total: total + m_plane[k], no_sums)
    exchange_start(small_line, planes)
    line_finish(0)
    exchange_finish(small_line, planes)
    for p in (2, 1, 0):
        gather_finish(p)

    totals = lax.fori_loop(0, planes, lambda k, total: total + m_line[k], no_sums)
    small_out[...] = totals[8:]
    small_square = jnp.sum(sublanes(totals[8:] * totals[8:]), axis=0, keepdims=True)
    small_square = jnp.sum(small_square, axis=1, keepdims=True)
    totals = jnp.broadcast_to(jnp.sum(totals[:8], axis=1, keepdims=True), (8, LANES))

    def squares(i, total):
        at = pl.ds(pl.multiple_of(i * 64, 64), 64)
        block = g_all[at, :].astype(F32)
        return total + jnp.sum((block * block).reshape(8, 8, 3 * CH), axis=0)

    square = lax.fori_loop(0, all_lines // 64, squares, jnp.zeros((8, 3 * CH), F32))
    square = jnp.sum(jnp.sum(square, axis=0, keepdims=True), axis=1, keepdims=True)
    count = totals[1:2]
    raw = square + small_square + totals[2:3] * totals[2:3] + totals[3:4] * totals[3:4]
    norm = jnp.sqrt(raw) / count
    factor = jnp.minimum(1.0, CLIP_NORM / norm) / count
    scalars[...] = jnp.concatenate([totals[:4], norm, factor, totals[6:]], axis=0)


def train(keyframes, boxes, velocity, targets, w_in, w_mid, norm_params, head_params):
    ranks = lax.axis_size("rows")
    planes = lax.axis_size("batch") // 2
    members = 2 * ranks
    starts, chunks, line_at, lines = gradient_lines(members)
    parts = ranks // 2
    tile = velocity.shape[2]
    rows, half, ext = 2 * tile, tile, 2 * tile + 2 * EDGE
    vmem = pl.BlockSpec(memory_space=pltpu.VMEM)

    def kept(count):
        return pltpu.VMEM((STEPS, count + 2, CH, LANES), BF)

    smem = pl.BlockSpec(memory_space=pltpu.SMEM)
    args = (keyframes, boxes, velocity, targets, w_in, w_mid, norm_params, head_params)
    return pl.pallas_call(
        functools.partial(train_kernel, ranks, planes),
        out_shape=(
            jax.ShapeDtypeStruct((lines, 3 * CH), BF),
            jax.ShapeDtypeStruct((CH // 2, LANES), F32),
            jax.ShapeDtypeStruct((8, LANES), F32),
        ),
        in_specs=[smem] * 2 + [vmem] * 6,
        out_specs=(vmem,) * 3,
        scratch_shapes=[
            pltpu.VMEM((2, 16, LANES), F32),
            pltpu.VMEM((LAYERS + 1, 3 * CH, 3 * CH), BF),
            pltpu.VMEM((LAYERS + 1, 3 * CH, 3 * CH), BF),
            pltpu.VMEM((CH, 48), BF),
            pltpu.VMEM((48, CH), BF),
            pltpu.VMEM((2, LAYERS + 1, CH, LANES), F32),
            pltpu.VMEM((16, CH), BF),
            pltpu.VMEM((CH, 16), BF),
            pltpu.VMEM((2, 1, LANES), F32),
            pltpu.VMEM((3, CH // 2, 8, LANES), F32),
            pltpu.VMEM((2, 3 * (LAYERS + 1), CH, LANES), F32),
            pltpu.VMEM((LANES, LANES), F32),
            pltpu.VMEM((lines, 3 * CH), F32),
            pltpu.VMEM((CH, 48), F32),
            pltpu.VMEM((2, LAYERS + 1, CH, LANES), F32),
            pltpu.VMEM((CH, 16), F32),
            pltpu.VMEM((4, 8, LANES), F32),
            pltpu.VMEM((2, ext, LANES), F32),
            pltpu.VMEM((2, 2, rows, LANES), F32),
            pltpu.VMEM((2, 16, LANES), F32),
            pltpu.VMEM((ext, LANES), F32),
            pltpu.VMEM((ext, LANES), F32),
            pltpu.VMEM((ext, 16, LANES), F32),
            pltpu.VMEM((STEPS, ext, 16, LANES), BF),
            pltpu.VMEM((STEPS, 2, ext, LANES), F32),
            pltpu.VMEM((STEPS, 2, rows, LANES), F32),
            pltpu.VMEM((2, ext, LANES), F32),
            pltpu.VMEM((2, rows, LANES), F32),
            pltpu.VMEM((rows, 16, LANES), F32),
            pltpu.VMEM((rows + 2, 48, LANES), F32),
            kept(rows),
            kept(rows),
            kept(half),
            kept(half),
            kept(half),
            pltpu.VMEM((3, STEPS, rows, CH, LANES), BF),
            pltpu.VMEM((2, STEPS, half, CH, LANES), BF),
            pltpu.VMEM((STEPS, LAYERS + 1, CH, LANES), F32),
            pltpu.VMEM((rows, CH, LANES), F32),
            pltpu.VMEM((rows, CH, LANES), F32),
            pltpu.VMEM((rows + 2, 3 * CH, LANES), BF),
            pltpu.VMEM((half + 2, 3 * CH, LANES), BF),
            pltpu.VMEM((10, 2, CH, LANES), BF),
            pltpu.VMEM((LAYERS + 1, 2, CH, LANES), BF),
            pltpu.VMEM((2 * LANES, 3 * LANES), BF),
            pltpu.VMEM((3, CH, LANES), F32),
            pltpu.VMEM((2, CH, LANES), F32),
            pltpu.VMEM((10, 16, LANES), F32),
            pltpu.VMEM((10, parts - 1, 16, LANES), F32),
            pltpu.VMEM((lines, 3 * CH), BF),
            pltpu.VMEM((members, sum(chunks), 3 * CH), BF),
            pltpu.VMEM((planes, sum(chunks), 3 * CH), BF),
            pltpu.VMEM((members, 8 + CH // 2, LANES), F32),
            pltpu.VMEM((planes, 8 + CH // 2, LANES), F32),
            pltpu.SemaphoreType.DMA((2, 3)),
            pltpu.SemaphoreType.DMA((2, 3)),
            pltpu.SemaphoreType.DMA((3,)),
            pltpu.SemaphoreType.DMA((13, 2)),
            pltpu.SemaphoreType.DMA((13, 2)),
            pltpu.SemaphoreType.DMA((10, parts - 1)),
            pltpu.SemaphoreType.DMA((10, parts - 1)),
            pltpu.SemaphoreType.DMA((7, members)),
            pltpu.SemaphoreType.DMA((7, members)),
            pltpu.SemaphoreType.DMA((4, planes)),
            pltpu.SemaphoreType.DMA((4, planes)),
        ],
        compiler_params=pltpu.CompilerParams(
            collective_id=0, has_side_effects=True, vmem_limit_bytes=60 * 2**20
        ),
        name="train",
    )(*args)


def adam_kernel(line_at, g_all, small, scalars, *refs):
    olds = [refs[3 * k : 3 * k + 3] for k in range(4)]
    news = [refs[12 + 3 * k : 15 + 3 * k] for k in range(4)]
    low_in, low_mid, low_head, loss, cells, norm, wide, turned, lines = refs[24:]
    factor = scalars[5, 0]
    at_step = pl.program_id(0)

    def update(which, at, g, low=None):
        weight, moment, second = (ref[at] for ref in olds[which])
        moment = BETA_ONE * moment + (1 - BETA_ONE) * g
        second = BETA_TWO * second + (1 - BETA_TWO) * g * g
        mhat = moment / (1 - BETA_ONE**STEP_NUM)
        vhat = second / (1 - BETA_TWO**STEP_NUM)
        change = mhat / (jnp.sqrt(vhat) + ADAM_EPS) + DECAY * weight
        weight = weight - RATES[which] * change
        for ref, value in zip(news[which], (weight, moment, second)):
            ref[at] = value
        if low is not None:
            low[at] = weight.astype(BF)

    @pl.when(at_step == 0)
    def _():
        loss[0, 0] = scalars[0, 0]
        cells[0, 0] = scalars[1, 0]
        norm[0, 0] = scalars[4, 0]
        for k in range(LAYERS + 1):
            at = pl.ds(line_at[k], 3 * CH)
            to = pl.ds(k * 3 * CH, 3 * CH)
            wide[0, to, :] = g_all[at, :LANES].astype(F32) * factor
            tail = g_all[at, LANES:].astype(F32) * factor
            wide[1, to, :] = jnp.concatenate([tail, jnp.zeros_like(tail)], axis=1)
        rest = small[...] * factor
        rest = jnp.concatenate([rest, pltpu.roll(rest, CH, 1), jnp.zeros((CH, LANES), F32)], axis=0)
        turned[...] = rest.T
        for ch in range(3):
            for ky in range(3):
                g = turned[pl.ds(16 * ky + ch, 3, 3), :]
                update(0, (ch, ky), g[:, :CH], low_in)
        for layer in range(LAYERS + 1):
            g = turned[pl.ds(48 + layer, 2, LAYERS + 1), :]
            update(2, (layer,), g[:, :CH])
        line_is = lax.broadcasted_iota(jnp.int32, (2, LANES), 0)
        bias = jnp.where(line_is == 0, scalars[2, 0] * factor, scalars[3, 0] * factor)
        g = jnp.where(lane_of((2, LANES)) < CH, turned[58:60, :], bias)
        update(3, (slice(None),), g[:, : CH + 1], low_head)

    low_lanes = lane_of((CH // 2, LANES)) < CH
    for ky in range(3):

        @pl.when(at_step == ky)
        def _():
            for k in range(LAYERS + 1):
                for kx in range(3):
                    base = k * 3 * CH + kx * CH
                    even = wide[ky // 2, pl.ds(base, CH // 2, 2), :]
                    odd = wide[ky // 2, pl.ds(base + 1, CH // 2, 2), :]
                    if ky % 2:
                        even = pltpu.roll(even, CH, 1)
                    else:
                        odd = pltpu.roll(odd, CH, 1)
                    lines[kx, :, k, :] = jnp.where(low_lanes, even, odd)

    for kx in range(3):
        g = jnp.concatenate(
            [lines[kx, a, : LAYERS + 1, :] for a in range(CH // 2)], axis=1
        )
        update(1, (kx,), g, low_mid)


def adam(g_all, small, scalars, params, moments, seconds):
    line_at = gradient_lines(2 * lax.axis_size("rows"))[2]
    smem = pl.BlockSpec(memory_space=pltpu.SMEM)
    shapes = [w.shape for w in params]
    whole = lambda shape: pl.BlockSpec(shape, lambda i: (0,) * len(shape))
    mid = pl.BlockSpec((3,) + shapes[1][1:], lambda i: (i, 0, 0))
    spec = lambda k: mid if k == 1 else whole(shapes[k])
    states = [x for group in zip(params, moments, seconds) for x in group]
    lows = (0, 1, 3)
    return pl.pallas_call(
        functools.partial(adam_kernel, line_at),
        grid=(3,),
        out_shape=tuple(jax.ShapeDtypeStruct(x.shape, F32) for x in states)
        + tuple(jax.ShapeDtypeStruct(shapes[k], BF) for k in lows)
        + (jax.ShapeDtypeStruct((1, 1), F32),) * 3,
        in_specs=[whole(g_all.shape), whole(small.shape), smem] + [spec(k // 3) for k in range(12)],
        out_specs=tuple(spec(k // 3) for k in range(12))
        + tuple(spec(k) for k in lows)
        + (smem,) * 3,
        scratch_shapes=[
            pltpu.VMEM((2, (LAYERS + 1) * 3 * CH, LANES), F32),
            pltpu.VMEM((LANES, LANES), F32),
            pltpu.VMEM((3, CH // 2, 8, LANES), F32),
        ],
        compiler_params=pltpu.CompilerParams(vmem_limit_bytes=60 * 2**20),
        name="adam",
    )(g_all, small, scalars, *states)


def in_order(group):
    first, mid, norm, head = group
    return (
        jnp.transpose(first, (1, 2, 3, 0)),
        jnp.transpose(mid, (1, 0, 2)),
        jnp.transpose(norm, (1, 0, 2)),
        head,
    )


def out_of_order(group):
    first, mid, norm, head = group
    return (
        jnp.transpose(first, (3, 0, 1, 2)),
        jnp.transpose(mid, (1, 0, 2)),
        jnp.transpose(norm, (1, 0, 2)),
        head,
    )


def shards(
    velocity,
    targets,
    keyframes,
    boxes,
    w_in,
    w_mid,
    norm_params,
    head_params,
    m_in,
    m_mid,
    m_norm,
    m_head,
    v_in,
    v_mid,
    v_norm,
    v_head,
):
    params = in_order((w_in, w_mid, norm_params, head_params))
    moments = in_order((m_in, m_mid, m_norm, m_head))
    seconds = in_order((v_in, v_mid, v_norm, v_head))
    g_all, small, scalars = train(keyframes, boxes, velocity, targets, *params)
    result = adam(g_all, small, scalars, params, moments, seconds)
    new_w, new_m, new_v = (out_of_order(result[k:12:3]) for k in range(3))
    low_in, low_mid, low_head, loss, cells, norm = result[12:]
    return (
        *new_w,
        *new_m,
        *new_v,
        jnp.transpose(low_in, (3, 0, 1, 2)),
        jnp.transpose(low_mid, (1, 0, 2)),
        low_head,
        loss.reshape(()),
        cells.reshape(()),
        norm.reshape(()),
    )


def solution(mesh):
    return jax.shard_map(
        shards,
        mesh=mesh,
        in_specs=(
            P("batch", None, "rows", None),
            P("batch", None, None, "rows", None),
            P("batch", None),
            P("batch", None, None),
        )
        + (P(),) * 12,
        out_specs=(P(),) * 18,
        check_vma=False,
    )
```

```python
import functools

import jax
import jax.numpy as jnp
from jax import lax
from jax.experimental import pallas as pl
from jax.experimental.pallas import tpu as pltpu
from jax.sharding import PartitionSpec as P

CH = 64
GROUPS = 8
LAYERS = 4
STEPS = 4
JACOBI = 4
STEP_NUM = 10
LANES = 128
EDGE = 8

EPS_NORM = 1e-05
DT_FORCE = 0.5
DT_ADV = 0.2
CLIP_NORM = 0.001
BETA_ONE = 0.9
BETA_TWO = 0.95
ADAM_EPS = 1e-08
DECAY = 0.01
RATES = (0.2, 0.05, 1.0, 0.15)

BF = jnp.bfloat16
F32 = jnp.float32
MESH = pl.DeviceIdType.MESH
FULL_SLOT = {0: 0, 1: 1, 4: 2}
HALF_SLOT = {2: 0, 3: 1}
ACT_LINES = 64
CONV_LINES = 64
BAR_LINES = 32
SUM_LINES = 64


def nt_dot(a, b):
    return lax.dot_general(a, b, (((1,), (1,)), ((), ())), preferred_element_type=F32)


def nn_dot(a, b):
    return jnp.dot(a, b, preferred_element_type=F32)


def beside(rows):
    return jnp.concatenate(rows, axis=1)


def lane_of(shape):
    return lax.broadcasted_iota(jnp.int32, shape, len(shape) - 1)


def from_left(x, by):
    return jnp.where(lane_of(x.shape) < by, jnp.zeros((), x.dtype), pltpu.roll(x, by, x.ndim - 1))


def from_right(x, by):
    moved = pltpu.roll(x, LANES - by, x.ndim - 1)
    return jnp.where(lane_of(x.shape) >= LANES - by, jnp.zeros((), x.dtype), moved)


def pair_sum(x):
    even = lane_of(x.shape) % 2 == 0
    last = x.ndim - 1
    return x + jnp.where(even, pltpu.roll(x, LANES - 1, last), pltpu.roll(x, 1, last))


def drows(x):
    count = x.shape[0]
    return 0.5 * (pltpu.roll(x, count - 1, 0) - pltpu.roll(x, 1, 0))


def dcols(x):
    return 0.5 * (from_right(x, 1) - from_left(x, 1))


def nsum(x):
    count = x.shape[0]
    return (
        pltpu.roll(x, count - 1, 0) + pltpu.roll(x, 1, 0) + from_right(x, 1) + from_left(x, 1)
    )


def project(vr, vc, grid):
    div = grid * (drows(vr) + dcols(vc))
    press = -0.25 * div
    for sweep in range(JACOBI - 1):
        press = grid * (0.25 * (nsum(press) - div))
    return vr - drows(press), vc - dcols(press)


def sublanes(x):
    return jnp.sum(x.reshape(x.shape[0] // 8, 8, LANES), axis=0)


def group_rows(x):
    return jnp.sum(x.reshape(GROUPS, CH // GROUPS, LANES), axis=1)


def spread(x):
    return jnp.concatenate(
        [jnp.broadcast_to(x[g : g + 1], (CH // GROUPS, LANES)) for g in range(GROUPS)], axis=0
    )


def gradient_lines(members):
    groups = ((0,), (1, 2), (3, 4))
    chunks, starts, at = [], [], []
    start = 0
    for group in groups:
        place = start
        for layer in group:
            at.append(place)
            place += 3 * CH
        chunk = -(-(place - start) // (16 * members)) * 16
        starts.append(start)
        chunks.append(chunk)
        start += chunk * members
    return starts, chunks, at, start


def train_kernel(
    ranks,
    planes,
    keys,
    boxes,
    vel,
    tgt,
    w_in,
    w_mid,
    norm_params,
    head,
    g_all,
    small_out,
    scalars,
    meta,
    wf,
    wb,
    w0f,
    w0b,
    norms,
    headf,
    headb,
    bias,
    lines,
    wide,
    small,
    gw,
    gw0,
    gnorm,
    ghead,
    misc,
    u_ext,
    t_own,
    m_own,
    opened,
    grid_mask,
    s0,
    s0b,
    q_ext,
    u_kept,
    q_edge,
    f_edge,
    w_ext,
    u_bar,
    frows,
    taps,
    h1,
    skip,
    pooled,
    h3,
    h4,
    xh_full,
    xh_half,
    inv_kept,
    zbuf,
    skip_bar,
    sg,
    sgh,
    edges,
    g_halo,
    pool_mat,
    coef,
    acc,
    st_send,
    st_recv,
    g_send,
    p_recv,
    z_recv,
    m_plane,
    m_line,
    in_send,
    in_recv,
    in_local,
    halo_send,
    halo_recv,
    st_ss,
    st_rs,
    p_ss,
    p_rs,
    z_ss,
    z_rs,
):
    quarter = ranks // 4
    parts = ranks // 2
    tile = vel.shape[2]
    rows = 2 * tile
    half = rows // 2
    batch_at = lax.axis_index("batch")
    row_at = lax.axis_index("rows")
    core = lax.rem(batch_at, 2)
    plane = batch_at - core
    sample = row_at // quarter
    part = 2 * lax.rem(row_at, quarter) + core

    def owner(which, piece):
        return (plane + lax.rem(piece, 2), which * quarter + piece // 2)

    u_ext[...] = jnp.zeros_like(u_ext)
    q_ext[...] = jnp.zeros_like(q_ext)
    w_ext[...] = jnp.zeros_like(w_ext)
    g_halo[...] = jnp.zeros_like(g_halo)
    for count, shifted in ((rows, sg), (half, sgh)):
        for at in (0, count + 1):
            shifted[at] = jnp.zeros((3 * CH, LANES), BF)
    for kept, count in ((h1, rows), (skip, rows), (pooled, half), (h3, half), (h4, half)):
        for t in range(STEPS):
            kept[t, 0] = jnp.zeros((CH, LANES), BF)
            kept[t, count + 1] = jnp.zeros((CH, LANES), BF)

    barrier = pltpu.get_barrier_semaphore()
    members = 2 * ranks
    starts, chunks, line_at, all_lines = gradient_lines(members)
    offsets = [sum(chunks[:k]) for k in range(3)]
    mine = core * ranks + row_at

    def plane_id(d):
        other = lax.rem(mine + d, members)
        return (plane + other // ranks, lax.rem(other, ranks))

    def greet(d, carry):
        pl.semaphore_signal(barrier, inc=1, device_id=plane_id(d), device_id_type=MESH)
        return carry

    lax.fori_loop(1, members, greet, 0)
    level = batch_at // 2

    def line_id(d):
        return (2 * lax.rem(level + d, planes) + core, row_at)

    def greet_line(d, carry):
        pl.semaphore_signal(barrier, inc=1, device_id=line_id(d), device_id_type=MESH)
        return carry

    lax.fori_loop(1, planes, greet_line, 0)

    line_is = lax.broadcasted_iota(jnp.int32, (16, LANES), 0)
    for j in range(2):
        values = [keys[j, k] for k in range(2)]
        values += [boxes[j, b, k] for b in range(2) for k in range(4)]
        facts = jnp.zeros((16, LANES), F32)
        for k, value in enumerate(values):
            facts = jnp.where(line_is == k, value.astype(F32), facts)
        meta[j] = facts

    low_lanes = lane_of((CH // 2, LANES)) < CH
    for ky in range(3):
        for kx in range(3):
            for a in range(CH // 2):
                lines[kx, a, : LAYERS + 1, :] = w_mid[3 * ky + kx, :, a * LANES : (a + 1) * LANES]
        for k in range(LAYERS + 1):
            left, mid, right = (lines[kx, :, k, :] for kx in range(3))
            slab = 3 * k + ky
            even, odd = pl.ds(0, CH // 2, 2), pl.ds(1, CH // 2, 2)
            wide[0, slab, even, :] = jnp.where(low_lanes, left, pltpu.roll(mid, CH, 1))
            wide[0, slab, odd, :] = jnp.where(low_lanes, pltpu.roll(left, CH, 1), mid)
            wide[1, slab, even, :] = right
            wide[1, slab, odd, :] = pltpu.roll(right, CH, 1)
    low_lanes = lane_of((CH, LANES)) < CH
    for k in range(LAYERS + 1):
        for ky in range(3):
            slab = 3 * k + ky
            at = slice(ky * CH, (ky + 1) * CH)
            first, last = wide[0, slab], wide[1, slab]
            wf[k, at, :] = jnp.concatenate([first, last[:, :CH]], axis=1).astype(BF)
            turned = jnp.concatenate([first, last], axis=0).T
            left, mid = turned[:CH], turned[CH:]
            first = jnp.where(low_lanes, left, pltpu.roll(mid, CH, 1))
            last = pltpu.roll(left, CH, 1)
            wb[k, at, :] = jnp.concatenate([first, last[:, :CH]], axis=1).astype(BF)
    pl.semaphore_wait(barrier, members + planes - 2)

    def incoming(place):
        at = pl.ds(pl.multiple_of(EDGE + place * tile, 8), tile)
        here = pl.ds(pl.multiple_of(place * tile, 8), tile)
        return u_ext.at[:, at, :], t_own.at[:, :, here, :], m_own.at[place]

    place = lax.rem(row_at, 2)
    for j, k in ((0, 0), (1, 0), (0, 2), (1, 2), (0, 1), (1, 1)):
        to_batch, to_row = owner(2 * core + j, row_at // 2)
        stays = (to_batch == batch_at) & (to_row == row_at)
        for src, dst in [((vel, tgt, meta)[k].at[j], incoming(place)[k])]:

            @pl.when(stays)
            def _():
                pltpu.make_async_copy(src, dst, in_local.at[k]).start()

            @pl.when(jnp.logical_not(stays))
            def _():
                pltpu.make_async_remote_copy(
                    src_ref=src,
                    dst_ref=dst,
                    send_sem=in_send.at[j, k],
                    recv_sem=in_recv.at[place, k],
                    device_id=(to_batch, to_row),
                    device_id_type=MESH,
                ).start()

    small[...] = jnp.zeros_like(small)
    for ch in range(3):
        for ky in range(3):
            taps_in = w_in[ch, ky]
            taps_in = jnp.concatenate([taps_in, jnp.zeros_like(taps_in)], axis=1)
            small[pl.ds(16 * ky + ch, 3, 3), :] = taps_in
    for layer in range(LAYERS + 1):
        pair = norm_params[layer]
        small[48 + 2 * layer : 50 + 2 * layer, :] = jnp.concatenate(
            [pair, jnp.zeros_like(pair)], axis=1
        )
    pair = head[:, :CH]
    small[64:66, :] = jnp.concatenate([pair, jnp.zeros_like(pair)], axis=1)
    w0b[...] = small[:48, :CH].astype(BF)
    headf[...] = small[64:80, :CH].astype(BF)
    turned = small[...].T[:CH]
    w0f[...] = turned[:, :48].astype(BF)
    headb[...] = turned[:, 64:80].astype(BF)
    for which in range(2):
        for layer in range(LAYERS + 1):
            at = 48 + 2 * layer + which
            norms[which, layer] = jnp.broadcast_to(turned[:, at : at + 1], (CH, LANES))
        bias[which] = jnp.broadcast_to(head[which : which + 1, CH : CH + 1], (1, LANES))

    def arrive(which):
        for i in range(2):
            from_batch = plane + sample // 2
            from_row = 2 * part + i
            stays = (from_batch == batch_at) & (from_row == row_at)
            for k, dst in enumerate(incoming(i)):
                if k not in which:
                    continue

                @pl.when(jnp.logical_not(stays))
                def _():
                    pltpu.make_async_copy(dst, dst, in_recv.at[i, k]).wait()

    def leave(which):
        for j in range(2):
            to_batch, to_row = owner(2 * core + j, row_at // 2)
            stays = (to_batch == batch_at) & (to_row == row_at)
            for k, src in enumerate((vel.at[j], tgt.at[j], meta.at[j])):
                if k not in which:
                    continue

                @pl.when(stays)
                def _():
                    pltpu.make_async_copy(src, src, in_local.at[k]).wait()

                @pl.when(jnp.logical_not(stays))
                def _():
                    pltpu.make_async_copy(src, src, in_send.at[j, k]).wait()

    leave((0, 2))
    arrive((0, 2))

    has_prev = part > 0
    has_next = part < parts - 1
    prev_id = owner(sample, jnp.maximum(part - 1, 0))
    next_id = owner(sample, jnp.minimum(part + 1, parts - 1))

    two = parts == 2
    near = 1 - part

    def halo_copy(slot, src, dst, side):
        return pltpu.make_async_remote_copy(
            src_ref=src(side),
            dst_ref=dst(1 - side),
            send_sem=halo_send.at[slot, side],
            recv_sem=halo_recv.at[slot, side],
            device_id=(prev_id, next_id)[side],
            device_id_type=MESH,
        )

    def only_copy(slot, src, dst):
        return pltpu.make_async_remote_copy(
            src_ref=src(near),
            dst_ref=dst(part),
            send_sem=halo_send.at[slot, 0],
            recv_sem=halo_recv.at[slot, 0],
            device_id=owner(sample, near),
            device_id_type=MESH,
        )

    def halo_start(slot, src, dst):
        if two:
            only_copy(slot, src, dst).start()
            return

        @pl.when(has_prev)
        def _():
            halo_copy(slot, src, dst, 0).start()

        @pl.when(has_next)
        def _():
            halo_copy(slot, src, dst, 1).start()

    def halo_wait(slot, src, dst):
        if two:
            only_copy(slot, src, dst).wait_send()
            landed = dst(near)
            pltpu.make_async_copy(landed, landed, halo_recv.at[slot, 0]).wait()
            return

        @pl.when(has_prev)
        def _():
            halo_copy(slot, src, dst, 0).wait_send()
            halo_copy(slot, src, dst, 1).wait_recv()

        @pl.when(has_next)
        def _():
            halo_copy(slot, src, dst, 1).wait_send()
            halo_copy(slot, src, dst, 0).wait_recv()

    def edge_lines(count):
        return [(0, near * count)] if two else [(0, 0), (1, count)]

    def edge_source(slot):
        return lambda side: edges.at[slot, 0 if two else side]

    def ext_args(slot, ref):
        def lines_at(start):
            return ref.at[:, pl.ds(pl.multiple_of(start, 8), EDGE), :]

        return (
            slot,
            lambda side: lines_at(EDGE + side * (rows - EDGE)),
            lambda side: lines_at(side * (rows + EDGE)),
        )

    def ext_halo(slot, ref):
        args = ext_args(slot, ref)
        halo_start(*args)
        halo_wait(*args)

    def group_copies(slot):
        return [
            pltpu.make_async_remote_copy(
                src_ref=st_send.at[slot],
                dst_ref=st_recv.at[slot, d - 1],
                send_sem=st_ss.at[slot, d - 1],
                recv_sem=st_rs.at[slot, d - 1],
                device_id=owner(sample, lax.rem(part + d, parts)),
                device_id_type=MESH,
            )
            for d in range(1, parts)
        ]

    def group_start(slot, first, second):
        st_send[slot] = jnp.concatenate([group_rows(first), group_rows(second)], axis=0)
        for copy in group_copies(slot):
            copy.start()

    def group_finish(slot):
        total = st_send[slot]
        for d, copy in enumerate(group_copies(slot)):
            copy.wait()
            total = total + st_recv[slot, d]
        total = jnp.broadcast_to(jnp.sum(total, axis=1, keepdims=True), total.shape)
        return total[:GROUPS], total[GROUPS:]

    ext = rows + 2 * EDGE
    row_is = lax.broadcasted_iota(jnp.int32, (ext, LANES), 0) - EDGE + part * rows
    inside_grid = ((row_is >= 0) & (row_is < parts * rows)).astype(F32)
    row_f = row_is.astype(F32)
    col_f = lane_of((ext, LANES)).astype(F32)
    covered = jnp.zeros((ext, LANES), F32)
    facts = m_own[0]
    for b in range(2):
        bounds = [facts[2 + 4 * b + k : 3 + 4 * b + k] for k in range(4)]
        inside = (
            (row_f >= bounds[0])
            & (row_f < bounds[1])
            & (col_f >= bounds[2])
            & (col_f < bounds[3])
        )
        covered = jnp.maximum(covered, inside.astype(F32))
    grid_mask[...] = inside_grid
    opened[...] = inside_grid * (1.0 - covered)
    own = pl.ds(EDGE, rows)
    misc[...] = jnp.zeros_like(misc)
    live_slots = (facts[0:1] > 0.5).astype(F32) + (facts[1:2] > 0.5).astype(F32)
    misc[1] = sublanes(opened[own, :] * live_slots)
    gw[...] = jnp.zeros_like(gw)
    gw0[...] = jnp.zeros_like(gw0)
    gnorm[...] = jnp.zeros_like(gnorm)
    ghead[...] = jnp.zeros_like(ghead)
    s0[...] = jnp.zeros_like(s0)
    frows[...] = jnp.zeros_like(frows)
    u_bar[...] = jnp.zeros_like(u_bar)

    ext_halo(10, u_ext)

    source = lax.broadcasted_iota(jnp.int32, pool_mat.shape, 0) % LANES
    target = lane_of(pool_mat.shape)
    column = target % LANES + 2 * (target // LANES - 1)
    pool_mat[...] = jnp.where(source // 2 == (column + 2) // 2 - 1, 0.25, 0.0).astype(BF)

    for kx in range(3):
        field = opened[...]
        s0[:, 3 * kx + 2, :] = (from_left(field, 1), field, from_right(field, 1))[kx]

    def put_shifted(dst, at, c, x, by, order):
        copies = (from_left(x, by), x, from_right(x, by))
        for place_at, which in enumerate(order):
            dst[at, slice(place_at * CH + c.start, place_at * CH + c.stop), :] = copies[which]

    FORWARD = (0, 1, 2)
    BACKWARD = (2, 1, 0)

    def halo_sides():
        return [near] if two else [0, 1]

    def spread_halo(dst, line_of, count, by, order):
        for side in halo_sides():
            put_shifted(dst, side * (count + 1), slice(0, CH), line_of(side), by, order)

    def for_blocks(count, size, body):
        size = min(size, count)
        if size == count:
            body(0, size)
            return

        def step(i, carry):
            body(pl.multiple_of(i * size, size), size)
            return carry

        lax.fori_loop(0, count // size, step, 0)

    def channel_blocks():
        return [slice(16 * c, 16 * c + 16) for c in range(CH // 16)]

    def make_norm(layer, t, sums, squares, count):
        group_start(layer, sums, squares)
        sums, squares = group_finish(layer)
        size = CH // GROUPS * count * LANES * parts
        mean = sums / size
        inverse = lax.rsqrt(squares / size - mean * mean + EPS_NORM)
        scale = spread(inverse)
        inv_kept[t, layer] = scale
        scale = 0.5 * scale * norms[0, layer]
        coef[0] = scale
        coef[1] = 0.5 * norms[1, layer] - spread(mean) * scale

    def activate(z, c):
        n = z * coef[0, c] + coef[1, c]
        return n, n * jnp.tanh(n) + n

    def conv_sums(count, size, rows_of):
        size = min(size, count)
        zero = jnp.zeros((CH, LANES), F32)

        def step(i, carry):
            sums, squares = carry
            base = i * size
            for j, z in enumerate(rows_of(base, size)):
                zbuf[base + j] = z
                sums = sums + z
                squares = squares + z * z
            return sums, squares

        if size == count:
            return step(0, (zero, zero))
        return lax.fori_loop(0, count // size, step, (zero, zero))

    def tap_rows(y, j, at):
        return y[at * CH : (at + 1) * CH, j * LANES : (j + 1) * LANES]

    def conv_of(src, layer):
        def rows_of(base, size):
            y = nn_dot(wf[layer], beside([src[base + j] for j in range(size + 2)]))
            return [
                tap_rows(y, j, 0) + tap_rows(y, j + 1, 1) + tap_rows(y, j + 2, 2)
                for j in range(size)
            ]

        return rows_of

    def conv_last(base, size):
        y = nn_dot(wf[4], beside([sg[base + j] for j in range(size + 2)]))
        low = base // 2
        x = nn_dot(wf[3], beside([sgh[low + j] for j in range(size // 2 + 2)]))
        result = []
        for j in range(size):
            z = tap_rows(y, j, 0) + tap_rows(y, j + 1, 1) + tap_rows(y, j + 2, 2)
            for ky in range(3):
                z = z + tap_rows(x, (j + ky - 1) // 2 + 1, ky)
            result.append(z)
        return result

    def finish_plain(t, layer, count, kept, xh, xh_at, dst, by, slot):
        for which, line in edge_lines(count - 1):
            edges[slot, which] = activate(zbuf[line], slice(0, CH))[1].astype(BF)
        args = (slot, edge_source(slot), lambda side: kept.at[t, side * (count + 1)])
        halo_start(*args)

        def block(base, size):
            at = pl.ds(base + 1, size)
            for c in channel_blocks():
                n, h = activate(zbuf[pl.ds(base, size), c, :], c)
                xh[xh_at, t, pl.ds(base, size), c, :] = n.astype(BF)
                low = h.astype(BF)
                kept[t, at, c, :] = low
                put_shifted(dst, at, c, low, by, FORWARD)

        for_blocks(count, ACT_LINES, block)
        halo_wait(*args)
        spread_halo(dst, lambda side: kept[t, side * (count + 1)], count, by, FORWARD)

    def pool_pairs(low, size):
        pairs = jnp.concatenate(
            [beside([low[2 * j], low[2 * j + 1]]) for j in range(size // 2)], axis=0
        )
        return nn_dot(pairs, pool_mat[...]).astype(BF).reshape(size // 2, CH, 3 * LANES)

    def finish_skip(t):
        for which, line in edge_lines(rows - 2):
            low = activate(zbuf[pl.ds(line, 2)], slice(0, CH))[1].astype(BF)
            edges[2, which] = pool_pairs(low, 2)[0, :, LANES : 2 * LANES]
            edges[1, which] = jnp.where(part == 0, low[1], low[0]) if two else low[which]
        skip_args = (1, edge_source(1), lambda side: skip.at[t, side * (rows + 1)])
        pool_args = (2, edge_source(2), lambda side: pooled.at[t, side * (half + 1)])
        halo_start(*pool_args)
        halo_start(*skip_args)

        def block(base, size):
            at = pl.ds(base + 1, size)
            lows = []
            for c in channel_blocks():
                n, h = activate(zbuf[pl.ds(base, size), c, :], c)
                xh_full[1, t, pl.ds(base, size), c, :] = n.astype(BF)
                low = h.astype(BF)
                skip[t, at, c, :] = low
                put_shifted(sg, at, c, low, 1, FORWARD)
                lows.append(low)
            small = pool_pairs(jnp.concatenate(lows, axis=1), size)
            at = pl.ds(base // 2 + 1, size // 2)
            pooled[t, at] = small[:, :, LANES : 2 * LANES]
            for k in range(3):
                sgh[at, k * CH : (k + 1) * CH, :] = small[:, :, k * LANES : (k + 1) * LANES]

        for_blocks(rows, ACT_LINES, block)
        halo_wait(*pool_args)
        halo_wait(*skip_args)
        spread_halo(sgh, lambda side: pooled[t, side * (half + 1)], half, 2, FORWARD)
        spread_halo(sg, lambda side: skip[t, side * (rows + 1)], rows, 1, FORWARD)

    def push_args(t):
        source, target = ext_args(11, q_ext.at[t])[1:]
        return (11, (lambda side: q_edge) if two else source, target)

    def finish_last(t):
        if two:
            line = pl.multiple_of(near * (rows - EDGE), EDGE)
            h = activate(zbuf[pl.ds(line, EDGE)], slice(0, CH))[1].astype(BF)
            force = nn_dot(headf[...], beside([h[j] for j in range(EDGE)]))
            for j in range(EDGE):
                f_edge[j] = force[:, j * LANES : (j + 1) * LANES]
            at = pl.ds(line + EDGE, EDGE)
            for c in range(2):
                force = f_edge[:, c, :] + bias[c]
                q_edge[c] = (u_ext[c, at, :] + DT_FORCE * force) * opened[at, :]
            halo_start(*push_args(t))

        def block(base, size):
            lows = []
            for c in channel_blocks():
                n, h = activate(zbuf[pl.ds(base, size), c, :], c)
                xh_full[2, t, pl.ds(base, size), c, :] = n.astype(BF)
                lows.append(h.astype(BF))
            low = jnp.concatenate(lows, axis=1)
            force = nn_dot(headf[...], beside([low[j] for j in range(size)]))
            for j in range(size):
                frows[base + j] = force[:, j * LANES : (j + 1) * LANES]

        for_blocks(rows, ACT_LINES, block)

    def forward_step(t, carry):
        for c in range(2):
            field = u_ext[c]
            for kx, moved in enumerate((from_left(field, 1), field, from_right(field, 1))):
                s0[:, 3 * kx + c, :] = moved
        s0b[t] = s0[...].astype(BF)

        def first_rows(base, size):
            x = beside(
                [s0b[t, pl.ds(base + EDGE - 1 + j, 3)].reshape(48, LANES) for j in range(size)]
            )
            z = nn_dot(w0f[...], x)
            return [z[:, j * LANES : (j + 1) * LANES] for j in range(size)]

        make_norm(0, t, *conv_sums(rows, CONV_LINES, first_rows), rows)
        finish_plain(t, 0, rows, h1, xh_full, 0, sg, 1, 0)
        make_norm(1, t, *conv_sums(rows, CONV_LINES, conv_of(sg, 0)), rows)
        finish_skip(t)
        make_norm(2, t, *conv_sums(half, CONV_LINES, conv_of(sgh, 1)), half)
        finish_plain(t, 2, half, h3, xh_half, 0, sgh, 2, 3)
        make_norm(3, t, *conv_sums(half, CONV_LINES, conv_of(sgh, 2)), half)
        finish_plain(t, 3, half, h4, xh_half, 1, sgh, 1, 4)
        make_norm(4, t, *conv_sums(rows, CONV_LINES, conv_last), rows)
        finish_last(t)

        for c in range(2):
            force = frows[:, c, :] + bias[c]
            q_ext[t, c, own, :] = (u_ext[c, own, :] + DT_FORCE * force) * opened[own, :]
        if not two:
            halo_start(*push_args(t))
        halo_wait(*push_args(t))

        @pl.when(t == 0)
        def _():
            leave((1,))
            arrive((1,))

        qr, qc = q_ext[t, 0], q_ext[t, 1]
        grid = grid_mask[...]
        vr = grid * (qr - DT_ADV * (qr * drows(qr) + qc * dcols(qr)))
        vc = grid * (qc - DT_ADV * (qr * drows(qc) + qc * dcols(qc)))
        facts = m_own[0]
        at = (t + 1).astype(F32)
        for c, moved in enumerate(project(vr, vc, grid)):
            u_ext[c] = opened[...] * moved
            u_now = u_ext[c, own, :]
            u_kept[t, c] = u_now
            for k in range(2):
                live = (facts[k : k + 1] == at).astype(F32)
                miss = u_now - t_own[k, c]
                misc[0] += sublanes(live * opened[own, :] * miss * miss)
        return carry

    lax.fori_loop(0, STEPS, forward_step, 0)

    def bar_block(xh, xh_at, t, base, size, c, h_bar):
        n = xh[xh_at, t, pl.ds(base, size), c, :].astype(F32)
        bend = jnp.tanh(n)
        moved = n * bend
        n_bar = h_bar * ((1.0 + bend) * ((1.0 + n) - moved))
        zbuf[pl.ds(base, size), c, :] = n_bar
        acc[0, c, :] += jnp.sum(n_bar, axis=0)
        acc[1, c, :] += jnp.sum(n_bar * n, axis=0)
        return n + moved

    def clear_sums():
        acc[...] = jnp.zeros_like(acc)

    def first_pass_last(t):
        clear_sums()

        def block(base, size):
            low = beside([frows[base + j].astype(BF) for j in range(size)])
            h_bar = nn_dot(headb[...], low)
            bars = jnp.stack([h_bar[:, j * LANES : (j + 1) * LANES] for j in range(size)], axis=0)
            lows = [
                bar_block(xh_full, 2, t, base, size, c, bars[:, c, :]).astype(BF)
                for c in channel_blocks()
            ]
            sg[pl.ds(base + 1, size), CH : 2 * CH, :] = jnp.concatenate(lows, axis=1)

        for_blocks(rows, BAR_LINES, block)

    def head_sums():
        def block(base, size):
            h = beside([sg[base + 1 + j, CH : 2 * CH, :] for j in range(size)])
            low = beside([frows[base + j].astype(BF) for j in range(size)])
            ghead[...] += nt_dot(h, low)

        for_blocks(rows, SUM_LINES, block)

    def sums_start(layer):
        gain = norms[0, layer]
        sums = 0.5 * acc[0]
        cross = (acc[1] - norms[1, layer] * sums) / gain
        group_start(5 + layer, gain * sums, gain * cross)
        gnorm[0, layer] += cross
        gnorm[1, layer] += sums

    def second_pass(layer, t, count, xh, xh_at, dst, by):
        size_all = CH // GROUPS * count * LANES * parts
        total, total_cross = group_finish(5 + layer)
        inverse = inv_kept[t, layer]
        gain = norms[0, layer]
        slope = inverse * spread(total_cross / size_all) / gain
        coef[0] = 0.5 * gain * inverse
        coef[1] = -2.0 * slope
        coef[2] = norms[1, layer] * slope - inverse * spread(total / size_all)

        def z_bar(at, c):
            n = xh[xh_at, t, at, c, :].astype(F32)
            return (zbuf[at, c, :] * coef[0, c] + n * coef[1, c] + coef[2, c]).astype(BF)

        slot = 5 + layer
        for which, line in edge_lines(count - 1):
            edges[slot, which] = z_bar(line, slice(0, CH))
        args = (slot, edge_source(slot), lambda side: g_halo.at[layer, side])
        halo_start(*args)

        def block(base, size):
            at = pl.ds(base + 1, size)
            for c in channel_blocks():
                z = z_bar(pl.ds(base, size), c)
                if by:
                    put_shifted(dst, at, c, z, by, BACKWARD)
                else:
                    dst[at, slice(CH + c.start, CH + c.stop), :] = z

        for_blocks(count, ACT_LINES, block)
        halo_wait(*args)
        if by:
            spread_halo(dst, lambda side: g_halo[layer, side], count, by, BACKWARD)
        else:
            for side in halo_sides():
                dst[side * (count + 1), CH : 2 * CH, :] = g_halo[layer, side]

    def tap_sums(y, size):
        return [
            tap_rows(y, j + 2, 0) + tap_rows(y, j + 1, 1) + tap_rows(y, j, 2) for j in range(size)
        ]

    def bars_of(layer, count, src, then):
        clear_sums()

        def block(base, size):
            g = beside([src[base + j] for j in range(size + 2)])
            then(base, size, jnp.stack(tap_sums(nn_dot(wb[layer], g), size), axis=0))

        for_blocks(count, BAR_LINES, block)

    def weight_sums(at, t, count, src, kept):
        def block(base, size):
            g = beside([src[base + 1 + j] for j in range(size)])
            h = beside([kept[t, pl.ds(base + j, 3)].reshape(3 * CH, LANES) for j in range(size)])
            gw[line_at[at] : line_at[at] + 3 * CH, :] += nt_dot(g, h)

        for_blocks(count, SUM_LINES, block)

    def bars_last(t):
        clear_sums()

        def block(base, size):
            g = beside([sg[base + j] for j in range(size + 2)])
            y = nn_dot(wb[3:5].reshape(6 * CH, 3 * CH), g)
            for j, bar in enumerate(tap_sums(y[3 * CH :], size)):
                skip_bar[base + j] = bar
            ups = tap_sums(y[: 3 * CH], size)
            low = base // 2
            bars = jnp.stack(
                [pair_sum(ups[2 * j] + ups[2 * j + 1]) for j in range(size // 2)], axis=0
            )
            for c in channel_blocks():
                bar_block(xh_half, 1, t, low, size // 2, c, bars[:, c, :])

        for_blocks(rows, BAR_LINES, block)

    def weight_sums_last(t):
        def block(base, size):
            g = beside([sg[base + 1 + j] for j in range(size)])
            low = base // 2
            h = beside([skip[t, pl.ds(base + j, 3)].reshape(3 * CH, LANES) for j in range(size)])
            up = beside(
                [
                    jnp.concatenate([h4[t, low + (j + ky - 1) // 2 + 1] for ky in range(3)], axis=0)
                    for j in range(size)
                ]
            )
            gw[line_at[4] : line_at[4] + 3 * CH, :] += nt_dot(g, h)
            gw[line_at[3] : line_at[3] + 3 * CH, :] += nt_dot(g, up)

        for_blocks(rows, SUM_LINES, block)

    def taps_first():
        def block(base, size):
            g = beside([sg[base + j, CH : 2 * CH, :] for j in range(size)])
            y = nn_dot(w0b[...], g)
            for j in range(size):
                taps[base + j] = y[:, j * LANES : (j + 1) * LANES]

        for_blocks(rows, SUM_LINES, block)
        g = beside([sg[rows + j, CH : 2 * CH, :] for j in range(2)])
        y = nn_dot(w0b[...], g)
        for j in range(2):
            taps[rows + j] = y[:, j * LANES : (j + 1) * LANES]

    def weight_sums_first(t):
        def weights(base, size):
            g = beside([sg[base + 1 + j, CH : 2 * CH, :] for j in range(size)])
            x = beside(
                [s0b[t, pl.ds(base + EDGE - 1 + j, 3)].reshape(48, LANES) for j in range(size)]
            )
            gw0[...] += nt_dot(g, x)

        for_blocks(rows, SUM_LINES, weights)

    def chunk_at(p, which):
        return pl.ds(pl.multiple_of(starts[p] + which * chunks[p], 16), chunks[p])

    def strip(p):
        return pl.ds(offsets[p], chunks[p])

    def exchange_start(copies, count, *args):
        def start(d, carry):
            src, dst, sent, landed, peer = copies(d, *args)[0]
            pltpu.make_async_remote_copy(
                src_ref=src,
                dst_ref=dst,
                send_sem=sent,
                recv_sem=landed,
                device_id=peer,
                device_id_type=MESH,
            ).start()
            return carry

        lax.fori_loop(1, count, start, 0)

    def exchange_finish(copies, count, *args):
        def finish(d, carry):
            (src, _, sent, _, _), (dst, landed) = copies(d, *args)
            pltpu.make_async_copy(src, src, sent).wait()
            pltpu.make_async_copy(dst, dst, landed).wait()
            return carry

        lax.fori_loop(1, count, finish, 0)

    def around(d, here, count):
        return lax.rem(here + d, count), lax.rem(here + count - d, count)

    def chunk_plane(d, p):
        other, source = around(d, mine, members)
        send = (g_send.at[chunk_at(p, other)], p_recv.at[mine, strip(p)])
        sems = (p_ss.at[p, d], p_rs.at[p, mine], plane_id(d))
        return send + sems, (p_recv.at[source, strip(p)], p_rs.at[p, source])

    def chunk_line(d, p):
        other, source = around(d, level, planes)
        block = z_recv.at[level, strip(p)]
        sems = (z_ss.at[p, d], z_rs.at[p, level], line_id(d))
        return (block, block) + sems, (z_recv.at[source, strip(p)], z_rs.at[p, source])

    def chunk_back(d, p):
        other, source = around(d, mine, members)
        block = g_all.at[chunk_at(p, mine)]
        sems = (p_ss.at[3 + p, d], p_rs.at[3 + p, mine], plane_id(d))
        return (block, block) + sems, (g_all.at[chunk_at(p, source)], p_rs.at[3 + p, source])

    def small_plane(d):
        other, source = around(d, mine, members)
        block = m_plane.at[mine]
        sems = (p_ss.at[6, d], p_rs.at[6, mine], plane_id(d))
        return (block, block) + sems, (m_plane.at[source], p_rs.at[6, source])

    def small_line(d):
        other, source = around(d, level, planes)
        block = m_line.at[level]
        sems = (z_ss.at[3, d], z_rs.at[3, level], line_id(d))
        return (block, block) + sems, (m_line.at[source], z_rs.at[3, source])

    def plane_start(p):
        at = slice(starts[p], starts[p] + chunks[p] * members)
        if p == 1:
            gw[at, :] = 0.5 * gw[at, :]
        g_send[at, :] = gw[at, :].astype(BF)
        exchange_start(chunk_plane, members, p)

    def plane_finish(p):
        exchange_finish(chunk_plane, members, p)

        def add(d, total):
            return total + p_recv[lax.rem(mine + d, members), strip(p), :].astype(F32)

        total = lax.fori_loop(1, members, add, gw[chunk_at(p, mine), :])
        z_recv[level, strip(p), :] = total.astype(BF)
        exchange_start(chunk_line, planes, p)

    def line_finish(p):
        exchange_finish(chunk_line, planes, p)

        def add(k, total):
            return total + z_recv[k, strip(p), :].astype(F32)

        total = lax.fori_loop(0, planes, add, jnp.zeros((chunks[p], 3 * CH), F32))
        g_all[chunk_at(p, mine), :] = total.astype(BF)
        exchange_start(chunk_back, members, p)

    def gather_finish(p):
        exchange_finish(chunk_back, members, p)

    def w_args():
        return ext_args(12, w_ext)

    def pull_start(t):
        facts = m_own[0]
        at = (t + 1).astype(F32)
        open_own = opened[own, :]
        for c in range(2):
            pull = jnp.zeros((rows, LANES), F32)
            for k in range(2):
                live = (facts[k : k + 1] == at).astype(F32)
                pull = pull + live * (u_kept[t, c] - t_own[k, c])
            w_ext[c, own, :] = open_own * (u_bar[c] + 2.0 * open_own * pull)
        halo_start(*w_args())

    def backward_step(t):
        def at_last(what, p):
            @pl.when(t == 0)
            def _():
                what(p)

        halo_wait(*w_args())
        grid = grid_mask[...]
        gr, gc = project(w_ext[0], w_ext[1], grid)
        gr, gc = grid * gr, grid * gc
        qr, qc = q_ext[t, 0], q_ext[t, 1]
        bar_r = gr + DT_ADV * (
            drows(gr * qr) + dcols(gr * qc) - (gr * drows(qr) + gc * drows(qc))
        )
        bar_c = gc + DT_ADV * (
            drows(gc * qr) + dcols(gc * qc) - (gr * dcols(qr) + gc * dcols(qc))
        )
        for c, bar in enumerate((bar_r, bar_c)):
            passed = opened[...] * bar
            q_ext[t, c] = passed
            passed = q_ext[t, c, own, :]
            u_bar[c] = passed
            force_bar = DT_FORCE * passed
            misc[2 + c] += sublanes(force_bar)
            frows[:, c, :] = force_bar
        for c in range(2, 16):
            frows[:, c, :] = jnp.zeros((rows, LANES), F32)

        first_pass_last(t)
        sums_start(4)
        head_sums()
        second_pass(4, t, rows, xh_full, 2, sg, 1)
        bars_last(t)
        sums_start(3)
        weight_sums_last(t)
        at_last(plane_start, 2)
        second_pass(3, t, half, xh_half, 1, sgh, 2)

        def into_two(base, size, bars):
            for c in channel_blocks():
                bar_block(xh_half, 0, t, base, size, c, bars[:, c, :])

        bars_of(2, half, sgh, into_two)
        sums_start(2)
        weight_sums(2, t, half, sgh, h3)
        second_pass(2, t, half, xh_half, 0, sgh, 2)

        def into_one(base, size, bars):
            at = 2 * base
            for c in channel_blocks():
                direct = skip_bar[pl.ds(at, 2 * size), c, :].reshape(size, 2, 16, LANES)
                total = (direct + 0.25 * bars[:, None, c, :]).reshape(2 * size, 16, LANES)
                bar_block(xh_full, 1, t, at, 2 * size, c, total)

        bars_of(1, half, sgh, into_one)
        sums_start(1)
        weight_sums(1, t, half, sgh, pooled)
        at_last(plane_finish, 2)
        at_last(plane_start, 1)
        second_pass(1, t, rows, xh_full, 1, sg, 1)

        def into_zero(base, size, bars):
            for c in channel_blocks():
                bar_block(xh_full, 0, t, base, size, c, bars[:, c, :])

        bars_of(0, rows, sg, into_zero)
        sums_start(0)
        weight_sums(0, t, rows, sg, h1)
        at_last(plane_start, 0)
        second_pass(0, t, rows, xh_full, 0, sg, 0)
        @pl.when(t > 0)
        def _():
            taps_first()
            for c in range(2):
                columns = []
                for kx in range(3):
                    total = jnp.zeros((rows, LANES), F32)
                    for ky in range(3):
                        total = total + taps[pl.ds(2 - ky, rows), 16 * ky + 3 * kx + c, :]
                    columns.append(total)
                u_bar[c] += from_right(columns[0], 1) + columns[1] + from_left(columns[2], 1)
            pull_start(t - 1)
        at_last(plane_finish, 1)
        weight_sums_first(t)
        at_last(line_finish, 2)

    pull_start(jnp.int32(STEPS - 1))
    def step_back(i, carry):
        backward_step(STEPS - 1 - i)
        return carry

    lax.fori_loop(0, STEPS, step_back, 0)

    lane = lane_of((CH, CH))
    small_sums = jnp.concatenate([gw0[...], jnp.zeros((CH, CH - 48), F32)], axis=1)
    for which in range(2):
        for layer in range(LAYERS + 1):
            column = jnp.sum(gnorm[which, layer], axis=1, keepdims=True)
            if layer in HALF_SLOT:
                column = 0.5 * column
            small_sums = jnp.where(lane == 48 + 5 * which + layer, column, small_sums)
    for c in range(2):
        small_sums = jnp.where(lane == 58 + c, ghead[:, c : c + 1], small_sums)
    m_plane[mine] = jnp.concatenate(
        [jnp.sum(misc[k], axis=0, keepdims=True) for k in range(4)]
        + [jnp.zeros((4, LANES), F32), beside([small_sums[: CH // 2], small_sums[CH // 2 :]])],
        axis=0,
    )
    exchange_start(small_plane, members)
    plane_finish(0)
    line_finish(1)
    exchange_finish(small_plane, members)
    no_sums = jnp.zeros(m_line.shape[1:], F32)
    m_line[level] = lax.fori_loop(0, members, lambda k, total: total + m_plane[k], no_sums)
    exchange_start(small_line, planes)
    line_finish(0)
    exchange_finish(small_line, planes)
    for p in (2, 1, 0):
        gather_finish(p)

    totals = lax.fori_loop(0, planes, lambda k, total: total + m_line[k], no_sums)
    small_out[...] = totals[8:]
    small_square = jnp.sum(sublanes(totals[8:] * totals[8:]), axis=0, keepdims=True)
    small_square = jnp.sum(small_square, axis=1, keepdims=True)
    totals = jnp.broadcast_to(jnp.sum(totals[:8], axis=1, keepdims=True), (8, LANES))

    def squares(i, total):
        at = pl.ds(pl.multiple_of(i * 64, 64), 64)
        block = g_all[at, :].astype(F32)
        return total + jnp.sum((block * block).reshape(8, 8, 3 * CH), axis=0)

    square = lax.fori_loop(0, all_lines // 64, squares, jnp.zeros((8, 3 * CH), F32))
    square = jnp.sum(jnp.sum(square, axis=0, keepdims=True), axis=1, keepdims=True)
    count = totals[1:2]
    raw = square + small_square + totals[2:3] * totals[2:3] + totals[3:4] * totals[3:4]
    norm = jnp.sqrt(raw) / count
    factor = jnp.minimum(1.0, CLIP_NORM / norm) / count
    scalars[...] = jnp.concatenate([totals[:4], norm, factor, totals[6:]], axis=0)


def train(keyframes, boxes, velocity, targets, w_in, w_mid, norm_params, head_params):
    ranks = lax.axis_size("rows")
    planes = lax.axis_size("batch") // 2
    members = 2 * ranks
    starts, chunks, line_at, lines = gradient_lines(members)
    parts = ranks // 2
    tile = velocity.shape[2]
    rows, half, ext = 2 * tile, tile, 2 * tile + 2 * EDGE
    vmem = pl.BlockSpec(memory_space=pltpu.VMEM)

    def kept(count):
        return pltpu.VMEM((STEPS, count + 2, CH, LANES), BF)

    smem = pl.BlockSpec(memory_space=pltpu.SMEM)
    args = (keyframes, boxes, velocity, targets, w_in, w_mid, norm_params, head_params)
    return pl.pallas_call(
        functools.partial(train_kernel, ranks, planes),
        out_shape=(
            jax.ShapeDtypeStruct((lines, 3 * CH), BF),
            jax.ShapeDtypeStruct((CH // 2, LANES), F32),
            jax.ShapeDtypeStruct((8, LANES), F32),
        ),
        in_specs=[smem] * 2 + [vmem] * 6,
        out_specs=(vmem,) * 3,
        scratch_shapes=[
            pltpu.VMEM((2, 16, LANES), F32),
            pltpu.VMEM((LAYERS + 1, 3 * CH, 3 * CH), BF),
            pltpu.VMEM((LAYERS + 1, 3 * CH, 3 * CH), BF),
            pltpu.VMEM((CH, 48), BF),
            pltpu.VMEM((48, CH), BF),
            pltpu.VMEM((2, LAYERS + 1, CH, LANES), F32),
            pltpu.VMEM((16, CH), BF),
            pltpu.VMEM((CH, 16), BF),
            pltpu.VMEM((2, 1, LANES), F32),
            pltpu.VMEM((3, CH // 2, 8, LANES), F32),
            pltpu.VMEM((2, 3 * (LAYERS + 1), CH, LANES), F32),
            pltpu.VMEM((LANES, LANES), F32),
            pltpu.VMEM((lines, 3 * CH), F32),
            pltpu.VMEM((CH, 48), F32),
            pltpu.VMEM((2, LAYERS + 1, CH, LANES), F32),
            pltpu.VMEM((CH, 16), F32),
            pltpu.VMEM((4, 8, LANES), F32),
            pltpu.VMEM((2, ext, LANES), F32),
            pltpu.VMEM((2, 2, rows, LANES), F32),
            pltpu.VMEM((2, 16, LANES), F32),
            pltpu.VMEM((ext, LANES), F32),
            pltpu.VMEM((ext, LANES), F32),
            pltpu.VMEM((ext, 16, LANES), F32),
            pltpu.VMEM((STEPS, ext, 16, LANES), BF),
            pltpu.VMEM((STEPS, 2, ext, LANES), F32),
            pltpu.VMEM((STEPS, 2, rows, LANES), F32),
            pltpu.VMEM((2, EDGE, LANES), F32),
            pltpu.VMEM((EDGE, 16, LANES), F32),
            pltpu.VMEM((2, ext, LANES), F32),
            pltpu.VMEM((2, rows, LANES), F32),
            pltpu.VMEM((rows, 16, LANES), F32),
            pltpu.VMEM((rows + 2, 48, LANES), F32),
            kept(rows),
            kept(rows),
            kept(half),
            kept(half),
            kept(half),
            pltpu.VMEM((3, STEPS, rows, CH, LANES), BF),
            pltpu.VMEM((2, STEPS, half, CH, LANES), BF),
            pltpu.VMEM((STEPS, LAYERS + 1, CH, LANES), F32),
            pltpu.VMEM((rows, CH, LANES), F32),
            pltpu.VMEM((rows, CH, LANES), F32),
            pltpu.VMEM((rows + 2, 3 * CH, LANES), BF),
            pltpu.VMEM((half + 2, 3 * CH, LANES), BF),
            pltpu.VMEM((10, 2, CH, LANES), BF),
            pltpu.VMEM((LAYERS + 1, 2, CH, LANES), BF),
            pltpu.VMEM((2 * LANES, 3 * LANES), BF),
            pltpu.VMEM((3, CH, LANES), F32),
            pltpu.VMEM((2, CH, LANES), F32),
            pltpu.VMEM((10, 16, LANES), F32),
            pltpu.VMEM((10, parts - 1, 16, LANES), F32),
            pltpu.VMEM((lines, 3 * CH), BF),
            pltpu.VMEM((members, sum(chunks), 3 * CH), BF),
            pltpu.VMEM((planes, sum(chunks), 3 * CH), BF),
            pltpu.VMEM((members, 8 + CH // 2, LANES), F32),
            pltpu.VMEM((planes, 8 + CH // 2, LANES), F32),
            pltpu.SemaphoreType.DMA((2, 3)),
            pltpu.SemaphoreType.DMA((2, 3)),
            pltpu.SemaphoreType.DMA((3,)),
            pltpu.SemaphoreType.DMA((13, 2)),
            pltpu.SemaphoreType.DMA((13, 2)),
            pltpu.SemaphoreType.DMA((10, parts - 1)),
            pltpu.SemaphoreType.DMA((10, parts - 1)),
            pltpu.SemaphoreType.DMA((7, members)),
            pltpu.SemaphoreType.DMA((7, members)),
            pltpu.SemaphoreType.DMA((4, planes)),
            pltpu.SemaphoreType.DMA((4, planes)),
        ],
        compiler_params=pltpu.CompilerParams(
            collective_id=0, has_side_effects=True, vmem_limit_bytes=60 * 2**20
        ),
        name="train",
    )(*args)


def adam_kernel(line_at, g_all, small, scalars, *refs):
    olds = [refs[3 * k : 3 * k + 3] for k in range(4)]
    news = [refs[12 + 3 * k : 15 + 3 * k] for k in range(4)]
    low_in, low_mid, low_head, loss, cells, norm, wide, turned, lines = refs[24:]
    factor = scalars[5, 0]
    at_step = pl.program_id(0)

    def update(which, at, g, low=None):
        weight, moment, second = (ref[at] for ref in olds[which])
        moment = BETA_ONE * moment + (1 - BETA_ONE) * g
        second = BETA_TWO * second + (1 - BETA_TWO) * g * g
        mhat = moment / (1 - BETA_ONE**STEP_NUM)
        vhat = second / (1 - BETA_TWO**STEP_NUM)
        change = mhat / (jnp.sqrt(vhat) + ADAM_EPS) + DECAY * weight
        weight = weight - RATES[which] * change
        for ref, value in zip(news[which], (weight, moment, second)):
            ref[at] = value
        if low is not None:
            low[at] = weight.astype(BF)

    @pl.when(at_step == 0)
    def _():
        loss[0, 0] = scalars[0, 0]
        cells[0, 0] = scalars[1, 0]
        norm[0, 0] = scalars[4, 0]
        for k in range(LAYERS + 1):
            at = pl.ds(line_at[k], 3 * CH)
            to = pl.ds(k * 3 * CH, 3 * CH)
            wide[0, to, :] = g_all[at, :LANES].astype(F32) * factor
            tail = g_all[at, LANES:].astype(F32) * factor
            wide[1, to, :] = jnp.concatenate([tail, jnp.zeros_like(tail)], axis=1)
        rest = small[...] * factor
        rest = jnp.concatenate([rest, pltpu.roll(rest, CH, 1), jnp.zeros((CH, LANES), F32)], axis=0)
        turned[...] = rest.T
        for ch in range(3):
            for ky in range(3):
                g = turned[pl.ds(16 * ky + ch, 3, 3), :]
                update(0, (ch, ky), g[:, :CH], low_in)
        for layer in range(LAYERS + 1):
            g = turned[pl.ds(48 + layer, 2, LAYERS + 1), :]
            update(2, (layer,), g[:, :CH])
        line_is = lax.broadcasted_iota(jnp.int32, (2, LANES), 0)
        bias = jnp.where(line_is == 0, scalars[2, 0] * factor, scalars[3, 0] * factor)
        g = jnp.where(lane_of((2, LANES)) < CH, turned[58:60, :], bias)
        update(3, (slice(None),), g[:, : CH + 1], low_head)

    low_lanes = lane_of((CH // 2, LANES)) < CH
    for ky in range(3):

        @pl.when(at_step == ky)
        def _():
            for k in range(LAYERS + 1):
                for kx in range(3):
                    base = k * 3 * CH + kx * CH
                    even = wide[ky // 2, pl.ds(base, CH // 2, 2), :]
                    odd = wide[ky // 2, pl.ds(base + 1, CH // 2, 2), :]
                    if ky % 2:
                        even = pltpu.roll(even, CH, 1)
                    else:
                        odd = pltpu.roll(odd, CH, 1)
                    lines[kx, :, k, :] = jnp.where(low_lanes, even, odd)

    for kx in range(3):
        g = jnp.concatenate(
            [lines[kx, a, : LAYERS + 1, :] for a in range(CH // 2)], axis=1
        )
        update(1, (kx,), g, low_mid)


def adam(g_all, small, scalars, params, moments, seconds):
    line_at = gradient_lines(2 * lax.axis_size("rows"))[2]
    smem = pl.BlockSpec(memory_space=pltpu.SMEM)
    shapes = [w.shape for w in params]
    whole = lambda shape: pl.BlockSpec(shape, lambda i: (0,) * len(shape))
    mid = pl.BlockSpec((3,) + shapes[1][1:], lambda i: (i, 0, 0))
    spec = lambda k: mid if k == 1 else whole(shapes[k])
    states = [x for group in zip(params, moments, seconds) for x in group]
    lows = (0, 1, 3)
    return pl.pallas_call(
        functools.partial(adam_kernel, line_at),
        grid=(3,),
        out_shape=tuple(jax.ShapeDtypeStruct(x.shape, F32) for x in states)
        + tuple(jax.ShapeDtypeStruct(shapes[k], BF) for k in lows)
        + (jax.ShapeDtypeStruct((1, 1), F32),) * 3,
        in_specs=[whole(g_all.shape), whole(small.shape), smem] + [spec(k // 3) for k in range(12)],
        out_specs=tuple(spec(k // 3) for k in range(12))
        + tuple(spec(k) for k in lows)
        + (smem,) * 3,
        scratch_shapes=[
            pltpu.VMEM((2, (LAYERS + 1) * 3 * CH, LANES), F32),
            pltpu.VMEM((LANES, LANES), F32),
            pltpu.VMEM((3, CH // 2, 8, LANES), F32),
        ],
        compiler_params=pltpu.CompilerParams(vmem_limit_bytes=60 * 2**20),
        name="adam",
    )(g_all, small, scalars, *states)


def in_order(group):
    first, mid, norm, head = group
    return (
        jnp.transpose(first, (1, 2, 3, 0)),
        jnp.transpose(mid, (1, 0, 2)),
        jnp.transpose(norm, (1, 0, 2)),
        head,
    )


def out_of_order(group):
    first, mid, norm, head = group
    return (
        jnp.transpose(first, (3, 0, 1, 2)),
        jnp.transpose(mid, (1, 0, 2)),
        jnp.transpose(norm, (1, 0, 2)),
        head,
    )


def shards(
    velocity,
    targets,
    keyframes,
    boxes,
    w_in,
    w_mid,
    norm_params,
    head_params,
    m_in,
    m_mid,
    m_norm,
    m_head,
    v_in,
    v_mid,
    v_norm,
    v_head,
):
    params = in_order((w_in, w_mid, norm_params, head_params))
    moments = in_order((m_in, m_mid, m_norm, m_head))
    seconds = in_order((v_in, v_mid, v_norm, v_head))
    g_all, small, scalars = train(keyframes, boxes, velocity, targets, *params)
    result = adam(g_all, small, scalars, params, moments, seconds)
    new_w, new_m, new_v = (out_of_order(result[k:12:3]) for k in range(3))
    low_in, low_mid, low_head, loss, cells, norm = result[12:]
    return (
        *new_w,
        *new_m,
        *new_v,
        jnp.transpose(low_in, (3, 0, 1, 2)),
        jnp.transpose(low_mid, (1, 0, 2)),
        low_head,
        loss.reshape(()),
        cells.reshape(()),
        norm.reshape(()),
    )


def solution(mesh):
    return jax.shard_map(
        shards,
        mesh=mesh,
        in_specs=(
            P("batch", None, "rows", None),
            P("batch", None, None, "rows", None),
            P("batch", None),
            P("batch", None, None),
        )
        + (P(),) * 12,
        out_specs=(P(),) * 18,
        check_vma=False,
    )
```

```python
import functools

import jax
import jax.numpy as jnp
from jax import lax
from jax.experimental import pallas as pl
from jax.experimental.pallas import tpu as pltpu
from jax.sharding import PartitionSpec as P

CH = 64
GROUPS = 8
LAYERS = 4
STEPS = 4
JACOBI = 4
STEP_NUM = 10
LANES = 128
EDGE = 8

EPS_NORM = 1e-05
DT_FORCE = 0.5
DT_ADV = 0.2
CLIP_NORM = 0.001
BETA_ONE = 0.9
BETA_TWO = 0.95
ADAM_EPS = 1e-08
DECAY = 0.01
RATES = (0.2, 0.05, 1.0, 0.15)

BF = jnp.bfloat16
F32 = jnp.float32
MESH = pl.DeviceIdType.MESH
FULL_SLOT = {0: 0, 1: 1, 4: 2}
HALF_SLOT = {2: 0, 3: 1}
ACT_LINES = 64
CONV_LINES = 64
BAR_LINES = 32
SUM_LINES = 64


def nt_dot(a, b):
    return lax.dot_general(a, b, (((1,), (1,)), ((), ())), preferred_element_type=F32)


def nn_dot(a, b):
    return jnp.dot(a, b, preferred_element_type=F32)


def beside(rows):
    return jnp.concatenate(rows, axis=1)


def lane_of(shape):
    return lax.broadcasted_iota(jnp.int32, shape, len(shape) - 1)


def from_left(x, by):
    return jnp.where(lane_of(x.shape) < by, jnp.zeros((), x.dtype), pltpu.roll(x, by, x.ndim - 1))


def from_right(x, by):
    moved = pltpu.roll(x, LANES - by, x.ndim - 1)
    return jnp.where(lane_of(x.shape) >= LANES - by, jnp.zeros((), x.dtype), moved)


def pair_sum(x):
    even = lane_of(x.shape) % 2 == 0
    last = x.ndim - 1
    return x + jnp.where(even, pltpu.roll(x, LANES - 1, last), pltpu.roll(x, 1, last))


def drows(x):
    count = x.shape[0]
    return 0.5 * (pltpu.roll(x, count - 1, 0) - pltpu.roll(x, 1, 0))


def dcols(x):
    return 0.5 * (from_right(x, 1) - from_left(x, 1))


def nsum(x):
    count = x.shape[0]
    return (
        pltpu.roll(x, count - 1, 0) + pltpu.roll(x, 1, 0) + from_right(x, 1) + from_left(x, 1)
    )


def project(vr, vc, grid):
    div = grid * (drows(vr) + dcols(vc))
    press = -0.25 * div
    for sweep in range(JACOBI - 1):
        press = grid * (0.25 * (nsum(press) - div))
    return vr - drows(press), vc - dcols(press)


def sublanes(x):
    return jnp.sum(x.reshape(x.shape[0] // 8, 8, LANES), axis=0)


def group_rows(x):
    return jnp.sum(x.reshape(GROUPS, CH // GROUPS, LANES), axis=1)


def spread(x):
    return jnp.concatenate(
        [jnp.broadcast_to(x[g : g + 1], (CH // GROUPS, LANES)) for g in range(GROUPS)], axis=0
    )


def gradient_lines(members):
    groups = ((0,), (1, 2), (3, 4))
    chunks, starts, at = [], [], []
    start = 0
    for group in groups:
        place = start
        for layer in group:
            at.append(place)
            place += 3 * CH
        chunk = -(-(place - start) // (16 * members)) * 16
        starts.append(start)
        chunks.append(chunk)
        start += chunk * members
    return starts, chunks, at, start


def train_kernel(
    ranks,
    planes,
    keys,
    boxes,
    vel,
    tgt,
    w_in,
    w_mid,
    norm_params,
    head,
    g_all,
    small_out,
    scalars,
    meta,
    wf,
    wb,
    w0f,
    w0b,
    norms,
    headf,
    headb,
    bias,
    lines,
    wide,
    small,
    gw,
    gw0,
    gnorm,
    ghead,
    misc,
    u_ext,
    t_own,
    m_own,
    opened,
    grid_mask,
    s0,
    s0b,
    q_ext,
    u_kept,
    q_edge,
    f_edge,
    w_ext,
    u_bar,
    frows,
    taps,
    h1,
    skip,
    pooled,
    h3,
    h4,
    xh_full,
    xh_half,
    inv_kept,
    zbuf,
    skip_bar,
    sg,
    sgh,
    edges,
    g_halo,
    pool_mat,
    coef,
    acc,
    st_send,
    st_recv,
    g_send,
    p_recv,
    z_recv,
    m_plane,
    m_line,
    in_send,
    in_recv,
    in_local,
    halo_send,
    halo_recv,
    st_ss,
    st_rs,
    p_ss,
    p_rs,
    z_ss,
    z_rs,
):
    quarter = ranks // 4
    parts = ranks // 2
    tile = vel.shape[2]
    rows = 2 * tile
    half = rows // 2
    batch_at = lax.axis_index("batch")
    row_at = lax.axis_index("rows")
    core = lax.rem(batch_at, 2)
    plane = batch_at - core
    sample = row_at // quarter
    part = 2 * lax.rem(row_at, quarter) + core

    def owner(which, piece):
        return (plane + lax.rem(piece, 2), which * quarter + piece // 2)

    u_ext[...] = jnp.zeros_like(u_ext)
    q_ext[...] = jnp.zeros_like(q_ext)
    w_ext[...] = jnp.zeros_like(w_ext)
    g_halo[...] = jnp.zeros_like(g_halo)
    for count, shifted in ((rows, sg), (half, sgh)):
        for at in (0, count + 1):
            shifted[at] = jnp.zeros((3 * CH, LANES), BF)
    for kept, count in ((h1, rows), (skip, rows), (pooled, half), (h3, half), (h4, half)):
        for t in range(STEPS):
            kept[t, 0] = jnp.zeros((CH, LANES), BF)
            kept[t, count + 1] = jnp.zeros((CH, LANES), BF)

    barrier = pltpu.get_barrier_semaphore()
    members = 2 * ranks
    starts, chunks, line_at, all_lines = gradient_lines(members)
    offsets = [sum(chunks[:k]) for k in range(3)]
    mine = core * ranks + row_at

    def plane_id(d):
        other = lax.rem(mine + d, members)
        return (plane + other // ranks, lax.rem(other, ranks))

    def greet(d, carry):
        pl.semaphore_signal(barrier, inc=1, device_id=plane_id(d), device_id_type=MESH)
        return carry

    lax.fori_loop(1, members, greet, 0)
    level = batch_at // 2

    def line_id(d):
        return (2 * lax.rem(level + d, planes) + core, row_at)

    def greet_line(d, carry):
        pl.semaphore_signal(barrier, inc=1, device_id=line_id(d), device_id_type=MESH)
        return carry

    lax.fori_loop(1, planes, greet_line, 0)

    line_is = lax.broadcasted_iota(jnp.int32, (16, LANES), 0)
    for j in range(2):
        values = [keys[j, k] for k in range(2)]
        values += [boxes[j, b, k] for b in range(2) for k in range(4)]
        facts = jnp.zeros((16, LANES), F32)
        for k, value in enumerate(values):
            facts = jnp.where(line_is == k, value.astype(F32), facts)
        meta[j] = facts

    low_lanes = lane_of((CH // 2, LANES)) < CH
    for ky in range(3):
        for kx in range(3):
            for a in range(CH // 2):
                lines[kx, a, : LAYERS + 1, :] = w_mid[3 * ky + kx, :, a * LANES : (a + 1) * LANES]
        for k in range(LAYERS + 1):
            left, mid, right = (lines[kx, :, k, :] for kx in range(3))
            slab = 3 * k + ky
            even, odd = pl.ds(0, CH // 2, 2), pl.ds(1, CH // 2, 2)
            wide[0, slab, even, :] = jnp.where(low_lanes, left, pltpu.roll(mid, CH, 1))
            wide[0, slab, odd, :] = jnp.where(low_lanes, pltpu.roll(left, CH, 1), mid)
            wide[1, slab, even, :] = right
            wide[1, slab, odd, :] = pltpu.roll(right, CH, 1)
    low_lanes = lane_of((CH, LANES)) < CH
    for k in range(LAYERS + 1):
        for ky in range(3):
            slab = 3 * k + ky
            at = slice(ky * CH, (ky + 1) * CH)
            first, last = wide[0, slab], wide[1, slab]
            wf[k, at, :] = jnp.concatenate([first, last[:, :CH]], axis=1).astype(BF)
            turned = jnp.concatenate([first, last], axis=0).T
            left, mid = turned[:CH], turned[CH:]
            first = jnp.where(low_lanes, left, pltpu.roll(mid, CH, 1))
            last = pltpu.roll(left, CH, 1)
            wb[k, at, :] = jnp.concatenate([first, last[:, :CH]], axis=1).astype(BF)
    pl.semaphore_wait(barrier, members + planes - 2)

    def incoming(place):
        at = pl.ds(pl.multiple_of(EDGE + place * tile, 8), tile)
        here = pl.ds(pl.multiple_of(place * tile, 8), tile)
        return u_ext.at[:, at, :], t_own.at[:, :, here, :], m_own.at[place]

    place = lax.rem(row_at, 2)
    for j, k in ((0, 0), (1, 0), (0, 2), (1, 2), (0, 1), (1, 1)):
        to_batch, to_row = owner(2 * core + j, row_at // 2)
        stays = (to_batch == batch_at) & (to_row == row_at)
        for src, dst in [((vel, tgt, meta)[k].at[j], incoming(place)[k])]:

            @pl.when(stays)
            def _():
                pltpu.make_async_copy(src, dst, in_local.at[k]).start()

            @pl.when(jnp.logical_not(stays))
            def _():
                pltpu.make_async_remote_copy(
                    src_ref=src,
                    dst_ref=dst,
                    send_sem=in_send.at[j, k],
                    recv_sem=in_recv.at[place, k],
                    device_id=(to_batch, to_row),
                    device_id_type=MESH,
                ).start()

    small[...] = jnp.zeros_like(small)
    for ch in range(3):
        for ky in range(3):
            taps_in = w_in[ch, ky]
            taps_in = jnp.concatenate([taps_in, jnp.zeros_like(taps_in)], axis=1)
            small[pl.ds(16 * ky + ch, 3, 3), :] = taps_in
    for layer in range(LAYERS + 1):
        pair = norm_params[layer]
        small[48 + 2 * layer : 50 + 2 * layer, :] = jnp.concatenate(
            [pair, jnp.zeros_like(pair)], axis=1
        )
    pair = head[:, :CH]
    small[64:66, :] = jnp.concatenate([pair, jnp.zeros_like(pair)], axis=1)
    w0b[...] = small[:48, :CH].astype(BF)
    headf[...] = small[64:80, :CH].astype(BF)
    turned = small[...].T[:CH]
    w0f[...] = turned[:, :48].astype(BF)
    headb[...] = turned[:, 64:80].astype(BF)
    for which in range(2):
        for layer in range(LAYERS + 1):
            at = 48 + 2 * layer + which
            norms[which, layer] = jnp.broadcast_to(turned[:, at : at + 1], (CH, LANES))
        bias[which] = jnp.broadcast_to(head[which : which + 1, CH : CH + 1], (1, LANES))

    def arrive(which):
        for i in range(2):
            from_batch = plane + sample // 2
            from_row = 2 * part + i
            stays = (from_batch == batch_at) & (from_row == row_at)
            for k, dst in enumerate(incoming(i)):
                if k not in which:
                    continue

                @pl.when(jnp.logical_not(stays))
                def _():
                    pltpu.make_async_copy(dst, dst, in_recv.at[i, k]).wait()

    def leave(which):
        for j in range(2):
            to_batch, to_row = owner(2 * core + j, row_at // 2)
            stays = (to_batch == batch_at) & (to_row == row_at)
            for k, src in enumerate((vel.at[j], tgt.at[j], meta.at[j])):
                if k not in which:
                    continue

                @pl.when(stays)
                def _():
                    pltpu.make_async_copy(src, src, in_local.at[k]).wait()

                @pl.when(jnp.logical_not(stays))
                def _():
                    pltpu.make_async_copy(src, src, in_send.at[j, k]).wait()

    leave((0, 2))
    arrive((0, 2))

    has_prev = part > 0
    has_next = part < parts - 1
    prev_id = owner(sample, jnp.maximum(part - 1, 0))
    next_id = owner(sample, jnp.minimum(part + 1, parts - 1))

    two = parts == 2
    near = 1 - part

    def halo_copy(slot, src, dst, side):
        return pltpu.make_async_remote_copy(
            src_ref=src(side),
            dst_ref=dst(1 - side),
            send_sem=halo_send.at[slot, side],
            recv_sem=halo_recv.at[slot, side],
            device_id=(prev_id, next_id)[side],
            device_id_type=MESH,
        )

    def only_copy(slot, src, dst):
        return pltpu.make_async_remote_copy(
            src_ref=src(near),
            dst_ref=dst(part),
            send_sem=halo_send.at[slot, 0],
            recv_sem=halo_recv.at[slot, 0],
            device_id=owner(sample, near),
            device_id_type=MESH,
        )

    def halo_start(slot, src, dst):
        if two:
            only_copy(slot, src, dst).start()
            return

        @pl.when(has_prev)
        def _():
            halo_copy(slot, src, dst, 0).start()

        @pl.when(has_next)
        def _():
            halo_copy(slot, src, dst, 1).start()

    def halo_wait(slot, src, dst):
        if two:
            only_copy(slot, src, dst).wait_send()
            landed = dst(near)
            pltpu.make_async_copy(landed, landed, halo_recv.at[slot, 0]).wait()
            return

        @pl.when(has_prev)
        def _():
            halo_copy(slot, src, dst, 0).wait_send()
            halo_copy(slot, src, dst, 1).wait_recv()

        @pl.when(has_next)
        def _():
            halo_copy(slot, src, dst, 1).wait_send()
            halo_copy(slot, src, dst, 0).wait_recv()

    def edge_lines(count):
        return [(0, near * count)] if two else [(0, 0), (1, count)]

    def edge_source(slot):
        return lambda side: edges.at[slot, 0 if two else side]

    def ext_args(slot, ref):
        def lines_at(start):
            return ref.at[:, pl.ds(pl.multiple_of(start, 8), EDGE), :]

        return (
            slot,
            lambda side: lines_at(EDGE + side * (rows - EDGE)),
            lambda side: lines_at(side * (rows + EDGE)),
        )

    def ext_halo(slot, ref):
        args = ext_args(slot, ref)
        halo_start(*args)
        halo_wait(*args)

    def group_copies(slot):
        return [
            pltpu.make_async_remote_copy(
                src_ref=st_send.at[slot],
                dst_ref=st_recv.at[slot, d - 1],
                send_sem=st_ss.at[slot, d - 1],
                recv_sem=st_rs.at[slot, d - 1],
                device_id=owner(sample, lax.rem(part + d, parts)),
                device_id_type=MESH,
            )
            for d in range(1, parts)
        ]

    def group_start(slot, first, second):
        st_send[slot] = jnp.concatenate([group_rows(first), group_rows(second)], axis=0)
        for copy in group_copies(slot):
            copy.start()

    def group_finish(slot):
        total = st_send[slot]
        for d, copy in enumerate(group_copies(slot)):
            copy.wait()
            total = total + st_recv[slot, d]
        total = jnp.broadcast_to(jnp.sum(total, axis=1, keepdims=True), total.shape)
        return total[:GROUPS], total[GROUPS:]

    ext = rows + 2 * EDGE
    row_is = lax.broadcasted_iota(jnp.int32, (ext, LANES), 0) - EDGE + part * rows
    inside_grid = ((row_is >= 0) & (row_is < parts * rows)).astype(F32)
    row_f = row_is.astype(F32)
    col_f = lane_of((ext, LANES)).astype(F32)
    covered = jnp.zeros((ext, LANES), F32)
    facts = m_own[0]
    for b in range(2):
        bounds = [facts[2 + 4 * b + k : 3 + 4 * b + k] for k in range(4)]
        inside = (
            (row_f >= bounds[0])
            & (row_f < bounds[1])
            & (col_f >= bounds[2])
            & (col_f < bounds[3])
        )
        covered = jnp.maximum(covered, inside.astype(F32))
    grid_mask[...] = inside_grid
    opened[...] = inside_grid * (1.0 - covered)
    own = pl.ds(EDGE, rows)
    misc[...] = jnp.zeros_like(misc)
    live_slots = (facts[0:1] > 0.5).astype(F32) + (facts[1:2] > 0.5).astype(F32)
    misc[1] = sublanes(opened[own, :] * live_slots)
    gw[...] = jnp.zeros_like(gw)
    gw0[...] = jnp.zeros_like(gw0)
    gnorm[...] = jnp.zeros_like(gnorm)
    ghead[...] = jnp.zeros_like(ghead)
    s0[...] = jnp.zeros_like(s0)
    frows[...] = jnp.zeros_like(frows)
    u_bar[...] = jnp.zeros_like(u_bar)

    ext_halo(10, u_ext)

    source = lax.broadcasted_iota(jnp.int32, pool_mat.shape, 0) % LANES
    target = lane_of(pool_mat.shape)
    column = target % LANES + 2 * (target // LANES - 1)
    pool_mat[...] = jnp.where(source // 2 == (column + 2) // 2 - 1, 0.25, 0.0).astype(BF)

    for kx in range(3):
        field = opened[...]
        s0[:, 3 * kx + 2, :] = (from_left(field, 1), field, from_right(field, 1))[kx]

    def put_shifted(dst, at, c, x, by, order):
        copies = (from_left(x, by), x, from_right(x, by))
        for place_at, which in enumerate(order):
            dst[at, slice(place_at * CH + c.start, place_at * CH + c.stop), :] = copies[which]

    FORWARD = (0, 1, 2)
    BACKWARD = (2, 1, 0)

    def halo_sides():
        return [near] if two else [0, 1]

    def spread_halo(dst, line_of, count, by, order):
        for side in halo_sides():
            put_shifted(dst, side * (count + 1), slice(0, CH), line_of(side), by, order)

    def for_blocks(count, size, body):
        size = min(size, count)
        if size == count:
            body(0, size)
            return

        def step(i, carry):
            body(pl.multiple_of(i * size, size), size)
            return carry

        lax.fori_loop(0, count // size, step, 0)

    def channel_blocks():
        return [slice(16 * c, 16 * c + 16) for c in range(CH // 16)]

    def make_norm(layer, t, sums, squares, count):
        group_start(layer, sums, squares)
        sums, squares = group_finish(layer)
        size = CH // GROUPS * count * LANES * parts
        mean = sums / size
        inverse = lax.rsqrt(squares / size - mean * mean + EPS_NORM)
        scale = spread(inverse)
        inv_kept[t, layer] = scale
        scale = 0.5 * scale * norms[0, layer]
        coef[0] = scale
        coef[1] = 0.5 * norms[1, layer] - spread(mean) * scale

    def activate(z, c):
        n = z * coef[0, c] + coef[1, c]
        return n, n * jnp.tanh(n) + n

    def conv_sums(count, size, rows_of):
        size = min(size, count)
        zero = jnp.zeros((CH, LANES), F32)

        def step(i, carry):
            sums, squares = carry
            base = i * size
            for j, z in enumerate(rows_of(base, size)):
                zbuf[base + j] = z
                sums = sums + z
                squares = squares + z * z
            return sums, squares

        if size == count:
            return step(0, (zero, zero))
        return lax.fori_loop(0, count // size, step, (zero, zero))

    def tap_rows(y, j, at):
        return y[at * CH : (at + 1) * CH, j * LANES : (j + 1) * LANES]

    def conv_of(src, layer):
        def rows_of(base, size):
            y = nn_dot(wf[layer], beside([src[base + j] for j in range(size + 2)]))
            return [
                tap_rows(y, j, 0) + tap_rows(y, j + 1, 1) + tap_rows(y, j + 2, 2)
                for j in range(size)
            ]

        return rows_of

    def conv_last(base, size):
        y = nn_dot(wf[4], beside([sg[base + j] for j in range(size + 2)]))
        low = base // 2
        x = nn_dot(wf[3], beside([sgh[low + j] for j in range(size // 2 + 2)]))
        result = []
        for j in range(size):
            z = tap_rows(y, j, 0) + tap_rows(y, j + 1, 1) + tap_rows(y, j + 2, 2)
            for ky in range(3):
                z = z + tap_rows(x, (j + ky - 1) // 2 + 1, ky)
            result.append(z)
        return result

    def finish_plain(t, layer, count, kept, xh, xh_at, dst, by, slot):
        for which, line in edge_lines(count - 1):
            edges[slot, which] = activate(zbuf[line], slice(0, CH))[1].astype(BF)
        args = (slot, edge_source(slot), lambda side: kept.at[t, side * (count + 1)])
        halo_start(*args)

        def block(base, size):
            at = pl.ds(base + 1, size)
            for c in channel_blocks():
                n, h = activate(zbuf[pl.ds(base, size), c, :], c)
                xh[xh_at, t, pl.ds(base, size), c, :] = n.astype(BF)
                low = h.astype(BF)
                kept[t, at, c, :] = low
                put_shifted(dst, at, c, low, by, FORWARD)

        for_blocks(count, ACT_LINES, block)
        halo_wait(*args)
        spread_halo(dst, lambda side: kept[t, side * (count + 1)], count, by, FORWARD)

    def pool_pairs(low, size):
        pairs = jnp.concatenate(
            [beside([low[2 * j], low[2 * j + 1]]) for j in range(size // 2)], axis=0
        )
        return nn_dot(pairs, pool_mat[...]).astype(BF).reshape(size // 2, CH, 3 * LANES)

    def finish_skip(t):
        for which, line in edge_lines(rows - 2):
            low = activate(zbuf[pl.ds(line, 2)], slice(0, CH))[1].astype(BF)
            edges[2, which] = pool_pairs(low, 2)[0, :, LANES : 2 * LANES]
            edges[1, which] = jnp.where(part == 0, low[1], low[0]) if two else low[which]
        skip_args = (1, edge_source(1), lambda side: skip.at[t, side * (rows + 1)])
        pool_args = (2, edge_source(2), lambda side: pooled.at[t, side * (half + 1)])
        halo_start(*pool_args)
        halo_start(*skip_args)

        def block(base, size):
            at = pl.ds(base + 1, size)
            lows = []
            for c in channel_blocks():
                n, h = activate(zbuf[pl.ds(base, size), c, :], c)
                xh_full[1, t, pl.ds(base, size), c, :] = n.astype(BF)
                low = h.astype(BF)
                skip[t, at, c, :] = low
                put_shifted(sg, at, c, low, 1, FORWARD)
                lows.append(low)
            small = pool_pairs(jnp.concatenate(lows, axis=1), size)
            at = pl.ds(base // 2 + 1, size // 2)
            pooled[t, at] = small[:, :, LANES : 2 * LANES]
            for k in range(3):
                sgh[at, k * CH : (k + 1) * CH, :] = small[:, :, k * LANES : (k + 1) * LANES]

        for_blocks(rows, ACT_LINES, block)
        halo_wait(*pool_args)
        halo_wait(*skip_args)
        spread_halo(sgh, lambda side: pooled[t, side * (half + 1)], half, 2, FORWARD)
        spread_halo(sg, lambda side: skip[t, side * (rows + 1)], rows, 1, FORWARD)

    def push_args(t):
        source, target = ext_args(11, q_ext.at[t])[1:]
        return (11, (lambda side: q_edge) if two else source, target)

    def finish_last(t):
        if two:
            line = pl.multiple_of(near * (rows - EDGE), EDGE)
            h = activate(zbuf[pl.ds(line, EDGE)], slice(0, CH))[1].astype(BF)
            force = nn_dot(headf[...], beside([h[j] for j in range(EDGE)]))
            for j in range(EDGE):
                f_edge[j] = force[:, j * LANES : (j + 1) * LANES]
            at = pl.ds(line + EDGE, EDGE)
            for c in range(2):
                force = f_edge[:, c, :] + bias[c]
                q_edge[c] = (u_ext[c, at, :] + DT_FORCE * force) * opened[at, :]
            halo_start(*push_args(t))

        def block(base, size):
            lows = []
            for c in channel_blocks():
                n, h = activate(zbuf[pl.ds(base, size), c, :], c)
                xh_full[2, t, pl.ds(base, size), c, :] = n.astype(BF)
                lows.append(h.astype(BF))
            low = jnp.concatenate(lows, axis=1)
            force = nn_dot(headf[...], beside([low[j] for j in range(size)]))
            for j in range(size):
                frows[base + j] = force[:, j * LANES : (j + 1) * LANES]

        for_blocks(rows, ACT_LINES, block)

    def forward_step(t, carry):
        for c in range(2):
            field = u_ext[c]
            for kx, moved in enumerate((from_left(field, 1), field, from_right(field, 1))):
                s0[:, 3 * kx + c, :] = moved
        s0b[t] = s0[...].astype(BF)

        def first_rows(base, size):
            x = beside(
                [s0b[t, pl.ds(base + EDGE - 1 + j, 3)].reshape(48, LANES) for j in range(size)]
            )
            z = nn_dot(w0f[...], x)
            return [z[:, j * LANES : (j + 1) * LANES] for j in range(size)]

        make_norm(0, t, *conv_sums(rows, CONV_LINES, first_rows), rows)
        finish_plain(t, 0, rows, h1, xh_full, 0, sg, 1, 0)
        make_norm(1, t, *conv_sums(rows, CONV_LINES, conv_of(sg, 0)), rows)
        finish_skip(t)
        make_norm(2, t, *conv_sums(half, CONV_LINES, conv_of(sgh, 1)), half)
        finish_plain(t, 2, half, h3, xh_half, 0, sgh, 2, 3)
        make_norm(3, t, *conv_sums(half, CONV_LINES, conv_of(sgh, 2)), half)
        finish_plain(t, 3, half, h4, xh_half, 1, sgh, 1, 4)
        make_norm(4, t, *conv_sums(rows, CONV_LINES, conv_last), rows)
        finish_last(t)

        for c in range(2):
            force = frows[:, c, :] + bias[c]
            q_ext[t, c, own, :] = (u_ext[c, own, :] + DT_FORCE * force) * opened[own, :]
        if not two:
            halo_start(*push_args(t))
        halo_wait(*push_args(t))

        @pl.when(t == 0)
        def _():
            leave((1,))
            arrive((1,))

        qr, qc = q_ext[t, 0], q_ext[t, 1]
        grid = grid_mask[...]
        vr = grid * (qr - DT_ADV * (qr * drows(qr) + qc * dcols(qr)))
        vc = grid * (qc - DT_ADV * (qr * drows(qc) + qc * dcols(qc)))
        facts = m_own[0]
        at = (t + 1).astype(F32)
        for c, moved in enumerate(project(vr, vc, grid)):
            u_ext[c] = opened[...] * moved
            u_now = u_ext[c, own, :]
            u_kept[t, c] = u_now
            for k in range(2):
                live = (facts[k : k + 1] == at).astype(F32)
                miss = u_now - t_own[k, c]
                misc[0] += sublanes(live * opened[own, :] * miss * miss)
        return carry

    lax.fori_loop(0, STEPS, forward_step, 0)

    def bar_block(xh, xh_at, t, base, size, c, h_bar):
        n = xh[xh_at, t, pl.ds(base, size), c, :].astype(F32)
        bend = jnp.tanh(n)
        moved = n * bend
        n_bar = h_bar * ((1.0 + bend) * ((1.0 + n) - moved))
        zbuf[pl.ds(base, size), c, :] = n_bar
        acc[0, c, :] += jnp.sum(n_bar, axis=0)
        acc[1, c, :] += jnp.sum(n_bar * n, axis=0)
        return n + moved

    def clear_sums():
        acc[...] = jnp.zeros_like(acc)

    def first_pass_last(t):
        clear_sums()

        def block(base, size):
            low = beside([frows[base + j].astype(BF) for j in range(size)])
            h_bar = nn_dot(headb[...], low)
            bars = jnp.stack([h_bar[:, j * LANES : (j + 1) * LANES] for j in range(size)], axis=0)
            lows = [
                bar_block(xh_full, 2, t, base, size, c, bars[:, c, :]).astype(BF)
                for c in channel_blocks()
            ]
            sg[pl.ds(base + 1, size), CH : 2 * CH, :] = jnp.concatenate(lows, axis=1)

        for_blocks(rows, BAR_LINES, block)

    def head_sums():
        def block(base, size):
            h = beside([sg[base + 1 + j, CH : 2 * CH, :] for j in range(size)])
            low = beside([frows[base + j].astype(BF) for j in range(size)])
            ghead[...] += nt_dot(h, low)

        for_blocks(rows, SUM_LINES, block)

    def sums_start(layer):
        gain = norms[0, layer]
        sums = 0.5 * acc[0]
        cross = (acc[1] - norms[1, layer] * sums) / gain
        group_start(5 + layer, gain * sums, gain * cross)
        gnorm[0, layer] += cross
        gnorm[1, layer] += sums

    def second_pass(layer, t, count, xh, xh_at, dst, by):
        size_all = CH // GROUPS * count * LANES * parts
        total, total_cross = group_finish(5 + layer)
        inverse = inv_kept[t, layer]
        gain = norms[0, layer]
        slope = inverse * spread(total_cross / size_all) / gain
        coef[0] = 0.5 * gain * inverse
        coef[1] = -2.0 * slope
        coef[2] = norms[1, layer] * slope - inverse * spread(total / size_all)

        def z_bar(at, c):
            n = xh[xh_at, t, at, c, :].astype(F32)
            return (zbuf[at, c, :] * coef[0, c] + n * coef[1, c] + coef[2, c]).astype(BF)

        slot = 5 + layer
        for which, line in edge_lines(count - 1):
            edges[slot, which] = z_bar(line, slice(0, CH))
        args = (slot, edge_source(slot), lambda side: g_halo.at[layer, side])
        halo_start(*args)

        def block(base, size):
            at = pl.ds(base + 1, size)
            for c in channel_blocks():
                z = z_bar(pl.ds(base, size), c)
                if by:
                    put_shifted(dst, at, c, z, by, BACKWARD)
                else:
                    dst[at, slice(CH + c.start, CH + c.stop), :] = z

        for_blocks(count, ACT_LINES, block)
        halo_wait(*args)
        if by:
            spread_halo(dst, lambda side: g_halo[layer, side], count, by, BACKWARD)
        else:
            for side in halo_sides():
                dst[side * (count + 1), CH : 2 * CH, :] = g_halo[layer, side]

    def tap_sums(y, size):
        return [
            tap_rows(y, j + 2, 0) + tap_rows(y, j + 1, 1) + tap_rows(y, j, 2) for j in range(size)
        ]

    def bars_of(layer, count, src, then):
        clear_sums()

        def block(base, size):
            g = beside([src[base + j] for j in range(size + 2)])
            then(base, size, jnp.stack(tap_sums(nn_dot(wb[layer], g), size), axis=0))

        for_blocks(count, BAR_LINES, block)

    def weight_sums(at, t, count, src, kept):
        def block(base, size):
            g = beside([src[base + 1 + j] for j in range(size)])
            h = beside([kept[t, pl.ds(base + j, 3)].reshape(3 * CH, LANES) for j in range(size)])
            gw[line_at[at] : line_at[at] + 3 * CH, :] += nt_dot(g, h)

        for_blocks(count, SUM_LINES, block)

    def bars_last(t):
        clear_sums()

        def block(base, size):
            g = beside([sg[base + j] for j in range(size + 2)])
            y = nn_dot(wb[3:5].reshape(6 * CH, 3 * CH), g)
            for j, bar in enumerate(tap_sums(y[3 * CH :], size)):
                skip_bar[base + j] = bar
            ups = tap_sums(y[: 3 * CH], size)
            low = base // 2
            bars = jnp.stack(
                [pair_sum(ups[2 * j] + ups[2 * j + 1]) for j in range(size // 2)], axis=0
            )
            for c in channel_blocks():
                bar_block(xh_half, 1, t, low, size // 2, c, bars[:, c, :])

        for_blocks(rows, BAR_LINES, block)

    def weight_sums_last(t):
        def block(base, size):
            g = beside([sg[base + 1 + j] for j in range(size)])
            low = base // 2
            h = beside([skip[t, pl.ds(base + j, 3)].reshape(3 * CH, LANES) for j in range(size)])
            up = beside(
                [
                    jnp.concatenate([h4[t, low + (j + ky - 1) // 2 + 1] for ky in range(3)], axis=0)
                    for j in range(size)
                ]
            )
            gw[line_at[4] : line_at[4] + 3 * CH, :] += nt_dot(g, h)
            gw[line_at[3] : line_at[3] + 3 * CH, :] += nt_dot(g, up)

        for_blocks(rows, SUM_LINES, block)

    def taps_first():
        def block(base, size):
            g = beside([sg[base + j, CH : 2 * CH, :] for j in range(size)])
            y = nn_dot(w0b[...], g)
            for j in range(size):
                taps[base + j] = y[:, j * LANES : (j + 1) * LANES]

        for_blocks(rows, SUM_LINES, block)
        g = beside([sg[rows + j, CH : 2 * CH, :] for j in range(2)])
        y = nn_dot(w0b[...], g)
        for j in range(2):
            taps[rows + j] = y[:, j * LANES : (j + 1) * LANES]

    def weight_sums_first(t):
        def weights(base, size):
            g = beside([sg[base + 1 + j, CH : 2 * CH, :] for j in range(size)])
            x = beside(
                [s0b[t, pl.ds(base + EDGE - 1 + j, 3)].reshape(48, LANES) for j in range(size)]
            )
            gw0[...] += nt_dot(g, x)

        for_blocks(rows, SUM_LINES, weights)

    def chunk_at(p, which):
        return pl.ds(pl.multiple_of(starts[p] + which * chunks[p], 16), chunks[p])

    def strip(p):
        return pl.ds(offsets[p], chunks[p])

    def exchange_start(copies, count, *args):
        def start(d, carry):
            src, dst, sent, landed, peer = copies(d, *args)[0]
            pltpu.make_async_remote_copy(
                src_ref=src,
                dst_ref=dst,
                send_sem=sent,
                recv_sem=landed,
                device_id=peer,
                device_id_type=MESH,
            ).start()
            return carry

        lax.fori_loop(1, count, start, 0)

    def exchange_finish(copies, count, *args):
        def finish(d, carry):
            (src, _, sent, _, _), (dst, landed) = copies(d, *args)
            pltpu.make_async_copy(src, src, sent).wait()
            pltpu.make_async_copy(dst, dst, landed).wait()
            return carry

        lax.fori_loop(1, count, finish, 0)

    def around(d, here, count):
        return lax.rem(here + d, count), lax.rem(here + count - d, count)

    def chunk_plane(d, p):
        other, source = around(d, mine, members)
        send = (g_send.at[chunk_at(p, other)], p_recv.at[mine, strip(p)])
        sems = (p_ss.at[p, d], p_rs.at[p, mine], plane_id(d))
        return send + sems, (p_recv.at[source, strip(p)], p_rs.at[p, source])

    def chunk_line(d, p):
        other, source = around(d, level, planes)
        block = z_recv.at[level, strip(p)]
        sems = (z_ss.at[p, d], z_rs.at[p, level], line_id(d))
        return (block, block) + sems, (z_recv.at[source, strip(p)], z_rs.at[p, source])

    def chunk_back(d, p):
        other, source = around(d, mine, members)
        block = g_all.at[chunk_at(p, mine)]
        sems = (p_ss.at[3 + p, d], p_rs.at[3 + p, mine], plane_id(d))
        return (block, block) + sems, (g_all.at[chunk_at(p, source)], p_rs.at[3 + p, source])

    def small_plane(d):
        other, source = around(d, mine, members)
        block = m_plane.at[mine]
        sems = (p_ss.at[6, d], p_rs.at[6, mine], plane_id(d))
        return (block, block) + sems, (m_plane.at[source], p_rs.at[6, source])

    def small_line(d):
        other, source = around(d, level, planes)
        block = m_line.at[level]
        sems = (z_ss.at[3, d], z_rs.at[3, level], line_id(d))
        return (block, block) + sems, (m_line.at[source], z_rs.at[3, source])

    def plane_start(p):
        at = slice(starts[p], starts[p] + chunks[p] * members)
        if p == 1:
            gw[at, :] = 0.5 * gw[at, :]
        g_send[at, :] = gw[at, :].astype(BF)
        exchange_start(chunk_plane, members, p)

    def plane_finish(p):
        exchange_finish(chunk_plane, members, p)

        def add(d, total):
            return total + p_recv[lax.rem(mine + d, members), strip(p), :].astype(F32)

        total = lax.fori_loop(1, members, add, gw[chunk_at(p, mine), :])
        z_recv[level, strip(p), :] = total.astype(BF)
        exchange_start(chunk_line, planes, p)

    def line_finish(p):
        exchange_finish(chunk_line, planes, p)

        def add(k, total):
            return total + z_recv[k, strip(p), :].astype(F32)

        total = lax.fori_loop(0, planes, add, jnp.zeros((chunks[p], 3 * CH), F32))
        g_all[chunk_at(p, mine), :] = total.astype(BF)
        exchange_start(chunk_back, members, p)

    def gather_finish(p):
        exchange_finish(chunk_back, members, p)

    def w_args():
        return ext_args(12, w_ext)

    def pull_start(t):
        facts = m_own[0]
        at = (t + 1).astype(F32)
        open_own = opened[own, :]
        for c in range(2):
            pull = jnp.zeros((rows, LANES), F32)
            for k in range(2):
                live = (facts[k : k + 1] == at).astype(F32)
                pull = pull + live * (u_kept[t, c] - t_own[k, c])
            w_ext[c, own, :] = open_own * (u_bar[c] + 2.0 * open_own * pull)
        halo_start(*w_args())

    def backward_step(t):
        def at_last(what, p):
            @pl.when(t == 0)
            def _():
                what(p)

        halo_wait(*w_args())
        grid = grid_mask[...]
        gr, gc = project(w_ext[0], w_ext[1], grid)
        gr, gc = grid * gr, grid * gc
        qr, qc = q_ext[t, 0], q_ext[t, 1]
        bar_r = gr + DT_ADV * (
            drows(gr * qr) + dcols(gr * qc) - (gr * drows(qr) + gc * drows(qc))
        )
        bar_c = gc + DT_ADV * (
            drows(gc * qr) + dcols(gc * qc) - (gr * dcols(qr) + gc * dcols(qc))
        )
        for c, bar in enumerate((bar_r, bar_c)):
            passed = opened[...] * bar
            q_ext[t, c] = passed
            passed = q_ext[t, c, own, :]
            u_bar[c] = passed
            force_bar = DT_FORCE * passed
            misc[2 + c] += sublanes(force_bar)
            frows[:, c, :] = force_bar

        first_pass_last(t)
        sums_start(4)
        head_sums()
        second_pass(4, t, rows, xh_full, 2, sg, 1)
        bars_last(t)
        sums_start(3)
        weight_sums_last(t)
        at_last(plane_start, 2)
        second_pass(3, t, half, xh_half, 1, sgh, 2)

        def into_two(base, size, bars):
            for c in channel_blocks():
                bar_block(xh_half, 0, t, base, size, c, bars[:, c, :])

        bars_of(2, half, sgh, into_two)
        sums_start(2)
        weight_sums(2, t, half, sgh, h3)
        second_pass(2, t, half, xh_half, 0, sgh, 2)

        def into_one(base, size, bars):
            at = 2 * base
            for c in channel_blocks():
                direct = skip_bar[pl.ds(at, 2 * size), c, :].reshape(size, 2, 16, LANES)
                total = (direct + 0.25 * bars[:, None, c, :]).reshape(2 * size, 16, LANES)
                bar_block(xh_full, 1, t, at, 2 * size, c, total)

        bars_of(1, half, sgh, into_one)
        sums_start(1)
        weight_sums(1, t, half, sgh, pooled)
        at_last(plane_finish, 2)
        at_last(plane_start, 1)
        second_pass(1, t, rows, xh_full, 1, sg, 1)

        def into_zero(base, size, bars):
            for c in channel_blocks():
                bar_block(xh_full, 0, t, base, size, c, bars[:, c, :])

        bars_of(0, rows, sg, into_zero)
        sums_start(0)
        weight_sums(0, t, rows, sg, h1)
        at_last(plane_start, 0)
        second_pass(0, t, rows, xh_full, 0, sg, 0)
        @pl.when(t > 0)
        def _():
            taps_first()
            for c in range(2):
                columns = []
                for kx in range(3):
                    total = jnp.zeros((rows, LANES), F32)
                    for ky in range(3):
                        total = total + taps[pl.ds(2 - ky, rows), 16 * ky + 3 * kx + c, :]
                    columns.append(total)
                u_bar[c] += from_right(columns[0], 1) + columns[1] + from_left(columns[2], 1)
            pull_start(t - 1)
        at_last(plane_finish, 1)
        weight_sums_first(t)
        at_last(line_finish, 2)

    pull_start(jnp.int32(STEPS - 1))
    def step_back(i, carry):
        backward_step(STEPS - 1 - i)
        return carry

    lax.fori_loop(0, STEPS, step_back, 0)

    lane = lane_of((CH, CH))
    small_sums = jnp.concatenate([gw0[...], jnp.zeros((CH, CH - 48), F32)], axis=1)
    for which in range(2):
        for layer in range(LAYERS + 1):
            column = jnp.sum(gnorm[which, layer], axis=1, keepdims=True)
            if layer in HALF_SLOT:
                column = 0.5 * column
            small_sums = jnp.where(lane == 48 + 5 * which + layer, column, small_sums)
    for c in range(2):
        small_sums = jnp.where(lane == 58 + c, ghead[:, c : c + 1], small_sums)
    m_plane[mine] = jnp.concatenate(
        [jnp.sum(misc[k], axis=0, keepdims=True) for k in range(4)]
        + [jnp.zeros((4, LANES), F32), beside([small_sums[: CH // 2], small_sums[CH // 2 :]])],
        axis=0,
    )
    exchange_start(small_plane, members)
    plane_finish(0)
    line_finish(1)
    exchange_finish(small_plane, members)
    no_sums = jnp.zeros(m_line.shape[1:], F32)
    m_line[level] = lax.fori_loop(0, members, lambda k, total: total + m_plane[k], no_sums)
    exchange_start(small_line, planes)
    line_finish(0)

    def squares(i, total):
        at = pl.ds(pl.multiple_of(i * 128, 128), 128)
        block = g_all[at, :].astype(F32)
        return total + jnp.sum((block * block).reshape(16, 8, 3 * CH), axis=0)

    gather_finish(2)
    gather_finish(1)
    early = starts[1] // 128
    square = lax.fori_loop(early, all_lines // 128, squares, jnp.zeros((8, 3 * CH), F32))
    exchange_finish(small_line, planes)
    totals = lax.fori_loop(0, planes, lambda k, total: total + m_line[k], no_sums)
    small_out[...] = totals[8:]
    small_square = jnp.sum(sublanes(totals[8:] * totals[8:]), axis=0, keepdims=True)
    small_square = jnp.sum(small_square, axis=1, keepdims=True)
    totals = jnp.broadcast_to(jnp.sum(totals[:8], axis=1, keepdims=True), (8, LANES))

    gather_finish(0)
    square = lax.fori_loop(0, early, squares, square)
    square = jnp.sum(jnp.sum(square, axis=0, keepdims=True), axis=1, keepdims=True)
    count = totals[1:2]
    raw = square + small_square + totals[2:3] * totals[2:3] + totals[3:4] * totals[3:4]
    norm = jnp.sqrt(raw) / count
    factor = jnp.minimum(1.0, CLIP_NORM / norm) / count
    scalars[...] = jnp.concatenate([totals[:4], norm, factor, totals[6:]], axis=0)


def train(keyframes, boxes, velocity, targets, w_in, w_mid, norm_params, head_params):
    ranks = lax.axis_size("rows")
    planes = lax.axis_size("batch") // 2
    members = 2 * ranks
    starts, chunks, line_at, lines = gradient_lines(members)
    parts = ranks // 2
    tile = velocity.shape[2]
    rows, half, ext = 2 * tile, tile, 2 * tile + 2 * EDGE
    vmem = pl.BlockSpec(memory_space=pltpu.VMEM)

    def kept(count):
        return pltpu.VMEM((STEPS, count + 2, CH, LANES), BF)

    smem = pl.BlockSpec(memory_space=pltpu.SMEM)
    args = (keyframes, boxes, velocity, targets, w_in, w_mid, norm_params, head_params)
    return pl.pallas_call(
        functools.partial(train_kernel, ranks, planes),
        out_shape=(
            jax.ShapeDtypeStruct((lines, 3 * CH), BF),
            jax.ShapeDtypeStruct((CH // 2, LANES), F32),
            jax.ShapeDtypeStruct((8, LANES), F32),
        ),
        in_specs=[smem] * 2 + [vmem] * 6,
        out_specs=(vmem,) * 3,
        scratch_shapes=[
            pltpu.VMEM((2, 16, LANES), F32),
            pltpu.VMEM((LAYERS + 1, 3 * CH, 3 * CH), BF),
            pltpu.VMEM((LAYERS + 1, 3 * CH, 3 * CH), BF),
            pltpu.VMEM((CH, 48), BF),
            pltpu.VMEM((48, CH), BF),
            pltpu.VMEM((2, LAYERS + 1, CH, LANES), F32),
            pltpu.VMEM((16, CH), BF),
            pltpu.VMEM((CH, 16), BF),
            pltpu.VMEM((2, 1, LANES), F32),
            pltpu.VMEM((3, CH // 2, 8, LANES), F32),
            pltpu.VMEM((2, 3 * (LAYERS + 1), CH, LANES), F32),
            pltpu.VMEM((LANES, LANES), F32),
            pltpu.VMEM((lines, 3 * CH), F32),
            pltpu.VMEM((CH, 48), F32),
            pltpu.VMEM((2, LAYERS + 1, CH, LANES), F32),
            pltpu.VMEM((CH, 16), F32),
            pltpu.VMEM((4, 8, LANES), F32),
            pltpu.VMEM((2, ext, LANES), F32),
            pltpu.VMEM((2, 2, rows, LANES), F32),
            pltpu.VMEM((2, 16, LANES), F32),
            pltpu.VMEM((ext, LANES), F32),
            pltpu.VMEM((ext, LANES), F32),
            pltpu.VMEM((ext, 16, LANES), F32),
            pltpu.VMEM((STEPS, ext, 16, LANES), BF),
            pltpu.VMEM((STEPS, 2, ext, LANES), F32),
            pltpu.VMEM((STEPS, 2, rows, LANES), F32),
            pltpu.VMEM((2, EDGE, LANES), F32),
            pltpu.VMEM((EDGE, 16, LANES), F32),
            pltpu.VMEM((2, ext, LANES), F32),
            pltpu.VMEM((2, rows, LANES), F32),
            pltpu.VMEM((rows, 16, LANES), F32),
            pltpu.VMEM((rows + 2, 48, LANES), F32),
            kept(rows),
            kept(rows),
            kept(half),
            kept(half),
            kept(half),
            pltpu.VMEM((3, STEPS, rows, CH, LANES), BF),
            pltpu.VMEM((2, STEPS, half, CH, LANES), BF),
            pltpu.VMEM((STEPS, LAYERS + 1, CH, LANES), F32),
            pltpu.VMEM((rows, CH, LANES), F32),
            pltpu.VMEM((rows, CH, LANES), F32),
            pltpu.VMEM((rows + 2, 3 * CH, LANES), BF),
            pltpu.VMEM((half + 2, 3 * CH, LANES), BF),
            pltpu.VMEM((10, 2, CH, LANES), BF),
            pltpu.VMEM((LAYERS + 1, 2, CH, LANES), BF),
            pltpu.VMEM((2 * LANES, 3 * LANES), BF),
            pltpu.VMEM((3, CH, LANES), F32),
            pltpu.VMEM((2, CH, LANES), F32),
            pltpu.VMEM((10, 16, LANES), F32),
            pltpu.VMEM((10, parts - 1, 16, LANES), F32),
            pltpu.VMEM((lines, 3 * CH), BF),
            pltpu.VMEM((members, sum(chunks), 3 * CH), BF),
            pltpu.VMEM((planes, sum(chunks), 3 * CH), BF),
            pltpu.VMEM((members, 8 + CH // 2, LANES), F32),
            pltpu.VMEM((planes, 8 + CH // 2, LANES), F32),
            pltpu.SemaphoreType.DMA((2, 3)),
            pltpu.SemaphoreType.DMA((2, 3)),
            pltpu.SemaphoreType.DMA((3,)),
            pltpu.SemaphoreType.DMA((13, 2)),
            pltpu.SemaphoreType.DMA((13, 2)),
            pltpu.SemaphoreType.DMA((10, parts - 1)),
            pltpu.SemaphoreType.DMA((10, parts - 1)),
            pltpu.SemaphoreType.DMA((7, members)),
            pltpu.SemaphoreType.DMA((7, members)),
            pltpu.SemaphoreType.DMA((4, planes)),
            pltpu.SemaphoreType.DMA((4, planes)),
        ],
        compiler_params=pltpu.CompilerParams(
            collective_id=0, has_side_effects=True, vmem_limit_bytes=60 * 2**20
        ),
        name="train",
    )(*args)


def adam_kernel(line_at, g_all, small, scalars, *refs):
    olds = [refs[3 * k : 3 * k + 3] for k in range(4)]
    news = [refs[12 + 3 * k : 15 + 3 * k] for k in range(4)]
    low_in, low_mid, low_head, loss, cells, norm, wide, turned, lines = refs[24:]
    factor = scalars[5, 0]
    at_step = pl.program_id(0)

    def update(which, at, g, low=None):
        weight, moment, second = (ref[at] for ref in olds[which])
        moment = BETA_ONE * moment + (1 - BETA_ONE) * g
        second = BETA_TWO * second + (1 - BETA_TWO) * g * g
        mhat = moment / (1 - BETA_ONE**STEP_NUM)
        vhat = second / (1 - BETA_TWO**STEP_NUM)
        change = mhat / (jnp.sqrt(vhat) + ADAM_EPS) + DECAY * weight
        weight = weight - RATES[which] * change
        for ref, value in zip(news[which], (weight, moment, second)):
            ref[at] = value
        if low is not None:
            low[at] = weight.astype(BF)

    @pl.when(at_step == 0)
    def _():
        loss[0, 0] = scalars[0, 0]
        cells[0, 0] = scalars[1, 0]
        norm[0, 0] = scalars[4, 0]
        for k in range(LAYERS + 1):
            at = pl.ds(line_at[k], 3 * CH)
            to = pl.ds(k * 3 * CH, 3 * CH)
            wide[0, to, :] = g_all[at, :LANES].astype(F32) * factor
            tail = g_all[at, LANES:].astype(F32) * factor
            wide[1, to, :] = jnp.concatenate([tail, jnp.zeros_like(tail)], axis=1)
        rest = small[...] * factor
        rest = jnp.concatenate([rest, pltpu.roll(rest, CH, 1), jnp.zeros((CH, LANES), F32)], axis=0)
        turned[...] = rest.T
        for ch in range(3):
            for ky in range(3):
                g = turned[pl.ds(16 * ky + ch, 3, 3), :]
                update(0, (ch, ky), g[:, :CH], low_in)
        for layer in range(LAYERS + 1):
            g = turned[pl.ds(48 + layer, 2, LAYERS + 1), :]
            update(2, (layer,), g[:, :CH])
        line_is = lax.broadcasted_iota(jnp.int32, (2, LANES), 0)
        bias = jnp.where(line_is == 0, scalars[2, 0] * factor, scalars[3, 0] * factor)
        g = jnp.where(lane_of((2, LANES)) < CH, turned[58:60, :], bias)
        update(3, (slice(None),), g[:, : CH + 1], low_head)

    low_lanes = lane_of((CH // 2, LANES)) < CH
    for ky in range(3):

        @pl.when(at_step == ky)
        def _():
            for k in range(LAYERS + 1):
                for kx in range(3):
                    base = k * 3 * CH + kx * CH
                    even = wide[ky // 2, pl.ds(base, CH // 2, 2), :]
                    odd = wide[ky // 2, pl.ds(base + 1, CH // 2, 2), :]
                    if ky % 2:
                        even = pltpu.roll(even, CH, 1)
                    else:
                        odd = pltpu.roll(odd, CH, 1)
                    lines[kx, :, k, :] = jnp.where(low_lanes, even, odd)

    for kx in range(3):
        g = jnp.concatenate(
            [lines[kx, a, : LAYERS + 1, :] for a in range(CH // 2)], axis=1
        )
        update(1, (kx,), g, low_mid)


def adam(g_all, small, scalars, params, moments, seconds):
    line_at = gradient_lines(2 * lax.axis_size("rows"))[2]
    smem = pl.BlockSpec(memory_space=pltpu.SMEM)
    shapes = [w.shape for w in params]
    whole = lambda shape: pl.BlockSpec(shape, lambda i: (0,) * len(shape))
    mid = pl.BlockSpec((3,) + shapes[1][1:], lambda i: (i, 0, 0))
    spec = lambda k: mid if k == 1 else whole(shapes[k])
    states = [x for group in zip(params, moments, seconds) for x in group]
    lows = (0, 1, 3)
    return pl.pallas_call(
        functools.partial(adam_kernel, line_at),
        grid=(3,),
        out_shape=tuple(jax.ShapeDtypeStruct(x.shape, F32) for x in states)
        + tuple(jax.ShapeDtypeStruct(shapes[k], BF) for k in lows)
        + (jax.ShapeDtypeStruct((1, 1), F32),) * 3,
        in_specs=[whole(g_all.shape), whole(small.shape), smem] + [spec(k // 3) for k in range(12)],
        out_specs=tuple(spec(k // 3) for k in range(12))
        + tuple(spec(k) for k in lows)
        + (smem,) * 3,
        scratch_shapes=[
            pltpu.VMEM((2, (LAYERS + 1) * 3 * CH, LANES), F32),
            pltpu.VMEM((LANES, LANES), F32),
            pltpu.VMEM((3, CH // 2, 8, LANES), F32),
        ],
        compiler_params=pltpu.CompilerParams(vmem_limit_bytes=60 * 2**20),
        name="adam",
    )(g_all, small, scalars, *states)


def in_order(group):
    first, mid, norm, head = group
    return (
        jnp.transpose(first, (1, 2, 3, 0)),
        jnp.transpose(mid, (1, 0, 2)),
        jnp.transpose(norm, (1, 0, 2)),
        head,
    )


def out_of_order(group):
    first, mid, norm, head = group
    return (
        jnp.transpose(first, (3, 0, 1, 2)),
        jnp.transpose(mid, (1, 0, 2)),
        jnp.transpose(norm, (1, 0, 2)),
        head,
    )


def shards(
    velocity,
    targets,
    keyframes,
    boxes,
    w_in,
    w_mid,
    norm_params,
    head_params,
    m_in,
    m_mid,
    m_norm,
    m_head,
    v_in,
    v_mid,
    v_norm,
    v_head,
):
    params = in_order((w_in, w_mid, norm_params, head_params))
    moments = in_order((m_in, m_mid, m_norm, m_head))
    seconds = in_order((v_in, v_mid, v_norm, v_head))
    g_all, small, scalars = train(keyframes, boxes, velocity, targets, *params)
    result = adam(g_all, small, scalars, params, moments, seconds)
    new_w, new_m, new_v = (out_of_order(result[k:12:3]) for k in range(3))
    low_in, low_mid, low_head, loss, cells, norm = result[12:]
    return (
        *new_w,
        *new_m,
        *new_v,
        jnp.transpose(low_in, (3, 0, 1, 2)),
        jnp.transpose(low_mid, (1, 0, 2)),
        low_head,
        loss.reshape(()),
        cells.reshape(()),
        norm.reshape(()),
    )


def solution(mesh):
    return jax.shard_map(
        shards,
        mesh=mesh,
        in_specs=(
            P("batch", None, "rows", None),
            P("batch", None, None, "rows", None),
            P("batch", None),
            P("batch", None, None),
        )
        + (P(),) * 12,
        out_specs=(P(),) * 18,
        check_vma=False,
    )
```
